32 devices in a mesh: batch: 2 (over core), seq: 8 (over z, x), tensor: 2 (over y).
Axes of the slice: x: 2, y: 2, z: 4, core: 2. Of those that a mesh axis runs over, the one named last changes fastest.
Arguments:
- hidden: bfloat16 [2, 4096, 1536], P('batch', 'seq'), may hold values from -6 to 6
- lengths: int32 [2, 7], P('batch'), may hold values from 1 to 2048, as said below
- norm_attn: bfloat16 [1536], P(('batch', 'seq')), may hold values from 0.5 to 1.5
- w_query: bfloat16 [1536, 1536], P(('batch', 'seq'), 'tensor'), may hold values from -0.15625 to 0.15625
- key_weight_matrix: bfloat16 [1536, 256], P(('batch', 'seq'), 'tensor'), may hold values from -0.15625 to 0.15625
- value_weight_matrix: bfloat16 [1536, 256], P(('batch', 'seq'), 'tensor'), may hold values from -0.15625 to 0.15625
- b_query: bfloat16 [12, 128], P('tensor', ('batch', 'seq')), may hold values from -3 to 3
- key_bias_rows: bfloat16 [2, 128], P('tensor', ('batch', 'seq')), may hold values from -3 to 3
- value_bias_rows: bfloat16 [2, 128], P('tensor', ('batch', 'seq')), may hold values from -3 to 3
- w_out: bfloat16 [1536, 1536], P('tensor', ('batch', 'seq')), may hold values from -1.5 to 1.5
- norm_mlp: bfloat16 [1536], P(('batch', 'seq')), may hold values from 0.5 to 1.5
- w_gate: bfloat16 [1536, 8960], P(('batch', 'seq'), 'tensor'), may hold values from -0.15625 to 0.15625
- w_up: bfloat16 [1536, 8960], P(('batch', 'seq'), 'tensor'), may hold values from -0.15625 to 0.15625
- w_down: bfloat16 [8960, 1536], P('tensor', ('batch', 'seq')), may hold values from -0.0625 to 0.0625
- cotangent: bfloat16 [2, 4096, 1536], P('batch', 'seq'), may hold values from -6 to 6
Outputs:
- output: bfloat16 [2, 4096, 1536], P('batch', 'seq')
- grad_hidden: float32 [2, 4096, 1536], P('batch', 'seq')
- grad_norm_attn: float32 [1536], P(('batch', 'seq'))
- grad_query: float32 [1536, 1536], P(('batch', 'seq'), 'tensor')
- grad_key: float32 [1536, 256], P(('batch', 'seq'), 'tensor')
- grad_value: float32 [1536, 256], P(('batch', 'seq'), 'tensor')
- grad_bias_query: float32 [12, 128], P('tensor', ('batch', 'seq'))
- grad_bias_key: float32 [2, 128], P('tensor', ('batch', 'seq'))
- grad_bias_value: float32 [2, 128], P('tensor', ('batch', 'seq'))
- grad_out: float32 [1536, 1536], P('tensor', ('batch', 'seq'))
- grad_norm_mlp: float32 [1536], P(('batch', 'seq'))
- grad_gate: float32 [1536, 8960], P(('batch', 'seq'), 'tensor')
- grad_up: float32 [1536, 8960], P(('batch', 'seq'), 'tensor')
- grad_down: float32 [8960, 1536], P('tensor', ('batch', 'seq'))
The draws below stay inside these ranges and needn't reach their ends.
Inputs may be any that keep to these rules, and one draw needn't show every extreme that they name: In each row the 7 lengths sum to 4096, and the first or the last of them is 2048.
All inputs are finite; a program needn't handle non-finite values.
Results may differ from the reference program's by a relative error of at most 0.03.
Values may be sent and summed in bfloat16 or wider, within the bound.
A program may use at most 256 MiB of HBM per device.

```python
import jax
import jax.numpy as jnp
from jax import lax

MODEL_WIDTH = 1536
FF = 8960
QUERY_HEADS = 12
KEY_VALUE_HEADS = 2
HEAD_SIZE = 128
TOK_DEV = 512
ROW = 4096
ROWS = 2
DOCS = 7
N_SEQ = 8


def draw_lengths(key, part):
    key = jax.random.fold_in(key, 7)
    half_row = ROW // 2
    side_key, cut_key = jax.random.split(key)
    row_keys = jax.random.split(cut_key, ROWS)
    pick_all = jax.vmap(lambda sub_key: jax.random.permutation(sub_key, half_row - 1)[:DOCS - 2])(row_keys)
    cut_points = jnp.sort(pick_all + 1, axis=1).astype(jnp.int32)
    edge_all = jnp.concatenate([jnp.zeros((ROWS, 1), jnp.int32), cut_points, jnp.full((ROWS, 1), half_row, jnp.int32)], axis=1)
    pieces = (edge_all[:, 1:] - edge_all[:, :-1]).astype(jnp.int32)
    longest = jnp.full((ROWS, 1), half_row, jnp.int32)
    side_flag = jax.random.randint(side_key, (ROWS, 1), 0, 2)
    leading = jnp.concatenate([longest, pieces], axis=1)
    trailing = jnp.concatenate([pieces, longest], axis=1)
    return jnp.where(side_flag == 1, leading, trailing).astype(jnp.int32)


def steps_of(rng, dims, cuts, smallest, top_value):
    def one(axis_at, shards_of):
        draws = jax.random.uniform(jax.random.fold_in(jax.random.fold_in(rng, 6), axis_at), (shards_of,), jnp.float32, smallest / len(cuts), top_value / len(cuts))
        return jnp.repeat(jnp.exp(draws), dims[axis_at] // shards_of).reshape((-1,) + (1,) * (len(dims) - axis_at - 1))

    loudness = one(*cuts[0])
    for cut in cuts[1:]:
        loudness = loudness * one(*cut)
    return loudness


def centred(rng, dims, scale, reach, cuts=(), kind=jnp.bfloat16):
    level = steps_of(rng, dims, cuts, -0.22, 0.18) if cuts else 1.0
    values = jax.random.normal(rng, dims, jnp.float32) * scale * level
    return jnp.minimum(jnp.maximum(values, -reach), reach).astype(kind)


def setup_inputs(seed: int = 0) -> dict:
    key_list = jax.random.split(jax.random.key(seed), 16)
    return {
        "hidden": centred(key_list[0], (ROWS, ROW, MODEL_WIDTH), 1.0, 6.0, ((0, 2), (1, 8))),
        "lengths": draw_lengths(jax.random.fold_in(key_list[15], 71), 0),
        "norm_attn": jnp.clip(1.0 + 0.1 * jax.random.normal(key_list[2], (MODEL_WIDTH,), jnp.float32), 0.5, 1.5).astype(jnp.bfloat16),
        "w_query": centred(key_list[3], (MODEL_WIDTH, QUERY_HEADS * HEAD_SIZE), MODEL_WIDTH ** -0.5, 0.15625, ((0, 16), (1, 2))),
        "key_weight_matrix": centred(key_list[4], (MODEL_WIDTH, KEY_VALUE_HEADS * HEAD_SIZE), MODEL_WIDTH ** -0.5, 0.15625, ((0, 16), (1, 2))),
        "value_weight_matrix": centred(key_list[5], (MODEL_WIDTH, KEY_VALUE_HEADS * HEAD_SIZE), MODEL_WIDTH ** -0.5, 0.15625, ((0, 16), (1, 2))),
        "b_query": centred(key_list[6], (QUERY_HEADS, HEAD_SIZE), 0.5, 3.0, ((0, 2), (1, 16))),
        "key_bias_rows": centred(key_list[7], (KEY_VALUE_HEADS, HEAD_SIZE), 0.5, 3.0, ((0, 2), (1, 16))),
        "value_bias_rows": centred(key_list[8], (KEY_VALUE_HEADS, HEAD_SIZE), 0.5, 3.0, ((0, 2), (1, 16))),
        "w_out": centred(key_list[9], (QUERY_HEADS * HEAD_SIZE, MODEL_WIDTH), 16 ** -0.5, 1.5, ((0, 2), (1, 16))),
        "norm_mlp": jnp.clip(1.0 + 0.1 * jax.random.normal(key_list[10], (MODEL_WIDTH,), jnp.float32), 0.5, 1.5).astype(jnp.bfloat16),
        "w_gate": centred(key_list[11], (MODEL_WIDTH, FF), MODEL_WIDTH ** -0.5, 0.15625, ((0, 16), (1, 2))),
        "w_up": centred(key_list[12], (MODEL_WIDTH, FF), MODEL_WIDTH ** -0.5, 0.15625, ((0, 16), (1, 2))),
        "w_down": centred(key_list[13], (FF, MODEL_WIDTH), FF ** -0.5, 0.0625, ((0, 2), (1, 16))),
        "cotangent": centred(key_list[14], (ROWS, ROW, MODEL_WIDTH), 1.0, 6.0, ((0, 2), (1, 8))),
    }


NORM_EPS = 1e-06
ROPE_BASE = 10000.0
MASKED = -1e+30
HIGHEST = lax.Precision.HIGHEST

@jax.custom_vjp
def lower_bound(v):
    return lax.optimization_barrier(v.astype(jnp.bfloat16)).astype(jnp.float32)

@jax.custom_vjp
def low_back(v):
    return v

def low_keep(v):
    return (lower_bound(v), None)

def low_pass(kept, grad):
    return (grad,)

def back_keep(v):
    return (v, None)

def back_low(kept, grad):
    return (lower_bound(grad),)
lower_bound.defvjp(low_keep, low_pass)
low_back.defvjp(back_keep, back_low)

def row_positions(stored, shards, half_rows):
    slot_id = stored // half_rows
    inner = stored % half_rows
    shard_id = slot_id // 2
    row_block = jnp.where(slot_id % 2 == 0, shard_id, 2 * shards - 1 - shard_id)
    return (row_block * half_rows + inner).astype(jnp.int32)

def doc_info(row_pos, doc_lengths):
    doc_ends = jnp.cumsum(doc_lengths).astype(jnp.int32)
    doc_starts = (doc_ends - doc_lengths).astype(jnp.int32)
    inside = (row_pos[:, None] >= doc_starts[None, :]) & (row_pos[:, None] < doc_ends[None, :])
    doc_ids = lax.optimization_barrier(jnp.sum(jnp.where(row_pos[:, None] >= doc_ends[None, :], 1, 0), axis=1)).astype(jnp.int32)
    offsets = lax.optimization_barrier(jnp.sum(jnp.where(inside, doc_starts[None, :], 0), axis=1)).astype(jnp.int32)
    return (doc_ids, (row_pos - offsets).astype(jnp.int32))

def rotary(doc_pos, head_dim):
    half_dim = head_dim // 2
    freqs = ROPE_BASE ** (-2.0 * jnp.arange(half_dim, dtype=jnp.float32) / head_dim)
    angles = doc_pos.astype(jnp.float32)[:, None] * freqs[None, :]
    return (jnp.cos(angles), jnp.sin(angles))

def apply_rotation(values, cosine_table, sine_table):
    half_dim = values.shape[-1] // 2
    first_half = values[..., :half_dim]
    second_half = values[..., half_dim:]
    cos_b = cosine_table[:, None, :]
    sin_b = sine_table[:, None, :]
    return jnp.concatenate([first_half * cos_b - second_half * sin_b, second_half * cos_b + first_half * sin_b], axis=-1)

def rms_norm(resid, gain):
    return resid * lax.rsqrt(lax.optimization_barrier(jnp.mean(resid * resid, axis=-1, keepdims=True)) + NORM_EPS) * gain

def layer_row(resid, doc_ids, doc_pos, params):
    norm_attn, w_query, key_weight_matrix, value_weight_matrix, b_query, key_bias_rows, value_bias_rows, w_out, norm_mlp, w_gate, w_up, w_down = params
    sequence_length = resid.shape[0]
    query_group_count = QUERY_HEADS // KEY_VALUE_HEADS
    cosine_table, sine_table = rotary(doc_pos, HEAD_SIZE)
    normed = lower_bound(rms_norm(resid, norm_attn))
    query_linear = low_back(jnp.dot(normed, w_query, precision=HIGHEST) + b_query.reshape(-1))
    key_linear = low_back(jnp.dot(normed, key_weight_matrix, precision=HIGHEST) + key_bias_rows.reshape(-1))
    value_linear = low_back(jnp.dot(normed, value_weight_matrix, precision=HIGHEST) + value_bias_rows.reshape(-1))
    query_rows = lower_bound(apply_rotation(query_linear.reshape(sequence_length, QUERY_HEADS, HEAD_SIZE), cosine_table, sine_table)).reshape(sequence_length, KEY_VALUE_HEADS, query_group_count, HEAD_SIZE)
    key_heads_full = lower_bound(apply_rotation(key_linear.reshape(sequence_length, KEY_VALUE_HEADS, HEAD_SIZE), cosine_table, sine_table))
    value_heads_full = lower_bound(value_linear.reshape(sequence_length, KEY_VALUE_HEADS, HEAD_SIZE))
    q_block = min(512, sequence_length)
    positions = jnp.arange(sequence_length, dtype=jnp.int32)

    def attend(first_row):
        q_part = lax.dynamic_slice_in_dim(query_rows, first_row, q_block, 0)
        q_rows = first_row + jnp.arange(q_block, dtype=jnp.int32)
        q_docs = lax.dynamic_slice_in_dim(doc_ids, first_row, q_block, 0)
        scores = low_back(jnp.einsum('qkgd,tkd->kgqt', q_part, key_heads_full, precision=HIGHEST) * HEAD_SIZE ** (-0.5))
        allowed = (q_docs[:, None] == doc_ids[None, :]) & (positions[None, :] <= q_rows[:, None])
        scores = jnp.where(allowed, scores, MASKED)
        row_max = lax.optimization_barrier(jnp.max(scores, axis=-1, keepdims=True))
        exp_scores = jnp.where(allowed, jnp.exp(scores - row_max), 0.0)
        weights = lower_bound(exp_scores / lax.optimization_barrier(jnp.sum(exp_scores, axis=-1, keepdims=True)))
        return jnp.einsum('kgqt,tkd->qkgd', weights, value_heads_full, precision=HIGHEST)
    firsts = jnp.arange(sequence_length // q_block, dtype=jnp.int32) * q_block
    attended = lax.map(jax.checkpoint(attend), firsts).reshape(sequence_length, QUERY_HEADS * HEAD_SIZE)
    attended = low_back(lower_bound(attended))
    mid_resid = resid + low_back(jnp.dot(attended, w_out, precision=HIGHEST))
    normed_mlp = lower_bound(rms_norm(mid_resid, norm_mlp))
    gate_lin = low_back(jnp.dot(normed_mlp, w_gate, precision=HIGHEST))
    up_lin = low_back(jnp.dot(normed_mlp, w_up, precision=HIGHEST))
    hidden_mid = lower_bound(jax.nn.silu(gate_lin) * up_lin)
    return mid_resid + jnp.dot(hidden_mid, w_down, precision=HIGHEST)

def reference(hidden, lengths, norm_attn, w_query, key_weight_matrix, value_weight_matrix, b_query, key_bias_rows, value_bias_rows, w_out, norm_mlp, w_gate, w_up, w_down, cotangent):
    row_order = row_positions(jnp.arange(ROW, dtype=jnp.int32), N_SEQ, TOK_DEV // 2)
    resid_rows = jnp.zeros((ROWS, ROW, MODEL_WIDTH), jnp.float32).at[:, row_order].set(hidden.astype(jnp.float32))
    grad_rows = jnp.zeros((ROWS, ROW, MODEL_WIDTH), jnp.float32).at[:, row_order].set(cotangent.astype(jnp.float32))
    positions = jnp.arange(ROW, dtype=jnp.int32)
    doc_tables = [doc_info(positions, lengths[row_index]) for row_index in range(ROWS)]
    params = tuple((weight.astype(jnp.float32) for weight in (norm_attn, w_query, key_weight_matrix, value_weight_matrix, b_query, key_bias_rows, value_bias_rows, w_out, norm_mlp, w_gate, w_up, w_down)))

    def forward(resid_all, weights_all):
        outputs = [layer_row(resid_all[row_index], doc_tables[row_index][0], doc_tables[row_index][1], weights_all) for row_index in range(ROWS)]
        return jnp.stack(outputs)
    result, pull_back = jax.vjp(forward, resid_rows, params)
    grad_resid, grad_params = pull_back(grad_rows)
    output = result[:, row_order].astype(jnp.bfloat16)
    grad_hidden = grad_resid[:, row_order]
    return (output, grad_hidden, grad_params[0], grad_params[1], grad_params[2], grad_params[3], grad_params[4], grad_params[5], grad_params[6], grad_params[7], grad_params[8], grad_params[9], grad_params[10], grad_params[11])
```

```python
import functools

import jax
import jax.numpy as jnp
from jax import lax
from jax.experimental import pallas as pl
from jax.experimental.pallas import tpu as pltpu
from jax.sharding import Mesh
from jax.sharding import PartitionSpec as P

HEAD_SIZE = 128
NORM_EPS = 1e-06
ROPE_BASE = 10000.0
MASKED = -1e30
FLOOR = -1e29
FC = 256
BF = jnp.bfloat16
F32 = jnp.float32
VMEM = pl.BlockSpec(memory_space=pltpu.VMEM)


def row_positions(stored, shards, half_rows):
    slot_id = stored // half_rows
    inner = stored % half_rows
    shard_id = slot_id // 2
    row_block = jnp.where(slot_id % 2 == 0, shard_id, 2 * shards - 1 - shard_id)
    return row_block * half_rows + inner


def doc_starts_of(row_pos, doc_lengths):
    doc_ends = jnp.cumsum(doc_lengths)
    doc_starts = doc_ends - doc_lengths
    inside = (row_pos[:, None] >= doc_starts[None, :]) & (row_pos[:, None] < doc_ends[None, :])
    return jnp.sum(jnp.where(inside, doc_starts[None, :], 0), axis=1).astype(jnp.int32)


def rotary(doc_pos, head_dim):
    half_dim = head_dim // 2
    freqs = ROPE_BASE ** (-2.0 * jnp.arange(half_dim, dtype=jnp.float32) / head_dim)
    angles = doc_pos.astype(jnp.float32)[:, None] * freqs[None, :]
    return (jnp.cos(angles), jnp.sin(angles))


def norm_factor(resid):
    return lax.rsqrt(jnp.mean(resid * resid, axis=-1, keepdims=True) + NORM_EPS)


def norm_backward(resid, factor, gain, grad_in):
    weighted = grad_in * gain
    grad_resid = factor * weighted - resid * factor**3 * jnp.mean(
        weighted * resid, axis=-1, keepdims=True
    )
    grad_gain = jnp.sum(grad_in * resid * factor, axis=0, keepdims=True)
    return (grad_resid, grad_gain)


def dot(a, b):
    return jnp.dot(a, b, preferred_element_type=F32)


def dot_nt(a, b):
    return lax.dot_general(a, b, (((1,), (1,)), ((), ())), preferred_element_type=F32)


def block_mask(sub, block, me, shards, half, start_row, heads):
    key_blk = jnp.where(sub == 0, block, 2 * shards - 1 - block)
    query_blk = jnp.where(sub == 0, me, 2 * shards - 1 - me)
    key_pos = key_blk * half + lax.broadcasted_iota(jnp.int32, (half, half), 0)
    query_pos = query_blk * half + lax.broadcasted_iota(jnp.int32, (half, half), 1)
    allowed = (key_pos <= query_pos) & (key_pos >= start_row)
    return jnp.concatenate([jnp.where(allowed, 0.0, MASKED).astype(F32)] * heads, axis=1)


def stack_heads(ref, sub, half, heads):
    return jnp.concatenate(
        [
            ref[sub * half : (sub + 1) * half, h * HEAD_SIZE : (h + 1) * HEAD_SIZE]
            for h in range(heads)
        ],
        axis=0,
    )


class Pool:
    def __init__(self, ref):
        self.ref, self.used = ref, 0

    def take(self, count=1):
        base = self.used
        self.used += count
        assert self.used <= self.ref.shape[0], self.used
        return lambda i=0: self.ref.at[base + i]


def merge_rows(value):
    homes, rows, cols = value.shape
    if rows % 16:
        return value.astype(F32).reshape(homes * rows, cols).astype(BF)
    return value.reshape(homes * rows, cols)


class Spread:
    def __init__(self, zs, src, buf, pool):
        self.zs, self.src, self.buf = zs, src, buf
        self.b, self.z, self.x = (lax.axis_index(a) for a in ("batch", "z", "x"))
        self.up_s, self.dn_s, self.z_r, self.x_s, self.x_r = (pool.take(zs) for _ in range(5))
        self.s_s, self.s_r = pool.take(2 * zs), pool.take(2 * zs)
        self.loc = pool.take()

    def at(self, b, z, x):
        return self.buf.at[(b * self.zs + z) * 2 + x]

    def up(self, s, src=None):
        dst = self.at(self.b, s, self.x)
        src = dst if src is None else src
        return remote(src, dst, self.up_s(s), self.z_r(s), {"z": self.z + 1})

    def dn(self, s, src=None):
        dst = self.at(self.b, s, self.x)
        src = dst if src is None else src
        return remote(src, dst, self.dn_s(s), self.z_r(s), {"z": self.z - 1})

    def side(self, s, src=None):
        dst = self.at(self.b, s, self.x)
        src = dst if src is None else src
        return remote(src, dst, self.x_s(s), self.x_r(s), {"x": 1 - self.x})

    def sib(self, s, far=0, src=None):
        dst = self.at(self.b, s, self.x if far == 0 else 1 - self.x)
        src = dst if src is None else src
        i = far * self.zs + s
        return remote(src, dst, self.s_s(i), self.s_r(i), {"batch": 1 - self.b})

    def local(self):
        return pltpu.make_async_copy(self.src, self.at(self.b, self.z, self.x), self.loc())

    def start(self):
        @pl.when(self.z < self.zs - 1)
        def _():
            self.up(self.z, self.src).start()

        @pl.when(self.z > 0)
        def _():
            self.dn(self.z, self.src).start()

        self.side(self.z, self.src).start()
        self.sib(self.z, 0, self.src).start()
        self.local().start()

    def hop(self, k):
        low, high = self.z - k, self.z + k

        @pl.when(low >= 0)
        def _():
            self.dn(low).wait_recv()

            @pl.when(self.z < self.zs - 1)
            def _():
                self.up(low).start()

            self.side(low).start()
            self.sib(low).start()

        @pl.when(high < self.zs)
        def _():
            self.dn(high).wait_recv()

            @pl.when(self.z > 0)
            def _():
                self.dn(high).start()

            self.side(high).start()
            self.sib(high).start()

    def cross(self):
        for s in range(self.zs):
            dst = self.at(self.b, s, 1 - self.x)
            remote(dst, dst, self.x_s(s), self.x_r(s), {"x": 1 - self.x}).wait_recv()
            self.sib(s, 1).start()

    def finish(self):
        self.local().wait()
        for far in range(2):
            for s in range(self.zs):
                dst = self.at(1 - self.b, s, self.x if far == 0 else 1 - self.x)
                i = far * self.zs + s
                remote(dst, dst, self.s_s(i), self.s_r(i), {"batch": 1 - self.b}).wait_recv()

    def drain(self):
        for s in range(self.zs):

            @pl.when((s <= self.z) & (self.z < self.zs - 1))
            def _():
                self.up(s).wait_send()

            @pl.when((s >= self.z) & (self.z > 0))
            def _():
                self.dn(s).wait_send()

            self.side(s).wait_send()
            self.sib(s, 0).wait_send()
            self.sib(s, 1).wait_send()


def lanes(vec, first, count):
    return jnp.concatenate([vec[r : r + 1, :] for r in range(first, first + count)], axis=1)


def thirds(zs):
    hops = list(range(1, zs))
    per = -(-len(hops) // 3)
    return [hops[i * per : (i + 1) * per] for i in range(3)]


def forward_kernel(
    zs,
    heads,
    n1,
    skip,
    scale,
    x_ref,
    wqkv_in,
    wo_in,
    small_in,
    cos_ref,
    sin_ref,
    start_ref,
    dy_in,
    *refs,
):
    refs = list(refs)
    if n1:
        mats = refs[:3]
        del refs[:3]
    h1_out, q_out, attn_out, lse_out, mid_out, vec_out = refs[:6]
    wqkv_all, wo_all, kv_all, h2_all, dy_all = refs[6:11]
    del refs[:11]
    if n1:
        full = refs.pop(0)
    small_buf, wqkv_buf, wo_buf, kv_buf, q_t, acc_ref, max_ref, sum_ref = refs[:8]
    att_send, att_recv, h2_half, xn_ref, sem_ref = refs[8:13]
    g_sems = refs[13:]
    b, z, x, t = (lax.axis_index(a) for a in ("batch", "z", "x", "tensor"))
    shards = 2 * zs
    me = 2 * z + x
    tok, width = x_ref.shape
    half = tok // 2
    q_cols = heads * HEAD_SIZE
    pool = Pool(sem_ref)
    greet(z, zs)

    small = Spread(zs, small_in, small_buf, pool)
    wqkv = Spread(zs, wqkv_in, wqkv_buf, pool)
    wo = Spread(zs, wo_in, wo_buf, pool)
    small.start()
    wqkv.start()
    wo.start()

    runs = thirds(zs)
    if n1:
        trade = Exchange(mats, full, 0, zs, skip, [pool.take(n1) for _ in range(3)])
        gather = Gather(zs, None, full, [None] + list(g_sems))
        for c in range(n1):
            trade.keep(c, c)

    def ship(first, last):
        if n1:
            for c in range(first, last):
                trade.ship(c, c)

    def prefetch(tick):
        if n1:
            for c in range(n1):
                hops = [k for k in range(1, zs) if min(k, 3) == tick - c]
                if tick == c:
                    trade.arrived(c, c)
                    gather.start(c)
                for k in hops:
                    gather.hop(c, k)

    quarter = half // 2
    dy_l, dyy_s, dyy_r = (pool.take() for _ in range(3))
    dyx_s, dyx_r = pool.take(3), pool.take(3)
    dy_own = pltpu.make_async_copy(dy_in, dy_all.at[pl.ds(2 * x, 2)], dy_l())
    dy_own.start()

    def dy_side(i):
        rows = pl.ds((i % 3 > 0) * quarter, quarter)
        block = t if i < 2 else 1 - t
        dst = dy_all.at[2 * x + block, rows]
        return remote(dy_in.at[block, rows], dst, dyx_s(i), dyx_r(i), {"x": 1 - x})

    dy_piece = dy_all.at[2 * (1 - x) + t, pl.ds(0, quarter)]
    dy_across = remote(dy_piece, dy_piece, dyy_s(), dyy_r(), {"tensor": 1 - t})

    ship(0, 2)
    for m in range(2):
        at = slice(m * half, (m + 1) * half)
        xv = x_ref[at].astype(F32)
        xn_ref[at] = xv * norm_factor(xv)
    for k in range(1, zs):
        small.hop(k)
        wqkv.hop(k)
    prefetch(0)
    ship(2, 3)
    for k in runs[0]:
        wo.hop(k)
    small.cross()
    small.finish()
    vec = jnp.sum(small_buf[...].astype(F32), axis=0)
    vec_out[...] = vec
    bias = lanes(vec, 0, 4)
    gain_attn = lanes(vec, 4, 6)
    gain_mlp = lanes(vec, 10, 6)
    for m in range(2):
        at = slice(m * half, (m + 1) * half)
        h1_out[at] = (xn_ref[at] * gain_attn).astype(BF)

    wqkv.cross()
    prefetch(1)
    wqkv.finish()
    wqkv_m = merge_rows(wqkv_buf[...])
    for m in range(2):
        at = slice(m * half, (m + 1) * half)
        lin = dot(h1_out[at], wqkv_m) + bias
        cos, sin = cos_ref[at], sin_ref[at]
        for h in range(heads + 1):
            v = lin[:, h * HEAD_SIZE : (h + 1) * HEAD_SIZE]
            v = (v * cos + pltpu.roll(v, HEAD_SIZE // 2, 1) * sin).astype(BF)
            if h < heads:
                q_out[at, h * HEAD_SIZE : (h + 1) * HEAD_SIZE] = v
            else:
                kv_buf[me + m, :, :HEAD_SIZE] = v
        kv_buf[me + m, :, HEAD_SIZE:] = lin[:, (heads + 1) * HEAD_SIZE :].astype(BF)

    ku_s, kd_s, k0_r, k1_r, x0_s, x1_s, x0_r, x1_r = (pool.take(zs) for _ in range(8))

    def kv_up(s):
        piece = kv_buf.at[2 * s + x]
        return remote(piece, piece, ku_s(s), k0_r(s), {"z": z + 1})

    def kv_dn(s):
        piece = kv_buf.at[2 * s + x + 1]
        return remote(piece, piece, kd_s(s), k1_r(s), {"z": z - 1})

    def kv_side(s, sub, col):
        piece = kv_buf.at[2 * s + col + sub]
        send, recv = (x0_s, x0_r) if sub == 0 else (x1_s, x1_r)
        return remote(piece, piece, send(s), recv(s), {"x": 1 - x})

    @pl.when(z < zs - 1)
    def _():
        kv_up(z).start()

    @pl.when(z > 0)
    def _():
        kv_dn(z).start()

    @pl.when(x == 0)
    def _():
        kv_side(z, 0, x).start()

    @pl.when(x == 1)
    def _():
        kv_side(z, 1, x).start()

    for k in runs[1]:
        wo.hop(k)
    for sub in range(2):
        q_t[sub] = stack_heads(q_out, sub, half, heads).T
    acc_ref[...] = jnp.zeros_like(acc_ref)
    max_ref[...] = jnp.full_like(max_ref, FLOOR)
    sum_ref[...] = jnp.zeros_like(sum_ref)

    def fold(sub, block):
        keys = kv_buf[block + sub, :, :HEAD_SIZE]
        vals = kv_buf[block + sub, :, HEAD_SIZE:]
        start_row = start_ref[:, sub * half : (sub + 1) * half]
        scores = dot(keys, q_t[sub]) * scale + block_mask(
            sub, block, me, shards, half, start_row, heads
        )
        old_max = max_ref[sub]
        new_max = jnp.maximum(old_max, jnp.max(scores, axis=0, keepdims=True))
        weights = jnp.exp(scores - new_max)
        shrink = jnp.exp(old_max - new_max)
        max_ref[sub] = new_max
        sum_ref[sub] = sum_ref[sub] * shrink + jnp.sum(weights, axis=0, keepdims=True)
        acc_ref[sub] = acc_ref[sub] * shrink + dot(vals.T, weights.astype(BF))

    def attend(k, carry):
        low, high = z - k, z + k

        @pl.when((low >= 0) & (k < zs))
        def _():
            @pl.when(k > 0)
            def _():
                kv_up(low).wait_recv()

                @pl.when(z < zs - 1)
                def _():
                    kv_up(low).start()

                kv_side(low, 0, x).start()

        @pl.when((high < zs) & (k < zs))
        def _():
            @pl.when(k > 0)
            def _():
                kv_dn(high).wait_recv()

                @pl.when(z > 0)
                def _():
                    kv_dn(high).start()

                kv_side(high, 1, x).start()

        @pl.when((low >= 0) & (k < zs))
        def _():
            fold(0, 2 * low + x)

        @pl.when((high < zs) & (k < zs))
        def _():
            fold(1, 2 * high + x)

        far_low, far_high = low + 1, high - 1

        @pl.when((k > 0) & (far_low >= 0) & ((k > 1) | (x == 1)))
        def _():
            kv_side(far_low, 0, 1 - x).wait_recv()
            fold(0, 2 * far_low + 1 - x)

        @pl.when((k > 0) & (far_high < zs) & ((k > 1) | (x == 0)))
        def _():
            kv_side(far_high, 1, 1 - x).wait_recv()
            fold(1, 2 * far_high + 1 - x)

        @pl.when(k == 1)
        def _():
            for hop in runs[2]:
                wo.hop(hop)

        @pl.when(k == 2)
        def _():
            prefetch(2)

        @pl.when(k == zs - 1)
        def _():
            ship(3, n1)

        return carry

    lax.fori_loop(0, zs + 1, attend, 0)
    wo.cross()
    for sub in range(2):
        lse_out[sub : sub + 1, :] = max_ref[sub] + jnp.log(sum_ref[sub])
        out_t = acc_ref[sub] / sum_ref[sub]
        for h in range(heads):
            attn_out[sub * half : (sub + 1) * half, h * HEAD_SIZE : (h + 1) * HEAD_SIZE] = (
                out_t[:, h * half : (h + 1) * half].T.astype(BF)
            )

    dy_side(1).start()
    dy_side(0).start()
    wo.finish()
    att_s, att_r = pool.take(2), pool.take(2)
    h_l, hx_s, hx_r, hy_s, hy_r = (pool.take(2) for _ in range(5))
    hxx_s, hxx_r, hyy_s, hyy_r = (pool.take() for _ in range(4))

    def rows(i):
        return pl.ds(i * quarter, quarter)

    def att_copy(i):
        to = {"tensor": 1 - t}
        return remote(att_send.at[rows(i)], att_recv.at[rows(i)], att_s(i), att_r(i), to)

    def h_copies(i):
        src, dst = h2_half.at[rows(i)], h2_all.at[2 * x + t, rows(i)]
        return (
            pltpu.make_async_copy(src, dst, h_l(i)),
            remote(src, dst, hx_s(i), hx_r(i), {"x": 1 - x}),
            remote(src, dst, hy_s(i), hy_r(i), {"tensor": 1 - t}),
        )

    wo_m = merge_rows(wo_buf[...])
    for i in range(2):
        at = pl.ds(pl.multiple_of((1 - t) * half + i * quarter, quarter), quarter)
        att_send[rows(i)] = dot_nt(attn_out[at], wo_m).astype(BF)
        att_copy(i).start()
    for i in range(2):
        at = pl.ds(pl.multiple_of(t * half + i * quarter, quarter), quarter)
        mid_out[rows(i)] = dot_nt(attn_out[at], wo_m) + x_ref[at].astype(F32)
    prefetch(3)
    for i in range(2):
        att_copy(i).wait_recv()
        mid = mid_out[rows(i)] + att_recv[rows(i)].astype(F32)
        mid_out[rows(i)] = mid
        h2_half[rows(i)] = (mid * norm_factor(mid) * gain_mlp).astype(BF)
        for copy in h_copies(i):
            copy.start()
    from_side = h2_all.at[2 * (1 - x) + t, rows(0)]
    from_across = h2_all.at[2 * x + 1 - t, rows(1)]
    relay_across = remote(from_side, from_side, hyy_s(), hyy_r(), {"tensor": 1 - t})
    relay_side = remote(from_across, from_across, hxx_s(), hxx_r(), {"x": 1 - x})
    h_copies(0)[1].wait_recv()
    relay_across.start()
    dy_side(0).wait_recv()
    dy_across.start()
    prefetch(4)
    dy_side(2).start()
    h_copies(1)[2].wait_recv()
    relay_side.start()
    for tick in range(5, n1 + 3):
        prefetch(tick)

    save = pool.take(3)
    saves = [
        pltpu.make_async_copy(src, dst, save(i))
        for i, (src, dst) in enumerate(
            ((wqkv_buf, wqkv_all), (wo_buf, wo_all), (kv_buf, kv_all))
        )
    ]
    for copy in saves:
        copy.start()

    for item in (small, wqkv, wo):
        item.drain()

    def kv_drain(s, carry):
        @pl.when((s <= z) & (z < zs - 1))
        def _():
            kv_up(s).wait_send()

        @pl.when((s >= z) & (z > 0))
        def _():
            kv_dn(s).wait_send()

        @pl.when((s < z) | ((s == z) & (x == 0)))
        def _():
            kv_side(s, 0, x).wait_send()

        @pl.when((s > z) | ((s == z) & (x == 1)))
        def _():
            kv_side(s, 1, x).wait_send()

        return carry

    lax.fori_loop(0, zs, kv_drain, 0)
    relay_across.wait()
    relay_side.wait()
    dy_across.wait()
    for i in range(3):
        dy_side(i).wait_send()
        if i > 0:
            dy_side(i).wait_recv()
    for i in range(2):
        att_copy(i).wait_send()
        own, side, across = h_copies(i)
        own.wait()
        side.wait_send()
        across.wait_send()
    h_copies(1)[1].wait_recv()
    h_copies(0)[2].wait_recv()
    if n1:
        for c in range(n1):
            trade.sent(c, c)
            gather.finish(c)
            gather.drain(c)
    for copy in saves + [dy_own]:
        copy.wait()


def forward_call(
    zs, heads, n1, skip, fc, x_in, wqkv_in, wo_in, small_in, cos, sin, start, dy_in, first
):
    tok, width = x_in.shape
    half = tok // 2
    homes = 4 * zs
    rows, qkv_cols = wqkv_in.shape
    q_cols = heads * HEAD_SIZE
    shape = jax.ShapeDtypeStruct
    any_spec = pl.BlockSpec(memory_space=pl.ANY)
    out = [
        shape((tok, width), BF),
        shape((tok, q_cols), BF),
        shape((tok, q_cols), BF),
        shape((2, heads * half), F32),
        shape((half, width), F32),
        shape(small_in.shape, F32),
        shape((homes, rows, qkv_cols), BF),
        shape((homes, rows, q_cols), BF),
        shape((2 * zs + 1, half, 2 * HEAD_SIZE), BF),
        shape((4, half, width), BF),
        shape((4, half, width), BF),
    ]
    sems = [pltpu.SemaphoreType.DMA((3 * (9 * zs + 1) + 8 * zs + 3 * n1 + 36,))]
    if n1:
        out.append(shape((n1, width, 3 * fc), BF))
        sems += [pltpu.SemaphoreType.DMA((n1, zs))] * 5
    return pl.pallas_call(
        functools.partial(forward_kernel, zs, heads, n1, skip, HEAD_SIZE ** (-0.5)),
        out_shape=out,
        in_specs=[VMEM] + [any_spec] * 3 + [VMEM] * (4 + len(first)),
        out_specs=[VMEM] * 6 + [any_spec] * (len(out) - 6),
        scratch_shapes=[
            pltpu.VMEM((homes,) + small_in.shape, BF),
            pltpu.VMEM((homes, rows, qkv_cols), BF),
            pltpu.VMEM((homes, rows, q_cols), BF),
            pltpu.VMEM((2 * zs + 1, half, 2 * HEAD_SIZE), BF),
            pltpu.VMEM((2, HEAD_SIZE, heads * half), BF),
            pltpu.VMEM((2, HEAD_SIZE, heads * half), F32),
            pltpu.VMEM((2, 1, heads * half), F32),
            pltpu.VMEM((2, 1, heads * half), F32),
            pltpu.VMEM((half, width), BF),
            pltpu.VMEM((half, width), BF),
            pltpu.VMEM((half, width), BF),
            pltpu.VMEM((tok, width), F32),
        ]
        + sems,
        compiler_params=pltpu.CompilerParams(
            collective_id=1, has_side_effects=True, vmem_limit_bytes=60 * 2**20
        ),
        cost_estimate=pl.CostEstimate(
            flops=2 * tok * width * (qkv_cols + q_cols) + 2**31,
            bytes_accessed=32 * 2**20,
            transcendentals=0,
        ),
    )(x_in, wqkv_in, wo_in, small_in, cos, sin, start, dy_in, *first)


class Square:
    def __init__(self, src, own, r_one, r_two, pool):
        self.src, self.own, self.r_one, self.r_two = src, own, r_one, r_two
        self.x, self.t = lax.axis_index("x"), lax.axis_index("tensor")
        self.cut = src.shape[2] // 2
        self.one_s, self.one_r = pool.take(3), pool.take(3)
        self.two_s, self.two_r = pool.take(2), pool.take(2)
        self.load = pool.take(3)

    def first(self):
        x, t, cut, src = self.x, self.t, self.cut, self.src
        left, right = pl.ds(0, cut), pl.ds(cut, cut)
        sends = [
            remote(
                src.at[pl.ds(2 * (1 - x), 2), :, left],
                self.r_one.at[pl.ds(0, 2)],
                self.one_s(0),
                self.one_r(0),
                {"x": 1 - x},
            )
        ]
        for i in range(2):
            sends.append(
                remote(
                    src.at[2 * i + 1 - t, :, right],
                    self.r_one.at[2 + i],
                    self.one_s(1 + i),
                    self.one_r(1 + i),
                    {"tensor": 1 - t},
                )
            )
        return sends

    def loads(self):
        x, t, cut, src = self.x, self.t, self.cut, self.src
        left, right = pl.ds(0, cut), pl.ds(cut, cut)
        loads = [
            pltpu.make_async_copy(
                src.at[pl.ds(2 * x, 2), :, left], self.own.at[pl.ds(0, 2)], self.load(0)
            )
        ]
        for i in range(2):
            loads.append(
                pltpu.make_async_copy(
                    src.at[2 * i + t, :, right], self.own.at[2 + i], self.load(1 + i)
                )
            )
        return loads

    def second(self):
        x, t = self.x, self.t
        return [
            remote(
                self.own.at[1 - t],
                self.r_two.at[0],
                self.two_s(0),
                self.two_r(0),
                {"tensor": 1 - t},
            ),
            remote(
                self.own.at[3 - x],
                self.r_two.at[1],
                self.two_s(1),
                self.two_r(1),
                {"x": 1 - x},
            ),
        ]

    def start(self):
        for copy in self.first() + self.loads():
            copy.start()

    def turn(self):
        for copy in self.loads():
            copy.wait()
        for copy in self.first():
            copy.wait_recv()
        for i in range(4):
            self.own[i] = (self.own[i].astype(F32) + self.r_one[i].astype(F32)).astype(BF)
        for copy in self.second():
            copy.start()

    def result(self):
        for copy in self.second():
            copy.wait_recv()
        left = self.own[self.t].astype(F32) + self.r_two[0].astype(F32)
        right = self.own[2 + self.x].astype(F32) + self.r_two[1].astype(F32)
        return jnp.concatenate([left, right], axis=1)

    def drain(self):
        for copy in self.first() + self.second():
            copy.wait_send()


class Collect:
    def __init__(self, zs, acc, to_sib, r_sib, r_x, r_z, out, pool):
        self.zs, self.acc, self.to_sib, self.r_sib = zs, acc, to_sib, r_sib
        self.r_x, self.r_z, self.out = r_x, r_z, out
        self.b, self.z, self.x = (lax.axis_index(a) for a in ("batch", "z", "x"))
        self.s_s, self.s_r, self.x_s, self.x_r, self.loc = (pool.take() for _ in range(5))
        self.d_s, self.d_r, self.u_s, self.u_r = (pool.take(zs) for _ in range(4))

    def sib(self):
        return remote(self.to_sib, self.r_sib, self.s_s(), self.s_r(), {"batch": 1 - self.b})

    def side(self):
        return remote(
            self.acc.at[1 - self.x], self.r_x, self.x_s(), self.x_r(), {"x": 1 - self.x}
        )

    def dn(self, h):
        return remote(
            self.acc.at[self.x, h], self.r_z.at[h], self.d_s(h), self.d_r(h), {"z": self.z - 1}
        )

    def up(self, h):
        return remote(
            self.acc.at[self.x, h], self.r_z.at[h + 1], self.u_s(h), self.u_r(h), {"z": self.z + 1}
        )

    def fill(self, make):
        rows = self.acc.shape[2]
        for buf, core in ((self.to_sib, 1 - self.b), (self.acc, self.b)):
            value = make(core)
            for h in range(self.zs):
                for col in range(2):
                    i = 2 * h + col
                    buf[col, h] = value[i * rows : (i + 1) * rows].astype(BF)
            if buf is self.to_sib:
                self.sib().start()

    def add(self, dst, src):
        dst[...] = (dst[...].astype(F32) + src[...].astype(F32)).astype(BF)

    def after_sib(self):
        self.sib().wait_recv()

        def one(h, carry):
            self.add(self.acc.at[1 - self.x, h], self.r_sib.at[1 - self.x, h])
            return carry

        lax.fori_loop(0, self.zs, one, 0)
        self.side().start()

        def other(h, carry):
            self.add(self.acc.at[self.x, h], self.r_sib.at[self.x, h])
            return carry

        lax.fori_loop(0, self.zs, other, 0)

    def after_side(self):
        self.side().wait_recv()

        def one(h, carry):
            self.add(self.acc.at[self.x, h], self.r_x.at[h])
            return carry

        lax.fori_loop(0, self.zs, one, 0)

        def ends(h, carry):
            @pl.when((self.z == self.zs - 1) & (h < self.z))
            def _():
                self.dn(h).start()

            @pl.when((self.z == 0) & (h > 0))
            def _():
                self.up(h).start()

            return carry

        lax.fori_loop(0, self.zs, ends, 0)

    def step(self, k):
        def one(i, carry):
            @pl.when((self.z == self.zs - 1 - k) & (i <= self.z))
            def _():
                self.dn(i).wait_recv()
                self.add(self.acc.at[self.x, i], self.r_z.at[i])

                @pl.when(i < self.z)
                def _():
                    self.dn(i).start()

            j = self.zs - 1 - i

            @pl.when((self.z == k) & (j >= self.z))
            def _():
                self.up(j).wait_recv()
                self.add(self.acc.at[self.x, j], self.r_z.at[j + 1])

                @pl.when(j > self.z)
                def _():
                    self.up(j).start()

            return carry

        lax.fori_loop(0, self.zs, one, 0)
        if k == self.zs - 1:
            self.result().start()

    def result(self):
        return pltpu.make_async_copy(self.acc.at[self.x, self.z], self.out, self.loc())

    def drain(self):
        self.sib().wait_send()
        self.side().wait_send()
        self.result().wait()

        def one(h, carry):
            @pl.when(h < self.z)
            def _():
                self.dn(h).wait_send()

            @pl.when(h > self.z)
            def _():
                self.up(h).wait_send()

            return carry

        lax.fori_loop(0, self.zs, one, 0)


class LineSum:
    def __init__(self, zs, acc, r_z, pool):
        self.zs, self.acc, self.r_z = zs, acc, r_z
        self.z = lax.axis_index("z")
        self.d_s, self.d_r, self.u_s, self.u_r = (pool.take(zs) for _ in range(4))

    def dn(self, h):
        to = {"z": self.z - 1}
        return remote(self.acc.at[:, h], self.r_z.at[:, h], self.d_s(h), self.d_r(h), to)

    def up(self, h):
        to = {"z": self.z + 1}
        return remote(self.acc.at[:, h], self.r_z.at[:, h + 1], self.u_s(h), self.u_r(h), to)

    def start(self):
        for h in range(self.zs):
            if h < self.zs - 1:

                @pl.when(self.z == self.zs - 1)
                def _():
                    self.dn(h).start()

            if h > 0:

                @pl.when(self.z == 0)
                def _():
                    self.up(self.zs - h).start()

    def plus(self, h, slot):
        for c in range(self.acc.shape[0]):
            total = self.acc[c, h].astype(F32) + self.r_z[c, slot].astype(F32)
            self.acc[c, h] = total.astype(BF)

    def step(self, k):
        def one(i, carry):
            @pl.when((self.z == self.zs - 1 - k) & (i <= self.z))
            def _():
                self.dn(i).wait_recv()
                self.plus(i, i)

                @pl.when(i < self.z)
                def _():
                    self.dn(i).start()

            j = self.zs - 1 - i

            @pl.when((self.z == k) & (j >= self.z))
            def _():
                self.up(j).wait_recv()
                self.plus(j, j + 1)

                @pl.when(j > self.z)
                def _():
                    self.up(j).start()

            return carry

        lax.fori_loop(0, self.zs, one, 0)

    def drain(self):
        def one(h, carry):
            @pl.when(h < self.z)
            def _():
                self.dn(h).wait_send()

            @pl.when(h > self.z)
            def _():
                self.up(h).wait_send()

            return carry

        lax.fori_loop(0, self.zs, one, 0)


def backward_kernel(zs, heads, nl, scale, *refs):
    refs = list(refs)

    def take(count):
        out = refs[:count]
        del refs[:count]
        return out

    y_in, g_mlp = take(2)
    if nl:
        (left_in,) = take(1)
    dh2_ref, mid_ref, vec_ref, x_ref, dy_ref, h1_ref, q_ref, attn_ref, lse_ref, kv_ref = take(10)
    wqkv_ref, wo_ref, cos_ref, sin_ref, start_ref = take(5)
    out_all, gh_all, g_q, g_kv, g_wo, g_vec, g_far = take(7)
    if nl:
        (left_out,) = take(1)
    y_own, y_one, y_two, dmid_ref, dat_ref, half_ref = take(6)
    q_s, do_s, q_t, do_t, delta_ref = take(5)
    dkv_ref, rx_ref, rz_ref, acc_ref, dqkv_ref, dh_send, dh_recv = take(7)
    bufs_q, bufs_kv, bufs_wo = take(5), take(5), take(5)
    vec_own, vec_recv, vec_z, sem_ref = take(4)
    if nl:
        left_acc, left_z = take(2)

    b, z, x, t = (lax.axis_index(a) for a in ("batch", "z", "x", "tensor"))
    shards = 2 * zs
    me = 2 * z + x
    half, width = mid_ref.shape
    q_cols = heads * HEAD_SIZE
    pool = Pool(sem_ref)
    greet(z, zs)

    sq_y = Square(y_in, y_own, y_one, y_two, pool)
    col_q = Collect(zs, *bufs_q, g_q, pool)
    col_kv = Collect(zs, *bufs_kv, g_kv, pool)
    col_wo = Collect(zs, *bufs_wo, g_wo, pool)
    runs = thirds(zs)
    if nl:
        lines = [
            LineSum(zs, left_acc.at[pl.ds(c, 1)], left_z.at[pl.ds(c, 1)], pool) for c in range(nl)
        ]
        left_l = pool.take()
        left_load = pltpu.make_async_copy(left_in, left_acc, left_l())
        left_load.start()

    def line_tick(tick):
        for c in range(nl):
            if tick == c:
                lines[c].start()
            for k in range(1, zs):
                if min(k, 3) == tick - c:
                    lines[c].step(k)

    vec = vec_ref[...]
    gain_attn = lanes(vec, 4, 6)
    gain_mlp = lanes(vec, 10, 6)

    mid = mid_ref[...]
    d_norm, g_norm_mlp = norm_backward(mid, norm_factor(mid), gain_mlp, dh2_ref[...])
    mine = pl.ds(pl.multiple_of(t * half, half), half)
    dmid_ref[...] = dy_ref[mine].astype(F32) + d_norm
    dat_ref[t] = dmid_ref[...].astype(BF)
    dat_s, dat_r = pool.take(), pool.take()

    def dat_copy(i):
        return remote(dat_ref.at[i], dat_ref.at[i], dat_s(), dat_r(), {"tensor": 1 - t})

    dat_copy(t).start()
    if nl:
        left_load.wait()
        line_tick(0)

    x0_s, x0_r, x1_s, x1_r = (pool.take(zs) for _ in range(4))
    c0_s, c0_r, c1_s, c1_r = (pool.take(zs) for _ in range(4))

    def side(s, sub):
        src = dkv_ref.at[2 * s + 1 - x + sub]
        send, recv = (x0_s, x0_r) if sub == 0 else (x1_s, x1_r)
        return remote(src, rx_ref.at[s + sub], send(s), recv(s), {"x": 1 - x})

    def chain(s, sub):
        src = dkv_ref.at[2 * s + x + sub]
        send, recv = (c0_s, c0_r) if sub == 0 else (c1_s, c1_r)
        to = z - 1 if sub == 0 else z + 1
        return remote(src, rz_ref.at[s + sub], send(s), recv(s), {"z": to})

    acc_ref[...] = jnp.zeros_like(acc_ref)

    def prepare(sub):
        d_out = dot(dat_ref[sub], merge_rows(wo_ref[...])).astype(BF)
        rows = pl.ds(pl.multiple_of(sub * half, half), half)
        out = attn_ref[rows]
        q = q_ref[rows]
        for h in range(heads):
            cols = slice(h * HEAD_SIZE, (h + 1) * HEAD_SIZE)
            at = slice(h * half, (h + 1) * half)
            q_s[sub, at] = q[:, cols]
            do_s[sub, at] = d_out[:, cols]
            q_t[sub, :, at] = q[:, cols].T
            do_h = d_out[:, cols].T
            do_t[sub, :, at] = do_h
            delta_ref[sub, :, at] = jnp.sum(
                do_h.astype(F32) * out[:, cols].T.astype(F32), axis=0, keepdims=True
            )

    def fold(sub, block):
        slot = block + sub
        keys = kv_ref[slot, :, :HEAD_SIZE]
        vals = kv_ref[slot, :, HEAD_SIZE:]
        scores = dot(keys, q_t[sub]) * scale + block_mask(
            sub, block, me, shards, half, start_ref[sub], heads
        )
        probs = jnp.exp(scores - lse_ref[sub])
        d_scores = (probs * (dot(vals, do_t[sub]) - delta_ref[sub])).astype(BF)
        dkv_ref[slot, :, HEAD_SIZE:] = dot(probs.astype(BF), do_s[sub]).astype(BF)
        dkv_ref[slot, :, :HEAD_SIZE] = (dot(d_scores, q_s[sub]) * scale).astype(BF)
        acc_ref[sub] += dot(keys.T, d_scores)

    def far_blocks(sub):
        def one(k, carry):
            s = jnp.where(sub == 0, z - k, z + k)

            @pl.when(in_range(s, zs) & ((k > 0) | (x != sub)))
            def _():
                fold(sub, 2 * s + 1 - x)

                @pl.when(sub == 0)
                def _():
                    side(s, 0).start()

                @pl.when(sub == 1)
                def _():
                    side(s, 1).start()

            return carry

        lax.fori_loop(0, zs, one, 0)

    def near_blocks(sub):
        def one(i, carry):
            k = zs - 1 - i
            s = jnp.where(sub == 0, z - k, z + k)

            @pl.when(in_range(s, zs))
            def _():
                fold(sub, 2 * s + x)

            return carry

        lax.fori_loop(0, zs, one, 0)

    def tokens(i, carry):
        sub = jnp.where(i == 0, t, 1 - t)

        @pl.when(i == 1)
        def _():
            line_tick(1)
            dat_copy(1 - t).wait_recv()

        prepare(sub)
        far_blocks(sub)
        near_blocks(sub)
        return carry

    lax.fori_loop(0, 2, tokens, 0)
    sq_y.start()

    def wo_part(core):
        rows = width // 2
        at = pl.ds(pl.multiple_of(core * rows, rows), rows)
        return dot(half_ref[at], attn_ref[...])

    def plus(slot, src):
        total = dkv_ref[slot].astype(F32) + src[...].astype(F32)
        dkv_ref[slot] = total.astype(BF)

    def kv_begin():
        def one(i, carry):
            j = zs - 1 - i

            @pl.when((i < z) | ((i == z) & (x == 0)))
            def _():
                side(i, 0).wait_recv()
                plus(2 * i + x, rx_ref.at[i])

            @pl.when((z == zs - 1) & (i < z))
            def _():
                chain(i, 0).start()

            @pl.when((j > z) | ((j == z) & (x == 1)))
            def _():
                side(j, 1).wait_recv()
                plus(2 * j + x + 1, rx_ref.at[j + 1])

            @pl.when((z == 0) & (j > z))
            def _():
                chain(j, 1).start()

            return carry

        lax.fori_loop(0, zs, one, 0)

    def kv_step(k):
        def one(i, carry):
            j = zs - 1 - i

            @pl.when((z == zs - 1 - k) & (i <= z))
            def _():
                chain(i, 0).wait_recv()
                plus(2 * i + x, rz_ref.at[i])

                @pl.when(i < z)
                def _():
                    chain(i, 0).start()

            @pl.when((z == k) & (j >= z))
            def _():
                chain(j, 1).wait_recv()
                plus(2 * j + x + 1, rz_ref.at[j + 1])

                @pl.when(j > z)
                def _():
                    chain(j, 1).start()

            return carry

        lax.fori_loop(0, zs, one, 0)

    kv_begin()
    for i in range(2):
        half_ref[:, i * half : (i + 1) * half] = dat_ref[i].T
    col_wo.fill(wo_part)


    def back(v, at):
        return v * cos_ref[at] - pltpu.roll(v, HEAD_SIZE // 2, 1) * sin_ref[at]

    for sub in range(2):
        at = slice(sub * half, (sub + 1) * half)
        for h in range(heads):
            v = acc_ref[sub, :, h * half : (h + 1) * half].T * scale
            dqkv_ref[at, h * HEAD_SIZE : (h + 1) * HEAD_SIZE] = back(v, at).astype(BF)
    half_ref[...] = h1_ref[...].T
    col_wo.after_sib()
    for k in runs[0]:
        kv_step(k)

    def part(first, last):
        def make(core):
            rows = width // 2
            at = pl.ds(pl.multiple_of(core * rows, rows), rows)
            return dot(half_ref[at], dqkv_ref[:, first:last])

        return make

    col_q.fill(part(0, q_cols))
    for k in runs[1]:
        kv_step(k)
    line_tick(2)
    for k in runs[2]:
        kv_step(k)
    for sub in range(2):
        at = slice(sub * half, (sub + 1) * half)
        dk = dkv_ref[me + sub, :, :HEAD_SIZE].astype(F32)
        dqkv_ref[at, q_cols : q_cols + HEAD_SIZE] = back(dk, at).astype(BF)
        dqkv_ref[at, q_cols + HEAD_SIZE :] = dkv_ref[me + sub, :, HEAD_SIZE:]

    dh_s, dh_r = pool.take(), pool.take()
    dh_copy = remote(dh_send, dh_recv, dh_s(), dh_r(), {"tensor": 1 - t})
    theirs = pl.ds(pl.multiple_of((1 - t) * half, half), half)
    own = pl.ds(pl.multiple_of(t * half, half), half)
    dh_send[...] = dot_nt(dqkv_ref[theirs], merge_rows(wqkv_ref[...])).astype(BF)
    dh_copy.start()
    col_kv.fill(part(q_cols, q_cols + 2 * HEAD_SIZE))
    dh1 = dot_nt(dqkv_ref[own], merge_rows(wqkv_ref[...]))
    col_q.after_sib()
    col_kv.after_sib()
    col_wo.after_side()
    sq_y.turn()
    line_tick(3)

    dh_copy.wait_recv()
    dh1 = dh1 + dh_recv[...].astype(F32)
    xv = x_ref[mine].astype(F32)
    d_norm, g_norm_attn = norm_backward(xv, norm_factor(xv), gain_attn, dh1)

    g_bias = jnp.sum(dqkv_ref[...].astype(F32), axis=0, keepdims=True)
    row = jnp.concatenate([g_bias, g_norm_attn, g_norm_mlp], axis=1)
    lane = vec_ref.shape[1]
    vec_own[...] = jnp.concatenate(
        [row[:, i * lane : (i + 1) * lane] for i in range(vec_ref.shape[0])], axis=0
    )
    v_s, v_r = pool.take(3), pool.take(3)
    vz_s, vz_r = pool.take(zs), pool.take(zs)
    norms = (lax.broadcasted_iota(jnp.int32, vec_ref.shape, 0) >= 4).astype(F32)

    def v_side(i):
        axis, index = (("tensor", t), ("x", x), ("batch", b))[i]
        return remote(vec_own, vec_recv.at[i], v_s(i), v_r(i), {axis: 1 - index})

    def v_add(i):
        v_side(i).wait()
        other = vec_recv[i]
        vec_own[...] = vec_own[...] + (other * norms if i == 0 else other)

    v_side(0).start()
    dat_copy(t).wait_send()
    dat_ref[t] = (dmid_ref[...] + d_norm).astype(BF)
    gh_s, gh_r, gh_l = (pool.take() for _ in range(3))
    gh_copy = remote(dat_ref.at[t], gh_all.at[t], gh_s(), gh_r(), {"tensor": 1 - t})
    gh_own = pltpu.make_async_copy(dat_ref.at[t], gh_all.at[t], gh_l())
    gh_copy.start()
    gh_own.start()
    line_tick(4)
    v_add(0)
    v_side(1).start()
    far_s, far_r = pool.take(), pool.take()
    far_copy = remote(
        g_mlp.at[:, 1 - x],
        g_far.at[pl.ds(0, g_mlp.shape[0])],
        far_s(),
        far_r(),
        {"x": 1 - x},
    )
    far_copy.start()
    col_kv.after_side()
    for k in runs[0]:
        col_wo.step(k)
    if nl:
        for tick in range(5, nl + 3):
            line_tick(tick)
    for k in runs[0]:
        col_kv.step(k)
    v_add(1)
    v_side(2).start()
    y_sum = sq_y.result()
    sq_y.drain()
    total = mid_ref[...] + y_sum
    cut = width // 2
    o_s, o_r, o_l = pool.take(2), pool.take(2), pool.take(2)
    sends, locals_ = [], []
    for i in range(2):
        y_own[i] = total[:, i * cut : (i + 1) * cut].astype(BF)
        dst = out_all.at[t, :, pl.ds(i * cut, cut)]
        sends.append(remote(y_own.at[i], dst, o_s(i), o_r(i), {"tensor": 1 - t}))
        locals_.append(pltpu.make_async_copy(y_own.at[i], dst, o_l(i)))
    for copy in sends + locals_:
        copy.start()
    for k in runs[1]:
        col_wo.step(k)
    col_q.after_side()
    if nl:
        lf_s, lf_r, lf_l = (pool.take() for _ in range(3))
        rows = g_far.shape[1]

        def left_rows(col):
            return left_acc.at[:, z, pl.ds(pl.multiple_of(col * rows, rows), rows)]

        left_far = remote(
            left_rows(1 - x),
            g_far.at[pl.ds(g_mlp.shape[0], nl)],
            lf_s(),
            lf_r(),
            {"x": 1 - x},
        )
        left_own = pltpu.make_async_copy(left_rows(x), left_out, lf_l())
        left_far.start()
        left_own.start()
    for k in runs[2]:
        col_wo.step(k)
    v_add(2)

    def v_copy(to):
        return remote(vec_own, vec_z.at[z], vz_s(to), vz_r(z), {"z": to})

    for to in range(zs):

        @pl.when(to != z)
        def _():
            v_copy(to).start()

    for k in runs[1]:
        col_kv.step(k)
    for run in runs:
        for k in run:
            col_q.step(k)
    for k in runs[2]:
        col_kv.step(k)
    total = jnp.zeros(vec_ref.shape, F32)
    for frm in range(zs):

        @pl.when(frm != z)
        def _():
            remote(vec_own, vec_z.at[frm], vz_s(frm), vz_r(frm), {"z": frm}).wait_recv()

        @pl.when(frm == z)
        def _():
            vec_z[frm] = vec_own[...]

        total = total + vec_z[frm]
    g_vec[...] = total

    for to in range(zs):

        @pl.when(to != z)
        def _():
            v_copy(to).wait_send()

    def dkv_drain(s, carry):
        @pl.when((s < z) | ((s == z) & (x == 1)))
        def _():
            side(s, 0).wait_send()

        @pl.when((s > z) | ((s == z) & (x == 0)))
        def _():
            side(s, 1).wait_send()

        @pl.when(s < z)
        def _():
            chain(s, 0).wait_send()

        @pl.when(s > z)
        def _():
            chain(s, 1).wait_send()

        return carry

    lax.fori_loop(0, zs, dkv_drain, 0)
    for item in (col_wo, col_q, col_kv):
        item.drain()
    dh_copy.wait_send()
    far_copy.wait()
    gh_own.wait()
    gh_copy.wait()
    for copy in sends + locals_:
        copy.wait()
    if nl:
        for item in lines:
            item.drain()
        left_far.wait()
        left_own.wait()


def backward_call(zs, heads, left, big, small):
    mid, vec = small[1:3]
    wqkv = small[10]
    half, width = mid.shape
    tok = 2 * half
    _, rows, qkv_cols = wqkv.shape
    q_cols = heads * HEAD_SIZE
    n2, _, _, three = big[1].shape
    nl = left[0].shape[0] if left else 0
    shape = jax.ShapeDtypeStruct
    any_spec = pl.BlockSpec(memory_space=pl.ANY)
    vm = pltpu.VMEM
    cut = width // 2

    def collect(cols):
        return [
            vm((2, zs, rows, cols), BF),
            vm((2, zs, rows, cols), BF),
            vm((2, zs, rows, cols), BF),
            vm((zs, rows, cols), BF),
            vm((zs + 1, rows, cols), BF),
        ]

    square = [vm((4, half, cut), BF), vm((4, half, cut), BF), vm((2, half, cut), BF)]
    lines = [vm(left[0].shape, BF), vm((nl, zs + 1) + left[0].shape[2:], BF)] if nl else []
    return pl.pallas_call(
        functools.partial(backward_kernel, zs, heads, nl, HEAD_SIZE ** (-0.5)),
        out_shape=[
            shape((2, half, width), BF),
            shape((2, half, width), BF),
            shape((rows, q_cols), BF),
            shape((rows, 2 * HEAD_SIZE), BF),
            shape((rows, q_cols), BF),
            shape(vec.shape, F32),
            shape((n2 + nl, rows, three), BF),
        ]
        + ([shape((nl, rows, three), BF)] if nl else []),
        in_specs=[any_spec] * (2 + len(left)) + [VMEM] * len(small),
        out_specs=[any_spec] * 5 + [VMEM, any_spec] + [any_spec] * len(left),
        scratch_shapes=square
        + [
            vm((half, width), F32),
            vm((2, half, width), BF),
            vm((width, tok), BF),
            vm((2, heads * half, HEAD_SIZE), BF),
            vm((2, heads * half, HEAD_SIZE), BF),
            vm((2, HEAD_SIZE, heads * half), BF),
            vm((2, HEAD_SIZE, heads * half), BF),
            vm((2, 1, heads * half), F32),
            vm((2 * zs + 1, half, 2 * HEAD_SIZE), BF),
            vm((zs + 1, half, 2 * HEAD_SIZE), BF),
            vm((zs + 1, half, 2 * HEAD_SIZE), BF),
            vm((2, HEAD_SIZE, heads * half), F32),
            vm((tok, qkv_cols), BF),
            vm((half, width), BF),
            vm((half, width), BF),
        ]
        + collect(q_cols)
        + collect(2 * HEAD_SIZE)
        + collect(q_cols)
        + [
            vm(vec.shape, F32),
            vm((3,) + vec.shape, F32),
            vm((zs,) + vec.shape, F32),
            pltpu.SemaphoreType.DMA(((22 + 4 * nl) * zs + 90,)),
        ]
        + lines,
        compiler_params=pltpu.CompilerParams(
            collective_id=2, has_side_effects=True, vmem_limit_bytes=63 * 2**20
        ),
        cost_estimate=pl.CostEstimate(
            flops=4 * tok * width * (qkv_cols + q_cols) + 2**32,
            bytes_accessed=32 * 2**20,
            transcendentals=0,
        ),
    )(*big, *left, *small)


def remote(src, dst, send, recv, to):
    return pltpu.make_async_remote_copy(
        src_ref=src,
        dst_ref=dst,
        send_sem=send,
        recv_sem=recv,
        device_id=to,
        device_id_type=pl.DeviceIdType.MESH,
    )


def greet(z, zs):
    barrier = pltpu.get_barrier_semaphore()
    for axis in ("batch", "x", "tensor"):
        other = {axis: 1 - lax.axis_index(axis)}
        pl.semaphore_signal(barrier, inc=1, device_id=other, device_id_type=pl.DeviceIdType.MESH)

    @pl.when(z > 0)
    def _():
        pl.semaphore_signal(
            barrier, inc=1, device_id={"z": z - 1}, device_id_type=pl.DeviceIdType.MESH
        )

    @pl.when(z < zs - 1)
    def _():
        pl.semaphore_signal(
            barrier, inc=1, device_id={"z": z + 1}, device_id_type=pl.DeviceIdType.MESH
        )

    pl.semaphore_wait(barrier, 5 - (z == 0).astype(jnp.int32) - (z == zs - 1).astype(jnp.int32))


def in_range(c, count):
    return (c >= 0) & (c < count)


class Exchange:
    def __init__(self, mats, full, first, zs, skip, sems):
        self.mats, self.full, self.first = mats, full, first
        self.x = lax.axis_index("x")
        home = (lax.axis_index("batch") * zs + lax.axis_index("z")) * 2 + self.x
        self.rows, self.cols = mats[0].shape[0], full.shape[2] // 3
        self.at = pl.ds(pl.multiple_of(home * self.rows, self.rows), self.rows)
        self.shift = mats[0].shape[1] // 2 - skip // 2
        self.send, self.recv, self.loc = sems

    def pieces(self, c):
        for w, mat in enumerate(self.mats):
            dst = self.full.at[c, self.at, pl.ds(w * self.cols, self.cols)]
            yield mat, dst

    def source(self, mat, c, x):
        first = pl.multiple_of(x * self.shift + (self.first + c) * self.cols, 128)
        return mat.at[:, pl.ds(first, self.cols)]

    def ship(self, c, i):
        for mat, dst in self.pieces(c):
            src = self.source(mat, c, 1 - self.x)
            remote(src, dst, self.send(i), self.recv(i), {"x": 1 - self.x}).start()

    def keep(self, c, i):
        for mat, dst in self.pieces(c):
            pltpu.make_async_copy(self.source(mat, c, self.x), dst, self.loc(i)).start()

    def fetch(self, c, other, buf, sem):
        x = 1 - self.x if other else self.x
        for w, mat in enumerate(self.mats):
            dst = buf.at[pl.ds(c * self.rows, self.rows), pl.ds(w * self.cols, self.cols)]
            pltpu.make_async_copy(self.source(mat, c, x), dst, sem).start()

    def both(self, c, i):
        spot = self.full.at[c, self.at]
        return remote(spot, spot, self.send(i), self.recv(i), {"x": 1 - self.x})

    def arrived(self, c, i):
        self.both(c, i).wait_recv()
        spot = self.full.at[c, self.at]
        pltpu.make_async_copy(spot, spot, self.loc(i)).wait()

    def sent(self, c, i):
        self.both(c, i).wait_send()


class Gather:
    def __init__(self, zs, mine, full, sems):
        self.zs, self.mine, self.full = zs, mine, full
        self.loc, self.up, self.dn, self.zr, self.ss, self.sr = sems
        self.b, self.z = lax.axis_index("batch"), lax.axis_index("z")
        self.size = full.shape[1] // (2 * zs)

    def at(self, c, b, z):
        rows = pl.ds(pl.multiple_of((b * self.zs + z) * self.size, self.size), self.size)
        return self.full.at[:, rows] if c is None else self.full.at[c, rows]

    def sems(self, c, s):
        i = 0 if c is None else c
        return (ref.at[i, s] for ref in (self.up, self.dn, self.zr, self.ss, self.sr))

    def up_copy(self, c, s, src=None):
        dst = self.at(c, self.b, s)
        up, _, zr, _, _ = self.sems(c, s)
        return remote(dst if src is None else src, dst, up, zr, {"z": self.z + 1})

    def dn_copy(self, c, s, src=None):
        dst = self.at(c, self.b, s)
        _, dn, zr, _, _ = self.sems(c, s)
        return remote(dst if src is None else src, dst, dn, zr, {"z": self.z - 1})

    def sib_copy(self, c, s, src=None):
        dst = self.at(c, self.b, s)
        _, _, _, ss, sr = self.sems(c, s)
        return remote(dst if src is None else src, dst, ss, sr, {"batch": 1 - self.b})

    def local(self, c):
        return pltpu.make_async_copy(self.mine.at[c], self.at(c, self.b, self.z), self.loc.at[c])

    def start(self, c):
        src = None if self.mine is None else self.mine.at[c]

        @pl.when(self.z < self.zs - 1)
        def _():
            self.up_copy(c, self.z, src).start()

        @pl.when(self.z > 0)
        def _():
            self.dn_copy(c, self.z, src).start()

        self.sib_copy(c, self.z, src).start()
        if self.mine is not None:
            self.local(c).start()

    def hop(self, c, k):
        low, high = self.z - k, self.z + k

        @pl.when(low >= 0)
        def _():
            self.dn_copy(c, low).wait_recv()

            @pl.when(self.z < self.zs - 1)
            def _():
                self.up_copy(c, low).start()

            self.sib_copy(c, low).start()

        @pl.when(high < self.zs)
        def _():
            self.dn_copy(c, high).wait_recv()

            @pl.when(self.z > 0)
            def _():
                self.dn_copy(c, high).start()

            self.sib_copy(c, high).start()

    def finish(self, c):
        if self.mine is not None:
            self.local(c).wait()
        for s in range(self.zs):
            dst = self.at(c, 1 - self.b, s)
            _, _, _, ss, sr = self.sems(c, s)
            remote(dst, dst, ss, sr, {"batch": 1 - self.b}).wait_recv()

    def drain(self, c):
        for s in range(self.zs):

            @pl.when((s <= self.z) & (self.z < self.zs - 1))
            def _():
                self.up_copy(c, s).wait_send()

            @pl.when((s >= self.z) & (self.z > 0))
            def _():
                self.dn_copy(c, s).wait_send()

            self.sib_copy(c, s).wait_send()


class Reduce:
    def __init__(self, zs, ends, ring, to_sib, r_sib, r_dn, r_up, tmp, out, left, sems):
        self.zs, self.ring, self.to_sib, self.out = zs, ring, to_sib, out
        self.ends, self.left = ends, left
        self.r_sib, self.r_dn, self.r_up = r_sib, r_dn, r_up
        self.tmp_s, self.tmp_d, self.tmp_u = tmp
        self.s_s, self.s_r, self.d_s, self.d_r, self.u_s, self.u_r, self.load, self.o_s, self.l_s = sems
        self.b, self.z = lax.axis_index("batch"), lax.axis_index("z")
        self.slots = ring.shape[0]
        self.size = ring.shape[1] // zs

    def rows(self, h):
        return pl.ds(pl.multiple_of(h * self.size, self.size), self.size)

    def sib(self, c):
        return remote(
            self.to_sib, self.r_sib.at[c], self.s_s.at[c], self.s_r.at[c], {"batch": 1 - self.b}
        )

    def dn(self, c, h):
        src = self.ring.at[lax.rem(c, self.slots), self.rows(h)]
        dst = self.r_dn.at[c, self.rows(h)]
        return remote(src, dst, self.d_s.at[c, h], self.d_r.at[c, h], {"z": self.z - 1})

    def up(self, c, h):
        src = self.ring.at[lax.rem(c, self.slots), self.rows(h)]
        dst = self.r_up.at[c, self.rows(h)]
        return remote(src, dst, self.u_s.at[c, h], self.u_r.at[c, h], {"z": self.z + 1})

    def load_sib(self, c):
        return pltpu.make_async_copy(self.r_sib.at[c], self.tmp_s, self.load.at[0])

    def load_dn(self, c, h):
        rows = self.rows(h)
        return pltpu.make_async_copy(self.r_dn.at[c, rows], self.tmp_d.at[rows], self.load.at[1 + h])

    def load_up(self, c, h):
        rows = self.rows(h)
        return pltpu.make_async_copy(
            self.r_up.at[c, rows], self.tmp_u.at[rows], self.load.at[1 + self.zs + h]
        )

    def arrive(self, c_sib, c_dn, c_up, count):
        @pl.when(in_range(c_sib, count))
        def _():
            self.sib(c_sib).wait_recv()
            self.load_sib(c_sib).start()

        for h in range(self.zs):

            @pl.when(in_range(c_dn, self.ends) & (self.z < self.zs - 1) & (h <= self.z))
            def _():
                self.dn(c_dn, h).wait_recv()
                self.load_dn(c_dn, h).start()

            @pl.when(in_range(c_up, self.ends) & (self.z > 0) & (h >= self.z))
            def _():
                self.up(c_up, h).wait_recv()
                self.load_up(c_up, h).start()

    def add(self, slot, rows, tmp):
        total = self.ring[slot, rows].astype(F32) + tmp[rows].astype(F32)
        self.ring[slot, rows] = total.astype(BF)

    def pass_on(self, c_sib, c_dn, c_up, count):
        @pl.when(in_range(c_sib, count))
        def _():
            self.load_sib(c_sib).wait()
            slot = lax.rem(c_sib, self.slots)
            for h in range(self.zs):
                self.add(slot, pl.ds(h * self.size, self.size), self.tmp_s)
            for h in range(self.zs - 1):

                @pl.when((self.z == self.zs - 1) & (c_sib < self.ends))
                def _():
                    self.dn(c_sib, h).start()

            for h in range(1, self.zs):

                @pl.when((self.z == 0) & (c_sib < self.ends))
                def _():
                    self.up(c_sib, h).start()

            if self.left is not None:

                @pl.when(c_sib >= self.ends)
                def _():
                    self.leave(c_sib).start()

        for h in range(self.zs):

            @pl.when(in_range(c_dn, self.ends) & (self.z < self.zs - 1) & (h <= self.z))
            def _():
                self.load_dn(c_dn, h).wait()
                self.add(lax.rem(c_dn, self.slots), pl.ds(h * self.size, self.size), self.tmp_d)

                @pl.when(h < self.z)
                def _():
                    self.dn(c_dn, h).start()

            @pl.when(in_range(c_up, self.ends) & (self.z > 0) & (h >= self.z))
            def _():
                self.load_up(c_up, h).wait()
                self.add(lax.rem(c_up, self.slots), pl.ds(h * self.size, self.size), self.tmp_u)

                @pl.when(h > self.z)
                def _():
                    self.up(c_up, h).start()

    def leave(self, c):
        src = self.ring.at[lax.rem(c, self.slots)]
        return pltpu.make_async_copy(src, self.left.at[c - self.ends], self.l_s.at[c - self.ends])

    def result(self, c):
        src = self.ring.at[lax.rem(c, self.slots), self.rows(self.z)]
        return pltpu.make_async_copy(src, self.out.at[c], self.o_s.at[0])

    def finish(self, c):
        for h in range(self.zs):

            @pl.when(h < self.z)
            def _():
                self.dn(c, h).wait_send()

            @pl.when(h > self.z)
            def _():
                self.up(c, h).wait_send()

        self.result(c).start()


def mlp_kernel(zs, nc, n1, n2, fc, skip, *refs):
    refs = list(refs)

    def take(count):
        out = refs[:count]
        del refs[:count]
        return out

    if n1:
        mats, full_one = take(3), take(1)[0]
        mine = None
    else:
        (mine,) = take(1)
    h2, dy, dh2_out, y_out, g_out, full, r_sib, r_dn, r_up = take(9)
    left = take(1)[0] if n2 < nc else None
    acc_y, acc_d, h2t, dyt, wbuf, hid_s, dgu_s, ring, to_sib, tmp_s, tmp_d, tmp_u = take(12)
    d_src, d_own, d_one, d_two = take(4)
    w_sem, x_s, x_r, k_s, sq_sem, st_sem = take(6)
    sems = refs
    b, z, x = lax.axis_index("batch"), lax.axis_index("z"), lax.axis_index("x")
    greet(z, zs)
    rest = nc - n1
    lag = 0 if n1 else zs
    ahead = n1 - zs + 1 if n1 else 0
    gather = Gather(zs, mine, full, sems[:6])
    reduce = Reduce(
        zs, n2, ring, to_sib, r_sib, r_dn, r_up, (tmp_s, tmp_d, tmp_u), g_out, left, sems[6:]
    )
    slots = ring.shape[0]
    half = ring.shape[1]
    toks = h2.shape[0]
    block = toks // 2
    part = toks // 4
    square = Square(d_src, d_own, d_one, d_two, Pool(sq_sem))

    if n1:
        trade = Exchange(
            mats, full, n1, zs, skip, [lambda i, r=r: r.at[i] for r in (x_s, x_r, k_s)]
        )
        stage = [ring.at[ring.shape[0] - 1], ring.at[ring.shape[0] - 2]]
        for c in range(rest):
            for side in range(2):
                trade.fetch(c, side, stage[side], st_sem.at[2 * c + side])

        def slices(c):
            rows = pl.ds(c * trade.rows, trade.rows)
            dst = full.at[c, trade.at]
            return (
                pltpu.make_async_copy(stage[0].at[rows], dst, k_s.at[c]),
                remote(stage[1].at[rows], dst, x_s.at[c], x_r.at[c], {"x": 1 - x}),
            )

        for c in range(rest):
            for side in range(2):
                rows = stage[side].at[pl.ds(c * trade.rows, trade.rows)]
                pltpu.make_async_copy(rows, rows, st_sem.at[2 * c + side]).wait()
                slices(c)[side].start()

    def weights(c):
        return pltpu.make_async_copy(full.at[c - n1], wbuf, w_sem.at[0])

    def weights_one(c):
        return pltpu.make_async_copy(full_one.at[c], wbuf, w_sem.at[0])

    if n1:
        weights_one(0).start()
    acc_y[...] = jnp.zeros_like(acc_y)
    acc_d[...] = jnp.zeros_like(acc_d)
    for m in range(4):
        at = slice(m * block // 2, (m + 1) * block // 2)
        h2t[:, at] = h2[at].T
        dyt[:, at] = dy[at].T

    def compute(c):
        col = lax.broadcasted_iota(jnp.int32, (1, fc), 1) + c * fc
        live = jnp.where((col >= skip) | (x == 0), 1.0, 0.0).astype(F32)
        for m in range(2):
            at = slice(m * block, (m + 1) * block)
            gate_up = dot(h2[at], wbuf[:, : 2 * fc])
            d_hidden = dot(dy[at], wbuf[:, 2 * fc :]) * live
            gate, up = gate_up[:, :fc], gate_up[:, fc:]
            sig = 1.0 / (1.0 + jnp.exp(-gate))
            silu = gate * sig
            hid_s[at] = (silu * up * live).astype(BF)
            dgu_s[at, :fc] = (d_hidden * up * sig * (1.0 + gate * (1.0 - sig))).astype(BF)
            dgu_s[at, fc:] = (d_hidden * silu).astype(BF)
            acc_y[at] += dot_nt(hid_s[at], wbuf[:, 2 * fc :])
            acc_d[at] += dot_nt(dgu_s[at], wbuf[:, : 2 * fc])

        @pl.when(c == nc - 1)
        def _():
            for i in range(4):
                d_src[i] = acc_d[i * part : (i + 1) * part].astype(BF)
            square.start()

        @pl.when(c > 0)
        def _():
            reduce.sib(c - 1).wait_send()

        theirs = pl.ds(pl.multiple_of((1 - b) * half, half), half)
        own = pl.ds(pl.multiple_of(b * half, half), half)
        to_sib[:, : 2 * fc] = dot(h2t[theirs], dgu_s[...]).astype(BF)
        to_sib[:, 2 * fc :] = dot(dyt[theirs], hid_s[...]).astype(BF)
        reduce.sib(c).start()
        slot = lax.rem(c, slots)
        ring[slot, :, : 2 * fc] = dot(h2t[own], dgu_s[...]).astype(BF)
        ring[slot, :, 2 * fc :] = dot(dyt[own], hid_s[...]).astype(BF)

    def begin(i):
        @pl.when(in_range(i, rest))
        def _():
            if n1:
                trade.arrived(i, i)
            gather.start(i)

    def tick(t, carry):
        if n1:
            @pl.when(t == slots - 3)
            def _():
                for c in range(rest):
                    trade.sent(c, c)

        g = t + ahead
        begin(g)
        for k in range(1, zs):

            @pl.when(in_range(g - k, rest))
            def _():
                gather.hop(g - k, k)

        @pl.when(in_range(g - zs, rest))
        def _():
            gather.finish(g - zs)

        c = t - lag
        c_sib = c - 1
        c_dn = c_sib - 2 * (zs - 1 - z)
        c_up = c_sib - 2 * z
        c_end = c_sib - 2 * zs + 1

        @pl.when(in_range(c - n1, rest))
        def _():
            weights(c).start()

        if n1:

            @pl.when((c > 0) & (c < n1))
            def _():
                weights_one(c).start()

        reduce.arrive(c_sib, c_dn, c_up, nc)
        reduce.pass_on(c_sib, c_dn, c_up, nc)

        @pl.when(in_range(c_end, n2))
        def _():
            reduce.finish(c_end)
            reduce.result(c_end).wait()

        @pl.when(in_range(c, nc))
        def _():
            weights(n1).wait()
            compute(c)

        return carry

    for i in range(ahead):
        begin(i)
    lax.fori_loop(0, nc + lag, tick, 0)

    lax.fori_loop(nc + lag, nc + lag + 1, tick, 0)
    square.turn()
    for copy in square.first():
        copy.wait_send()
    for i in range(4):
        d_src[i] = acc_y[i * part : (i + 1) * part].astype(BF)
    y_copy = pltpu.make_async_copy(d_src, y_out, w_sem.at[0])
    y_copy.start()
    lax.fori_loop(nc + lag + 1, max(nc + 1, n2 + 2 * zs) + lag, tick, 0)
    dh2_out[...] = square.result()
    for copy in square.second():
        copy.wait_send()
    y_copy.wait()
    reduce.sib(nc - 1).wait_send()
    for c in range(n2, nc):
        reduce.leave(c).wait()

    def drain(c, carry):
        gather.drain(c)
        return carry

    lax.fori_loop(0, rest, drain, 0)


def mlp_call(zs, nc, n1, n2, fc, skip, weights, h2, dy):
    toks, width = h2.shape
    half = width // 2
    slots = min(2 * zs, nc)
    rest = nc - n1
    dma = pltpu.SemaphoreType.DMA
    vm = pltpu.VMEM
    shape = jax.ShapeDtypeStruct
    any_spec = pl.BlockSpec(memory_space=pl.ANY)
    out = [
        shape((toks // 4, width), F32),
        shape((4, toks // 4, width), BF),
        shape((n2, half // zs, 3 * fc), BF),
        shape((rest, width, 3 * fc), BF),
        shape((nc, half, 3 * fc), BF),
        shape((n2, half, 3 * fc), BF),
        shape((n2, half, 3 * fc), BF),
    ]
    if n2 < nc:
        out.append(shape((nc - n2, half, 3 * fc), BF))
    result = pl.pallas_call(
        functools.partial(mlp_kernel, zs, nc, n1, n2, fc, skip),
        out_shape=out,
        in_specs=[any_spec] * len(weights) + [VMEM, VMEM],
        out_specs=[VMEM] + [any_spec] * (len(out) - 1),
        scratch_shapes=[
            vm((toks, width), F32),
            vm((toks, width), F32),
            vm((width, toks), BF),
            vm((width, toks), BF),
            vm((width, 3 * fc), BF),
            vm((toks, fc), BF),
            vm((toks, 2 * fc), BF),
            vm((slots, half, 3 * fc), BF),
            vm((half, 3 * fc), BF),
            vm((half, 3 * fc), BF),
            vm((half, 3 * fc), BF),
            vm((half, 3 * fc), BF),
            vm((4, toks // 4, width), BF),
            vm((4, toks // 4, half), BF),
            vm((4, toks // 4, half), BF),
            vm((2, toks // 4, half), BF),
            dma((1,)),
        ]
        + [dma((rest,))] * 3
        + [dma((13,)), dma((2 * rest,)), dma((rest,))]
        + [dma((rest, zs))] * 5
        + [dma((nc,))] * 2
        + [dma((nc, zs))] * 4
        + [dma((1 + 2 * zs,)), dma((1,)), dma((nc,))],
        compiler_params=pltpu.CompilerParams(
            collective_id=0, has_side_effects=True, vmem_limit_bytes=62 * 2**20
        ),
        cost_estimate=pl.CostEstimate(
            flops=18 * toks * width * fc * nc, bytes_accessed=80 * 2**20, transcendentals=0
        ),
    )(*weights, h2, dy)
    return list(result[:3]) + list(result[7:])


def final_kernel(skip, *refs):
    refs = list(refs)
    inputs = refs[:8]
    d_hidden, g_query, g_key, g_value, g_out, g_gate, g_up, g_down, output = refs[8:17]
    bufs, sem = refs[17:24] + [output], refs[24]
    x = lax.axis_index("x")
    copies = [
        pltpu.make_async_copy(src, dst, sem.at[i])
        for i, (src, dst) in enumerate(zip(inputs, bufs))
    ]
    for copy in copies:
        copy.start()
    near, left, far, gh, s_q, s_kv, s_wo, _ = bufs
    n2, nl = near.shape[0], left.shape[0]
    half = gh.shape[1]
    fc = far.shape[2] // 3
    split = (n2 + nl) * fc
    for i in (0, 2, 1):
        copies[i].wait()
    for c in range(n2 + nl):
        own = (near[c, x] if c < n2 else left[c - n2]).astype(F32)
        other = far[c].astype(F32)
        low = jnp.where(x == 0, own, other)
        high = jnp.where(x == 0, other, own)
        for w, out in enumerate((g_gate, g_up, g_down)):
            b = high[:, w * fc : (w + 1) * fc]
            first = split - skip + c * fc
            if c == 0:
                b = b[:, skip:]
                first = split
            out[:, c * fc : (c + 1) * fc] = low[:, w * fc : (w + 1) * fc]
            out[:, first : first + b.shape[1]] = b
    for i in (3, 4, 5, 6):
        copies[i].wait()
    for i in range(2):
        d_hidden[i * half : (i + 1) * half] = gh[i].astype(F32)
    g_query[...] = s_q[...].astype(F32)
    g_key[...] = s_kv[:, :HEAD_SIZE].astype(F32)
    g_value[...] = s_kv[:, HEAD_SIZE:].astype(F32)
    g_out[...] = s_wo[...].astype(F32)
    copies[7].wait()


def final_call(skip, ff, inputs):
    rows, three = inputs[2].shape[1:]
    _, half, width = inputs[3].shape
    q_cols = inputs[4].shape[1]
    shape = jax.ShapeDtypeStruct
    any_spec = pl.BlockSpec(memory_space=pl.ANY)
    out = [
        shape((2 * half, width), F32),
        shape((rows, q_cols), F32),
        shape((rows, HEAD_SIZE), F32),
        shape((rows, HEAD_SIZE), F32),
        shape((rows, q_cols), F32),
        shape((rows, ff), F32),
        shape((rows, ff), F32),
        shape((rows, ff), F32),
        shape(inputs[7].shape, BF),
    ]
    return pl.pallas_call(
        functools.partial(final_kernel, skip),
        out_shape=out,
        in_specs=[any_spec] * len(inputs),
        out_specs=[VMEM] * 9,
        scratch_shapes=[pltpu.VMEM(v.shape, BF) for v in inputs[:7]]
        + [pltpu.SemaphoreType.DMA((8,))],
        compiler_params=pltpu.CompilerParams(vmem_limit_bytes=60 * 2**20),
    )(*inputs)


def on_device(
    hidden,
    lengths,
    norm_attn,
    w_query,
    key_weight_matrix,
    value_weight_matrix,
    b_query,
    key_bias_rows,
    value_bias_rows,
    w_out,
    norm_mlp,
    w_gate,
    w_up,
    w_down,
    cotangent,
):
    homes = lax.axis_size("batch") * lax.axis_size("z") * lax.axis_size("x")
    shards = lax.axis_size("z") * lax.axis_size("x")
    z_i, x_i = lax.axis_index("z"), lax.axis_index("x")
    me = z_i * lax.axis_size("x") + x_i
    tok = hidden.shape[1]
    width = hidden.shape[2]
    half = tok // 2
    doc_lengths = lengths[0]
    heads = b_query.shape[0]
    heads_all = heads + 2
    q_cols = heads * HEAD_SIZE
    rows = norm_attn.shape[0]
    ff = w_gate.shape[1]
    ffh = -(-ff // 512) * 256
    fc = FC
    nc = ffh // fc

    home = (lax.axis_index("batch") * lax.axis_size("z") + z_i) * 2 + x_i
    per_home = HEAD_SIZE // homes

    def spot(value, count):
        out = jnp.zeros((value.shape[0], homes, count), BF)
        return lax.dynamic_update_slice(out, value[:, None, :], (0, home, 0)).reshape(-1)

    biases = jnp.concatenate([b_query, key_bias_rows, value_bias_rows], axis=0)
    small = jnp.concatenate(
        [spot(biases, per_home), spot(norm_attn[None], rows), spot(norm_mlp[None], rows)]
    ).reshape(16, -1)
    w_qkv = jnp.concatenate([w_query, key_weight_matrix, value_weight_matrix], axis=1)

    zs = lax.axis_size("z")
    n1, n2 = (zs, nc - zs + 1) if rows % 16 == 0 and 2 * zs < nc else (0, nc)
    three = (w_gate, w_up, w_down.T)
    skip = 2 * ffh - ff

    stored = me * tok + jnp.arange(tok, dtype=jnp.int32)
    q_rows = row_positions(stored, shards, half)
    doc_start = doc_starts_of(q_rows, doc_lengths)
    cosine_table, sine_table = rotary(q_rows - doc_start, HEAD_SIZE)
    cos2 = jnp.concatenate([cosine_table, cosine_table], axis=1)
    sin2 = jnp.concatenate([-sine_table, sine_table], axis=1)
    start_row = doc_start[None, :]

    x_in = hidden[0]
    (
        h_first,
        q_mat,
        out_low,
        lse,
        mid,
        vec,
        wqkv,
        wo_t,
        kv_all,
        h2,
        dy,
        *full_one,
    ) = forward_call(
        zs,
        heads,
        n1,
        skip,
        fc,
        x_in,
        w_qkv,
        w_out.T,
        small,
        cos2,
        sin2,
        start_row,
        cotangent[0].reshape(2, half, width),
        three if n1 else (),
    )
    h2 = h2.reshape(4 * half, width)
    dy = dy.reshape(4 * half, width)
    if n1:
        mlp_w = (*three, *full_one)
    else:

        def stacked(x_at):
            halves = [
                lax.dynamic_slice_in_dim(mat, x_at * (ff - ffh), ffh, axis=1).reshape(rows, nc, fc)
                for mat in three
            ]
            return jnp.transpose(jnp.concatenate(halves, axis=2), (1, 0, 2))

        keep = stacked(x_i)
        other = lax.ppermute(stacked(1 - x_i), "x", [(0, 1), (1, 0)])
        low = jnp.where(x_i == 0, keep, other)
        high = jnp.where(x_i == 0, other, keep)
        mlp_w = (jnp.concatenate([low, high], axis=1),)
    dh2, y_sum, mlp_g, *left = mlp_call(zs, nc, n1, n2, fc, skip, mlp_w, h2, dy)
    mlp_g = mlp_g.reshape(n2, 2, rows, 3 * fc)
    left = [v.reshape(nc - n2, zs, 2 * rows, 3 * fc) for v in left]

    output, d_hidden, s_q, s_kv, s_wo, g_vec, other, *left_own = backward_call(
        zs,
        heads,
        left,
        (y_sum, mlp_g),
        (
            dh2,
            mid,
            vec,
            x_in,
            cotangent[0],
            h_first,
            q_mat,
            out_low,
            lse[:, None],
            kv_all,
            wqkv,
            wo_t,
            cos2,
            sin2,
            start_row.reshape(2, 1, half),
        ),
    )
    g_vec = g_vec.reshape(-1)
    g_bias = lax.dynamic_slice_in_dim(
        g_vec[: heads_all * HEAD_SIZE].reshape(heads_all, HEAD_SIZE), home * per_home, per_home, 1
    )
    g_norms = g_vec[heads_all * HEAD_SIZE :].reshape(2, width)
    g_norms = lax.dynamic_slice_in_dim(g_norms, home * rows, rows, 1)

    if n1:
        grads = final_call(skip, ff, (mlp_g, *left_own, other, d_hidden, s_q, s_kv, s_wo, output))
    else:
        keep = lax.dynamic_index_in_dim(mlp_g, x_i, 1, False)
        low = jnp.where(x_i == 0, keep, other)
        high = jnp.where(x_i == 0, other, keep)

        def whole(k):
            def cols(value):
                piece = value[:, :, k * fc : (k + 1) * fc]
                return jnp.transpose(piece, (1, 0, 2)).reshape(rows, ffh)

            return jnp.concatenate([cols(low), cols(high)[:, skip:]], axis=1).astype(F32)

        grads = (
            d_hidden.astype(F32).reshape(tok, width),
            s_q.astype(F32),
            s_kv[:, :HEAD_SIZE].astype(F32),
            s_kv[:, HEAD_SIZE:].astype(F32),
            s_wo.astype(F32),
            whole(0),
            whole(1),
            whole(2),
            output,
        )
    d_hidden, g_query, g_key, g_value, g_out, g_gate, g_up, g_down, output = grads
    return (
        output.reshape(1, tok, width),
        d_hidden[None],
        g_norms[0],
        g_query,
        g_key,
        g_value,
        g_bias[:heads],
        g_bias[heads : heads + 1],
        g_bias[heads + 1 :],
        g_out.T,
        g_norms[1],
        g_gate,
        g_up,
        g_down.T,
    )


def solution(mesh):
    seq = mesh.shape["seq"]
    fine = Mesh(
        mesh.devices.reshape(mesh.shape["batch"], seq // 2, 2, mesh.shape["tensor"]),
        ("batch", "z", "x", "tensor"),
    )
    toks = P("batch", ("z", "x"), None)
    home = ("batch", "z", "x")
    down = P(home, "tensor")
    across = P("tensor", home)
    return jax.shard_map(
        on_device,
        mesh=fine,
        in_specs=(
            toks,
            P("batch", None),
            P(home),
            down,
            down,
            down,
            across,
            across,
            across,
            across,
            P(home),
            down,
            down,
            across,
            toks,
        ),
        out_specs=(
            toks,
            toks,
            P(home),
            down,
            down,
            down,
            across,
            across,
            across,
            across,
            P(home),
            down,
            down,
            across,
        ),
        check_vma=False,
    )
```

```python
import functools

import jax
import jax.numpy as jnp
from jax import lax
from jax.experimental import pallas as pl
from jax.experimental.pallas import tpu as pltpu
from jax.sharding import Mesh
from jax.sharding import PartitionSpec as P

HEAD_SIZE = 128
NORM_EPS = 1e-06
ROPE_BASE = 10000.0
MASKED = -1e30
FLOOR = -1e29
FC = 256
BF = jnp.bfloat16
F32 = jnp.float32
VMEM = pl.BlockSpec(memory_space=pltpu.VMEM)


def row_positions(stored, shards, half_rows):
    slot_id = stored // half_rows
    inner = stored % half_rows
    shard_id = slot_id // 2
    row_block = jnp.where(slot_id % 2 == 0, shard_id, 2 * shards - 1 - shard_id)
    return row_block * half_rows + inner


def doc_starts_of(row_pos, doc_lengths):
    doc_ends = jnp.cumsum(doc_lengths)
    doc_starts = doc_ends - doc_lengths
    inside = (row_pos[:, None] >= doc_starts[None, :]) & (row_pos[:, None] < doc_ends[None, :])
    return jnp.sum(jnp.where(inside, doc_starts[None, :], 0), axis=1).astype(jnp.int32)


def rotary(doc_pos, head_dim):
    half_dim = head_dim // 2
    freqs = ROPE_BASE ** (-2.0 * jnp.arange(half_dim, dtype=jnp.float32) / head_dim)
    angles = doc_pos.astype(jnp.float32)[:, None] * freqs[None, :]
    return (jnp.cos(angles), jnp.sin(angles))


def norm_factor(resid):
    return lax.rsqrt(jnp.mean(resid * resid, axis=-1, keepdims=True) + NORM_EPS)


def norm_backward(resid, factor, gain, grad_in):
    weighted = grad_in * gain
    grad_resid = factor * weighted - resid * factor**3 * jnp.mean(
        weighted * resid, axis=-1, keepdims=True
    )
    grad_gain = jnp.sum(grad_in * resid * factor, axis=0, keepdims=True)
    return (grad_resid, grad_gain)


def dot(a, b):
    return jnp.dot(a, b, preferred_element_type=F32)


def dot_nt(a, b):
    return lax.dot_general(a, b, (((1,), (1,)), ((), ())), preferred_element_type=F32)


def block_mask(sub, block, me, shards, half, start_row, heads):
    key_blk = jnp.where(sub == 0, block, 2 * shards - 1 - block)
    query_blk = jnp.where(sub == 0, me, 2 * shards - 1 - me)
    key_pos = key_blk * half + lax.broadcasted_iota(jnp.int32, (half, half), 0)
    query_pos = query_blk * half + lax.broadcasted_iota(jnp.int32, (half, half), 1)
    allowed = (key_pos <= query_pos) & (key_pos >= start_row)
    return jnp.concatenate([jnp.where(allowed, 0.0, MASKED).astype(F32)] * heads, axis=1)


def stack_heads(ref, sub, half, heads):
    return jnp.concatenate(
        [
            ref[sub * half : (sub + 1) * half, h * HEAD_SIZE : (h + 1) * HEAD_SIZE]
            for h in range(heads)
        ],
        axis=0,
    )


class Pool:
    def __init__(self, ref):
        self.ref, self.used = ref, 0

    def take(self, count=1):
        base = self.used
        self.used += count
        assert self.used <= self.ref.shape[0], self.used
        return lambda i=0: self.ref.at[base + i]


def merge_rows(value):
    homes, rows, cols = value.shape
    if rows % 16:
        return value.astype(F32).reshape(homes * rows, cols).astype(BF)
    return value.reshape(homes * rows, cols)


class Spread:
    def __init__(self, zs, src, buf, pool):
        self.zs, self.src, self.buf = zs, src, buf
        self.b, self.z, self.x = (lax.axis_index(a) for a in ("batch", "z", "x"))
        self.up_s, self.dn_s, self.z_r, self.x_s, self.x_r = (pool.take(zs) for _ in range(5))
        self.s_s, self.s_r = pool.take(2 * zs), pool.take(2 * zs)
        self.loc = pool.take()

    def at(self, b, z, x):
        return self.buf.at[(b * self.zs + z) * 2 + x]

    def up(self, s, src=None):
        dst = self.at(self.b, s, self.x)
        src = dst if src is None else src
        return remote(src, dst, self.up_s(s), self.z_r(s), {"z": self.z + 1})

    def dn(self, s, src=None):
        dst = self.at(self.b, s, self.x)
        src = dst if src is None else src
        return remote(src, dst, self.dn_s(s), self.z_r(s), {"z": self.z - 1})

    def side(self, s, src=None):
        dst = self.at(self.b, s, self.x)
        src = dst if src is None else src
        return remote(src, dst, self.x_s(s), self.x_r(s), {"x": 1 - self.x})

    def sib(self, s, far=0, src=None):
        dst = self.at(self.b, s, self.x if far == 0 else 1 - self.x)
        src = dst if src is None else src
        i = far * self.zs + s
        return remote(src, dst, self.s_s(i), self.s_r(i), {"batch": 1 - self.b})

    def local(self):
        return pltpu.make_async_copy(self.src, self.at(self.b, self.z, self.x), self.loc())

    def start(self):
        @pl.when(self.z < self.zs - 1)
        def _():
            self.up(self.z, self.src).start()

        @pl.when(self.z > 0)
        def _():
            self.dn(self.z, self.src).start()

        self.side(self.z, self.src).start()
        self.sib(self.z, 0, self.src).start()
        self.local().start()

    def hop(self, k):
        low, high = self.z - k, self.z + k

        @pl.when(low >= 0)
        def _():
            self.dn(low).wait_recv()

            @pl.when(self.z < self.zs - 1)
            def _():
                self.up(low).start()

            self.side(low).start()
            self.sib(low).start()

        @pl.when(high < self.zs)
        def _():
            self.dn(high).wait_recv()

            @pl.when(self.z > 0)
            def _():
                self.dn(high).start()

            self.side(high).start()
            self.sib(high).start()

    def cross(self):
        for s in range(self.zs):
            dst = self.at(self.b, s, 1 - self.x)
            remote(dst, dst, self.x_s(s), self.x_r(s), {"x": 1 - self.x}).wait_recv()
            self.sib(s, 1).start()

    def finish(self):
        self.local().wait()
        for far in range(2):
            for s in range(self.zs):
                dst = self.at(1 - self.b, s, self.x if far == 0 else 1 - self.x)
                i = far * self.zs + s
                remote(dst, dst, self.s_s(i), self.s_r(i), {"batch": 1 - self.b}).wait_recv()

    def drain(self):
        for s in range(self.zs):

            @pl.when((s <= self.z) & (self.z < self.zs - 1))
            def _():
                self.up(s).wait_send()

            @pl.when((s >= self.z) & (self.z > 0))
            def _():
                self.dn(s).wait_send()

            self.side(s).wait_send()
            self.sib(s, 0).wait_send()
            self.sib(s, 1).wait_send()


def lanes(vec, first, count):
    return jnp.concatenate([vec[r : r + 1, :] for r in range(first, first + count)], axis=1)


def thirds(zs):
    hops = list(range(1, zs))
    per = -(-len(hops) // 3)
    return [hops[i * per : (i + 1) * per] for i in range(3)]


def forward_kernel(
    zs,
    heads,
    n1,
    skip,
    scale,
    x_ref,
    wkv_in,
    wq_in,
    wo_in,
    small_in,
    cos_ref,
    sin_ref,
    start_ref,
    dy_in,
    *refs,
):
    refs = list(refs)
    if n1:
        mats = refs[:3]
        del refs[:3]
    h1_out, q_out, attn_out, lse_out, mid_out, vec_out = refs[:6]
    wkv_all, wq_all, wo_all, kv_all, h2_all, dy_all = refs[6:12]
    del refs[:12]
    if n1:
        full = refs.pop(0)
    small_buf, wkv_buf, wq_buf, wo_buf, kv_buf, q_t, acc_ref, max_ref, sum_ref = refs[:9]
    att_send, att_recv, h2_half, xn_ref, sem_ref = refs[9:14]
    g_sems = refs[14:]
    b, z, x, t = (lax.axis_index(a) for a in ("batch", "z", "x", "tensor"))
    shards = 2 * zs
    me = 2 * z + x
    tok, width = x_ref.shape
    half = tok // 2
    q_cols = heads * HEAD_SIZE
    pool = Pool(sem_ref)
    greet(z, zs)

    small = Spread(zs, small_in, small_buf, pool)
    wkv = Spread(zs, wkv_in, wkv_buf, pool)
    wq = Spread(zs, wq_in, wq_buf, pool)
    wo = Spread(zs, wo_in, wo_buf, pool)
    small.start()
    wkv.start()
    wq.start()

    runs = thirds(zs)
    if n1:
        trade = Exchange(mats, full, 0, zs, skip, [pool.take(n1) for _ in range(3)])
        gather = Gather(zs, None, full, [None] + list(g_sems))
        for c in range(n1):
            trade.keep(c, c)

    def ship(first, last):
        if n1:
            for c in range(first, last):
                trade.ship(c, c)

    def prefetch(tick):
        if n1:
            for c in range(n1):
                hops = [k for k in range(1, zs) if min(k, 3) == tick - c]
                if tick == c:
                    trade.arrived(c, c)
                    gather.start(c)
                for k in hops:
                    gather.hop(c, k)

    quarter = half // 2
    dy_l, dyy_s, dyy_r = (pool.take() for _ in range(3))
    dyx_s, dyx_r = pool.take(3), pool.take(3)
    dy_own = pltpu.make_async_copy(dy_in, dy_all.at[pl.ds(2 * x, 2)], dy_l())
    dy_own.start()

    def dy_side(i):
        rows = pl.ds((i % 3 > 0) * quarter, quarter)
        block = t if i < 2 else 1 - t
        dst = dy_all.at[2 * x + block, rows]
        return remote(dy_in.at[block, rows], dst, dyx_s(i), dyx_r(i), {"x": 1 - x})

    dy_piece = dy_all.at[2 * (1 - x) + t, pl.ds(0, quarter)]
    dy_across = remote(dy_piece, dy_piece, dyy_s(), dyy_r(), {"tensor": 1 - t})

    for m in range(2):
        at = slice(m * half, (m + 1) * half)
        xv = x_ref[at].astype(F32)
        xn_ref[at] = xv * norm_factor(xv)
    for k in range(1, zs):
        small.hop(k)
        wkv.hop(k)
        if k == 1:
            ship(0, 1)
    for k in runs[0]:
        wq.hop(k)
    wo.start()
    prefetch(0)
    small.cross()
    small.finish()
    vec = jnp.sum(small_buf[...].astype(F32), axis=0)
    vec_out[...] = vec
    bias = lanes(vec, 0, 4)
    gain_attn = lanes(vec, 4, 6)
    gain_mlp = lanes(vec, 10, 6)
    for m in range(2):
        at = slice(m * half, (m + 1) * half)
        h1_out[at] = (xn_ref[at] * gain_attn).astype(BF)

    def turned(value, at):
        return value * cos_ref[at] + pltpu.roll(value, HEAD_SIZE // 2, 1) * sin_ref[at]

    wkv.cross()
    ship(1, 2)
    wkv.finish()
    for k in runs[1]:
        wq.hop(k)
    wkv_m = merge_rows(wkv_buf[...])
    for m in range(2):
        at = slice(m * half, (m + 1) * half)
        lin = dot(h1_out[at], wkv_m) + bias[:, q_cols:]
        kv_buf[me + m, :, :HEAD_SIZE] = turned(lin[:, :HEAD_SIZE], at).astype(BF)
        kv_buf[me + m, :, HEAD_SIZE:] = lin[:, HEAD_SIZE:].astype(BF)

    ku_s, kd_s, k0_r, k1_r, x0_s, x1_s, x0_r, x1_r = (pool.take(zs) for _ in range(8))

    def kv_up(s):
        piece = kv_buf.at[2 * s + x]
        return remote(piece, piece, ku_s(s), k0_r(s), {"z": z + 1})

    def kv_dn(s):
        piece = kv_buf.at[2 * s + x + 1]
        return remote(piece, piece, kd_s(s), k1_r(s), {"z": z - 1})

    def kv_side(s, sub, col):
        piece = kv_buf.at[2 * s + col + sub]
        send, recv = (x0_s, x0_r) if sub == 0 else (x1_s, x1_r)
        return remote(piece, piece, send(s), recv(s), {"x": 1 - x})

    def kv_hop(k):
        low, high = z - k, z + k

        @pl.when(low >= 0)
        def _():
            kv_up(low).wait_recv()

            @pl.when(z < zs - 1)
            def _():
                kv_up(low).start()

            kv_side(low, 0, x).start()

        @pl.when(high < zs)
        def _():
            kv_dn(high).wait_recv()

            @pl.when(z > 0)
            def _():
                kv_dn(high).start()

            kv_side(high, 1, x).start()

    @pl.when(z < zs - 1)
    def _():
        kv_up(z).start()

    @pl.when(z > 0)
    def _():
        kv_dn(z).start()

    @pl.when(x == 0)
    def _():
        kv_side(z, 0, x).start()

    @pl.when(x == 1)
    def _():
        kv_side(z, 1, x).start()

    for k in runs[2]:
        wq.hop(k)
    for k in runs[0]:
        wo.hop(k)
    for k in runs[0]:
        kv_hop(k)
    wq.cross()
    for k in runs[1]:
        kv_hop(k)
    for k in runs[1]:
        wo.hop(k)
    ship(2, 3)
    prefetch(1)
    wq.finish()
    wq_m = merge_rows(wq_buf[...])
    for m in range(2):
        at = slice(m * half, (m + 1) * half)
        lin = dot(h1_out[at], wq_m) + bias[:, :q_cols]
        for h in range(heads):
            cols = slice(h * HEAD_SIZE, (h + 1) * HEAD_SIZE)
            q_out[at, cols] = turned(lin[:, cols], at).astype(BF)
    for sub in range(2):
        q_t[sub] = stack_heads(q_out, sub, half, heads).T
    acc_ref[...] = jnp.zeros_like(acc_ref)
    max_ref[...] = jnp.full_like(max_ref, FLOOR)
    sum_ref[...] = jnp.zeros_like(sum_ref)

    def fold(sub, block):
        keys = kv_buf[block + sub, :, :HEAD_SIZE]
        vals = kv_buf[block + sub, :, HEAD_SIZE:]
        start_row = start_ref[:, sub * half : (sub + 1) * half]
        scores = dot(keys, q_t[sub]) * scale + block_mask(
            sub, block, me, shards, half, start_row, heads
        )
        old_max = max_ref[sub]
        new_max = jnp.maximum(old_max, jnp.max(scores, axis=0, keepdims=True))
        weights = jnp.exp(scores - new_max)
        shrink = jnp.exp(old_max - new_max)
        max_ref[sub] = new_max
        sum_ref[sub] = sum_ref[sub] * shrink + jnp.sum(weights, axis=0, keepdims=True)
        acc_ref[sub] = acc_ref[sub] * shrink + dot(vals.T, weights.astype(BF))

    def attend(k, carry):
        low, high = z - k, z + k

        @pl.when((low >= 0) & (k < zs))
        def _():
            fold(0, 2 * low + x)

        @pl.when((high < zs) & (k < zs))
        def _():
            fold(1, 2 * high + x)

        far_low, far_high = low + 1, high - 1

        @pl.when((k > 0) & (far_low >= 0) & ((k > 1) | (x == 1)))
        def _():
            kv_side(far_low, 0, 1 - x).wait_recv()
            fold(0, 2 * far_low + 1 - x)

        @pl.when((k > 0) & (far_high < zs) & ((k > 1) | (x == 0)))
        def _():
            kv_side(far_high, 1, 1 - x).wait_recv()
            fold(1, 2 * far_high + 1 - x)

        @pl.when(k == 0)
        def _():
            for hop in runs[2]:
                kv_hop(hop)

        @pl.when(k == 1)
        def _():
            for hop in runs[2]:
                wo.hop(hop)

        @pl.when(k == 2)
        def _():
            dy_side(1).start()

        @pl.when(k == zs - 1)
        def _():
            prefetch(2)

        return carry

    lax.fori_loop(0, zs + 1, attend, 0)
    dy_side(0).start()
    ship(3, n1)
    wo.cross()
    for sub in range(2):
        lse_out[sub : sub + 1, :] = max_ref[sub] + jnp.log(sum_ref[sub])
        out_t = acc_ref[sub] / sum_ref[sub]
        for h in range(heads):
            attn_out[sub * half : (sub + 1) * half, h * HEAD_SIZE : (h + 1) * HEAD_SIZE] = (
                out_t[:, h * half : (h + 1) * half].T.astype(BF)
            )

    wo.finish()
    att_s, att_r = pool.take(2), pool.take(2)
    h_l, hx_s, hx_r, hy_s, hy_r = (pool.take(2) for _ in range(5))
    hxx_s, hxx_r, hyy_s, hyy_r = (pool.take() for _ in range(4))

    def rows(i):
        return pl.ds(i * quarter, quarter)

    def att_copy(i):
        to = {"tensor": 1 - t}
        return remote(att_send.at[rows(i)], att_recv.at[rows(i)], att_s(i), att_r(i), to)

    def h_copies(i):
        src, dst = h2_half.at[rows(i)], h2_all.at[2 * x + t, rows(i)]
        return (
            pltpu.make_async_copy(src, dst, h_l(i)),
            remote(src, dst, hx_s(i), hx_r(i), {"x": 1 - x}),
            remote(src, dst, hy_s(i), hy_r(i), {"tensor": 1 - t}),
        )

    wo_m = merge_rows(wo_buf[...])
    for i in range(2):
        at = pl.ds(pl.multiple_of((1 - t) * half + i * quarter, quarter), quarter)
        att_send[rows(i)] = dot_nt(attn_out[at], wo_m).astype(BF)
        att_copy(i).start()
    for i in range(2):
        at = pl.ds(pl.multiple_of(t * half + i * quarter, quarter), quarter)
        mid_out[rows(i)] = dot_nt(attn_out[at], wo_m) + x_ref[at].astype(F32)
    prefetch(3)
    for i in range(2):
        att_copy(i).wait_recv()
        mid = mid_out[rows(i)] + att_recv[rows(i)].astype(F32)
        mid_out[rows(i)] = mid
        h2_half[rows(i)] = (mid * norm_factor(mid) * gain_mlp).astype(BF)
        for copy in h_copies(i):
            copy.start()
    from_side = h2_all.at[2 * (1 - x) + t, rows(0)]
    from_across = h2_all.at[2 * x + 1 - t, rows(1)]
    relay_across = remote(from_side, from_side, hyy_s(), hyy_r(), {"tensor": 1 - t})
    relay_side = remote(from_across, from_across, hxx_s(), hxx_r(), {"x": 1 - x})
    dy_side(2).start()
    h_copies(0)[1].wait_recv()
    relay_across.start()
    prefetch(4)
    h_copies(1)[2].wait_recv()
    relay_side.start()
    dy_side(0).wait_recv()
    dy_across.start()
    for tick in range(5, n1 + 3):
        prefetch(tick)

    save = pool.take(4)
    saves = [
        pltpu.make_async_copy(src, dst, save(i))
        for i, (src, dst) in enumerate(
            ((wkv_buf, wkv_all), (wq_buf, wq_all), (wo_buf, wo_all), (kv_buf, kv_all))
        )
    ]
    for copy in saves:
        copy.start()

    for item in (small, wkv, wq, wo):
        item.drain()

    def kv_drain(s, carry):
        @pl.when((s <= z) & (z < zs - 1))
        def _():
            kv_up(s).wait_send()

        @pl.when((s >= z) & (z > 0))
        def _():
            kv_dn(s).wait_send()

        @pl.when((s < z) | ((s == z) & (x == 0)))
        def _():
            kv_side(s, 0, x).wait_send()

        @pl.when((s > z) | ((s == z) & (x == 1)))
        def _():
            kv_side(s, 1, x).wait_send()

        return carry

    lax.fori_loop(0, zs, kv_drain, 0)
    relay_across.wait()
    relay_side.wait()
    dy_across.wait()
    for i in range(3):
        dy_side(i).wait_send()
        if i > 0:
            dy_side(i).wait_recv()
    for i in range(2):
        att_copy(i).wait_send()
        own, side, across = h_copies(i)
        own.wait()
        side.wait_send()
        across.wait_send()
    h_copies(1)[1].wait_recv()
    h_copies(0)[2].wait_recv()
    if n1:
        for c in range(n1):
            trade.sent(c, c)
            gather.finish(c)
            gather.drain(c)
    for copy in saves + [dy_own]:
        copy.wait()


def forward_call(
    zs, heads, n1, skip, fc, x_in, wkv_in, wq_in, wo_in, small_in, cos, sin, start, dy_in, first
):
    tok, width = x_in.shape
    half = tok // 2
    homes = 4 * zs
    rows, q_cols = wq_in.shape
    shape = jax.ShapeDtypeStruct
    any_spec = pl.BlockSpec(memory_space=pl.ANY)
    out = [
        shape((tok, width), BF),
        shape((tok, q_cols), BF),
        shape((tok, q_cols), BF),
        shape((2, heads * half), F32),
        shape((half, width), F32),
        shape(small_in.shape, F32),
        shape((homes, rows, 2 * HEAD_SIZE), BF),
        shape((homes, rows, q_cols), BF),
        shape((homes, rows, q_cols), BF),
        shape((2 * zs + 1, half, 2 * HEAD_SIZE), BF),
        shape((4, half, width), BF),
        shape((4, half, width), BF),
    ]
    sems = [pltpu.SemaphoreType.DMA((4 * (9 * zs + 1) + 8 * zs + 3 * n1 + 40,))]
    if n1:
        out.append(shape((n1, width, 3 * fc), BF))
        sems += [pltpu.SemaphoreType.DMA((n1, zs))] * 5
    return pl.pallas_call(
        functools.partial(forward_kernel, zs, heads, n1, skip, HEAD_SIZE ** (-0.5)),
        out_shape=out,
        in_specs=[VMEM] + [any_spec] * 4 + [VMEM] * (4 + len(first)),
        out_specs=[VMEM] * 6 + [any_spec] * (len(out) - 6),
        scratch_shapes=[
            pltpu.VMEM((homes,) + small_in.shape, BF),
            pltpu.VMEM((homes, rows, 2 * HEAD_SIZE), BF),
            pltpu.VMEM((homes, rows, q_cols), BF),
            pltpu.VMEM((homes, rows, q_cols), BF),
            pltpu.VMEM((2 * zs + 1, half, 2 * HEAD_SIZE), BF),
            pltpu.VMEM((2, HEAD_SIZE, heads * half), BF),
            pltpu.VMEM((2, HEAD_SIZE, heads * half), F32),
            pltpu.VMEM((2, 1, heads * half), F32),
            pltpu.VMEM((2, 1, heads * half), F32),
            pltpu.VMEM((half, width), BF),
            pltpu.VMEM((half, width), BF),
            pltpu.VMEM((half, width), BF),
            pltpu.VMEM((tok, width), F32),
        ]
        + sems,
        compiler_params=pltpu.CompilerParams(
            collective_id=1, has_side_effects=True, vmem_limit_bytes=60 * 2**20
        ),
        cost_estimate=pl.CostEstimate(
            flops=4 * tok * width * (q_cols + HEAD_SIZE) + 2**31,
            bytes_accessed=32 * 2**20,
            transcendentals=0,
        ),
    )(x_in, wkv_in, wq_in, wo_in, small_in, cos, sin, start, dy_in, *first)


class Square:
    def __init__(self, src, own, r_one, r_two, pool):
        self.src, self.own, self.r_one, self.r_two = src, own, r_one, r_two
        self.x, self.t = lax.axis_index("x"), lax.axis_index("tensor")
        self.cut = src.shape[2] // 2
        self.one_s, self.one_r = pool.take(3), pool.take(3)
        self.two_s, self.two_r = pool.take(2), pool.take(2)
        self.load = pool.take(3)

    def first(self):
        x, t, cut, src = self.x, self.t, self.cut, self.src
        left, right = pl.ds(0, cut), pl.ds(cut, cut)
        sends = [
            remote(
                src.at[pl.ds(2 * (1 - x), 2), :, left],
                self.r_one.at[pl.ds(0, 2)],
                self.one_s(0),
                self.one_r(0),
                {"x": 1 - x},
            )
        ]
        for i in range(2):
            sends.append(
                remote(
                    src.at[2 * i + 1 - t, :, right],
                    self.r_one.at[2 + i],
                    self.one_s(1 + i),
                    self.one_r(1 + i),
                    {"tensor": 1 - t},
                )
            )
        return sends

    def loads(self):
        x, t, cut, src = self.x, self.t, self.cut, self.src
        left, right = pl.ds(0, cut), pl.ds(cut, cut)
        loads = [
            pltpu.make_async_copy(
                src.at[pl.ds(2 * x, 2), :, left], self.own.at[pl.ds(0, 2)], self.load(0)
            )
        ]
        for i in range(2):
            loads.append(
                pltpu.make_async_copy(
                    src.at[2 * i + t, :, right], self.own.at[2 + i], self.load(1 + i)
                )
            )
        return loads

    def second(self):
        x, t = self.x, self.t
        return [
            remote(
                self.own.at[1 - t],
                self.r_two.at[0],
                self.two_s(0),
                self.two_r(0),
                {"tensor": 1 - t},
            ),
            remote(
                self.own.at[3 - x],
                self.r_two.at[1],
                self.two_s(1),
                self.two_r(1),
                {"x": 1 - x},
            ),
        ]

    def start(self):
        for copy in self.first() + self.loads():
            copy.start()

    def turn(self):
        for copy in self.loads():
            copy.wait()
        for copy in self.first():
            copy.wait_recv()
        for i in range(4):
            self.own[i] = self.own[i] + self.r_one[i]
        for copy in self.second():
            copy.start()

    def result(self):
        for copy in self.second():
            copy.wait_recv()
        left = self.own[self.t].astype(F32) + self.r_two[0].astype(F32)
        right = self.own[2 + self.x].astype(F32) + self.r_two[1].astype(F32)
        return jnp.concatenate([left, right], axis=1)

    def drain(self):
        for copy in self.first() + self.second():
            copy.wait_send()


class Collect:
    def __init__(self, zs, acc, to_sib, r_sib, r_x, r_z, out, pool):
        self.zs, self.acc, self.to_sib, self.r_sib = zs, acc, to_sib, r_sib
        self.r_x, self.r_z, self.out = r_x, r_z, out
        self.b, self.z, self.x = (lax.axis_index(a) for a in ("batch", "z", "x"))
        self.s_s, self.s_r, self.x_s, self.x_r, self.loc = (pool.take() for _ in range(5))
        self.d_s, self.d_r, self.u_s, self.u_r = (pool.take(zs) for _ in range(4))

    def sib(self):
        return remote(self.to_sib, self.r_sib, self.s_s(), self.s_r(), {"batch": 1 - self.b})

    def side(self):
        return remote(
            self.acc.at[1 - self.x], self.r_x, self.x_s(), self.x_r(), {"x": 1 - self.x}
        )

    def dn(self, h):
        return remote(
            self.acc.at[self.x, h], self.r_z.at[h], self.d_s(h), self.d_r(h), {"z": self.z - 1}
        )

    def up(self, h):
        return remote(
            self.acc.at[self.x, h], self.r_z.at[h + 1], self.u_s(h), self.u_r(h), {"z": self.z + 1}
        )

    def fill(self, make):
        rows = self.acc.shape[2]
        for buf, core in ((self.to_sib, 1 - self.b), (self.acc, self.b)):
            value = make(core)
            for h in range(self.zs):
                for col in range(2):
                    i = 2 * h + col
                    buf[col, h] = value[i * rows : (i + 1) * rows].astype(BF)
            if buf is self.to_sib:
                self.sib().start()

    def add(self, dst, src):
        dst[...] = dst[...] + src[...]

    def after_sib(self):
        self.sib().wait_recv()

        def one(h, carry):
            self.add(self.acc.at[1 - self.x, h], self.r_sib.at[1 - self.x, h])
            return carry

        lax.fori_loop(0, self.zs, one, 0)
        self.side().start()

        def other(h, carry):
            self.add(self.acc.at[self.x, h], self.r_sib.at[self.x, h])
            return carry

        lax.fori_loop(0, self.zs, other, 0)

    def after_side(self):
        self.side().wait_recv()

        def one(h, carry):
            self.add(self.acc.at[self.x, h], self.r_x.at[h])
            return carry

        lax.fori_loop(0, self.zs, one, 0)

        def ends(h, carry):
            @pl.when((self.z == self.zs - 1) & (h < self.z))
            def _():
                self.dn(h).start()

            @pl.when((self.z == 0) & (h > 0))
            def _():
                self.up(h).start()

            return carry

        lax.fori_loop(0, self.zs, ends, 0)

    def step(self, k):
        def one(i, carry):
            @pl.when((self.z == self.zs - 1 - k) & (i <= self.z))
            def _():
                self.dn(i).wait_recv()
                self.add(self.acc.at[self.x, i], self.r_z.at[i])

                @pl.when(i < self.z)
                def _():
                    self.dn(i).start()

            j = self.zs - 1 - i

            @pl.when((self.z == k) & (j >= self.z))
            def _():
                self.up(j).wait_recv()
                self.add(self.acc.at[self.x, j], self.r_z.at[j + 1])

                @pl.when(j > self.z)
                def _():
                    self.up(j).start()

            return carry

        lax.fori_loop(0, self.zs, one, 0)
        if k == self.zs - 1:
            self.result().start()

    def result(self):
        return pltpu.make_async_copy(self.acc.at[self.x, self.z], self.out, self.loc())

    def drain(self):
        self.sib().wait_send()
        self.side().wait_send()
        self.result().wait()

        def one(h, carry):
            @pl.when(h < self.z)
            def _():
                self.dn(h).wait_send()

            @pl.when(h > self.z)
            def _():
                self.up(h).wait_send()

            return carry

        lax.fori_loop(0, self.zs, one, 0)


class LineSum:
    def __init__(self, zs, acc, r_z, pool):
        self.zs, self.acc, self.r_z = zs, acc, r_z
        self.z = lax.axis_index("z")
        self.d_s, self.d_r, self.u_s, self.u_r = (pool.take(zs) for _ in range(4))

    def dn(self, h):
        to = {"z": self.z - 1}
        return remote(self.acc.at[:, h], self.r_z.at[:, h], self.d_s(h), self.d_r(h), to)

    def up(self, h):
        to = {"z": self.z + 1}
        return remote(self.acc.at[:, h], self.r_z.at[:, h + 1], self.u_s(h), self.u_r(h), to)

    def start(self):
        for h in range(self.zs):
            if h < self.zs - 1:

                @pl.when(self.z == self.zs - 1)
                def _():
                    self.dn(h).start()

            if h > 0:

                @pl.when(self.z == 0)
                def _():
                    self.up(self.zs - h).start()

    def plus(self, h, slot):
        for c in range(self.acc.shape[0]):
            self.acc[c, h] = self.acc[c, h] + self.r_z[c, slot]

    def step(self, k):
        def one(i, carry):
            @pl.when((self.z == self.zs - 1 - k) & (i <= self.z))
            def _():
                self.dn(i).wait_recv()
                self.plus(i, i)

                @pl.when(i < self.z)
                def _():
                    self.dn(i).start()

            j = self.zs - 1 - i

            @pl.when((self.z == k) & (j >= self.z))
            def _():
                self.up(j).wait_recv()
                self.plus(j, j + 1)

                @pl.when(j > self.z)
                def _():
                    self.up(j).start()

            return carry

        lax.fori_loop(0, self.zs, one, 0)

    def drain(self):
        def one(h, carry):
            @pl.when(h < self.z)
            def _():
                self.dn(h).wait_send()

            @pl.when(h > self.z)
            def _():
                self.up(h).wait_send()

            return carry

        lax.fori_loop(0, self.zs, one, 0)


def backward_kernel(zs, heads, nl, scale, *refs):
    refs = list(refs)

    def take(count):
        out = refs[:count]
        del refs[:count]
        return out

    y_in, g_mlp, x_in, dy_in = take(4)
    if nl:
        (left_in,) = take(1)
    dh2_ref, mid_ref, vec_ref, h1_ref, q_ref, attn_ref, lse_ref, kv_ref = take(8)
    wkv_ref, wq_ref, wo_ref, cos_ref, sin_ref, start_ref = take(6)
    out_all, gh_all, g_q, g_kv, g_wo, g_vec, g_far = take(7)
    if nl:
        (left_out,) = take(1)
    y_own, y_one, y_two, dmid_ref, dat_ref, half_ref = take(6)
    q_s, do_s, q_t, do_t, delta_ref = take(5)
    dkv_ref, rx_ref, rz_ref, acc_ref, dqkv_ref, dh_send, dh_recv = take(7)
    bufs_q, bufs_kv, bufs_wo = take(5), take(5), take(5)
    vec_own, vec_recv, vec_z, x_ref, dy_ref, sem_ref = take(6)
    if nl:
        left_acc, left_z = take(2)

    b, z, x, t = (lax.axis_index(a) for a in ("batch", "z", "x", "tensor"))
    shards = 2 * zs
    me = 2 * z + x
    half, width = mid_ref.shape
    q_cols = heads * HEAD_SIZE
    pool = Pool(sem_ref)
    greet(z, zs)

    sq_y = Square(y_in, y_own, y_one, y_two, pool)
    col_q = Collect(zs, *bufs_q, g_q, pool)
    col_kv = Collect(zs, *bufs_kv, g_kv, pool)
    col_wo = Collect(zs, *bufs_wo, g_wo, pool)
    runs = thirds(zs)
    mine = pl.ds(pl.multiple_of(t * half, half), half)
    fetch = pool.take(2)
    x_load = pltpu.make_async_copy(x_in.at[mine], x_ref, fetch(0))
    dy_load = pltpu.make_async_copy(dy_in.at[mine], dy_ref, fetch(1))
    x_load.start()
    dy_load.start()
    if nl:
        lines = [
            LineSum(zs, left_acc.at[pl.ds(c, 1)], left_z.at[pl.ds(c, 1)], pool) for c in range(nl)
        ]
        left_l = pool.take()
        left_load = pltpu.make_async_copy(left_in, left_acc, left_l())
        left_load.start()

    def line_tick(tick):
        for c in range(nl):
            if tick == c:
                lines[c].start()
            for k in range(1, zs):
                if min(k, 3) == tick - c:
                    lines[c].step(k)

    vec = vec_ref[...]
    gain_attn = lanes(vec, 4, 6)
    gain_mlp = lanes(vec, 10, 6)

    mid = mid_ref[...]
    d_norm, g_norm_mlp = norm_backward(mid, norm_factor(mid), gain_mlp, dh2_ref[...])
    dy_load.wait()
    dmid_ref[...] = dy_ref[...].astype(F32) + d_norm
    dat_ref[t] = dmid_ref[...].astype(BF)
    dat_s, dat_r = pool.take(), pool.take()

    def dat_copy(i):
        return remote(dat_ref.at[i], dat_ref.at[i], dat_s(), dat_r(), {"tensor": 1 - t})

    dat_copy(t).start()
    if nl:
        left_load.wait()
        line_tick(0)

    x0_s, x0_r, x1_s, x1_r = (pool.take(zs) for _ in range(4))
    c0_s, c0_r, c1_s, c1_r = (pool.take(zs) for _ in range(4))

    def side(s, sub):
        src = dkv_ref.at[2 * s + 1 - x + sub]
        send, recv = (x0_s, x0_r) if sub == 0 else (x1_s, x1_r)
        return remote(src, rx_ref.at[s + sub], send(s), recv(s), {"x": 1 - x})

    def chain(s, sub):
        src = dkv_ref.at[2 * s + x + sub]
        send, recv = (c0_s, c0_r) if sub == 0 else (c1_s, c1_r)
        to = z - 1 if sub == 0 else z + 1
        return remote(src, rz_ref.at[s + sub], send(s), recv(s), {"z": to})

    acc_ref[...] = jnp.zeros_like(acc_ref)

    def prepare(sub):
        d_out = dot(dat_ref[sub], merge_rows(wo_ref[...])).astype(BF)
        rows = pl.ds(pl.multiple_of(sub * half, half), half)
        out = attn_ref[rows]
        q = q_ref[rows]
        for h in range(heads):
            cols = slice(h * HEAD_SIZE, (h + 1) * HEAD_SIZE)
            at = slice(h * half, (h + 1) * half)
            q_s[sub, at] = q[:, cols]
            do_s[sub, at] = d_out[:, cols]
            q_t[sub, :, at] = q[:, cols].T
            do_h = d_out[:, cols].T
            do_t[sub, :, at] = do_h
            delta_ref[sub, :, at] = jnp.sum(
                do_h.astype(F32) * out[:, cols].T.astype(F32), axis=0, keepdims=True
            )

    def fold(sub, block):
        slot = block + sub
        keys = kv_ref[slot, :, :HEAD_SIZE]
        vals = kv_ref[slot, :, HEAD_SIZE:]
        scores = dot(keys, q_t[sub]) * scale + block_mask(
            sub, block, me, shards, half, start_ref[sub], heads
        )
        probs = jnp.exp(scores - lse_ref[sub])
        d_scores = (probs * (dot(vals, do_t[sub]) - delta_ref[sub])).astype(BF)
        dkv_ref[slot, :, HEAD_SIZE:] = dot(probs.astype(BF), do_s[sub]).astype(BF)
        dkv_ref[slot, :, :HEAD_SIZE] = (dot(d_scores, q_s[sub]) * scale).astype(BF)
        acc_ref[sub] += dot(keys.T, d_scores)

    def far_blocks(sub):
        def one(k, carry):
            s = jnp.where(sub == 0, z - k, z + k)

            @pl.when(in_range(s, zs) & ((k > 0) | (x != sub)))
            def _():
                fold(sub, 2 * s + 1 - x)

                @pl.when(sub == 0)
                def _():
                    side(s, 0).start()

                @pl.when(sub == 1)
                def _():
                    side(s, 1).start()

            return carry

        lax.fori_loop(0, zs, one, 0)

    def near_blocks(sub):
        def one(i, carry):
            k = zs - 1 - i
            s = jnp.where(sub == 0, z - k, z + k)

            @pl.when(in_range(s, zs))
            def _():
                fold(sub, 2 * s + x)

            return carry

        lax.fori_loop(0, zs, one, 0)

    def tokens(i, carry):
        sub = jnp.where(i == 0, t, 1 - t)

        @pl.when(i == 1)
        def _():
            line_tick(1)
            dat_copy(1 - t).wait_recv()

        prepare(sub)
        far_blocks(sub)
        near_blocks(sub)
        return carry

    lax.fori_loop(0, 2, tokens, 0)
    sq_y.start()

    def wo_part(core):
        rows = width // 2
        at = pl.ds(pl.multiple_of(core * rows, rows), rows)
        return dot(half_ref[at], attn_ref[...])

    def plus(slot, src):
        dkv_ref[slot] = dkv_ref[slot] + src[...]

    def kv_begin():
        def one(i, carry):
            j = zs - 1 - i

            @pl.when((i < z) | ((i == z) & (x == 0)))
            def _():
                side(i, 0).wait_recv()
                plus(2 * i + x, rx_ref.at[i])

            @pl.when((z == zs - 1) & (i < z))
            def _():
                chain(i, 0).start()

            @pl.when((j > z) | ((j == z) & (x == 1)))
            def _():
                side(j, 1).wait_recv()
                plus(2 * j + x + 1, rx_ref.at[j + 1])

            @pl.when((z == 0) & (j > z))
            def _():
                chain(j, 1).start()

            return carry

        lax.fori_loop(0, zs, one, 0)

    def kv_step(k):
        def one(i, carry):
            j = zs - 1 - i

            @pl.when((z == zs - 1 - k) & (i <= z))
            def _():
                chain(i, 0).wait_recv()
                plus(2 * i + x, rz_ref.at[i])

                @pl.when(i < z)
                def _():
                    chain(i, 0).start()

            @pl.when((z == k) & (j >= z))
            def _():
                chain(j, 1).wait_recv()
                plus(2 * j + x + 1, rz_ref.at[j + 1])

                @pl.when(j > z)
                def _():
                    chain(j, 1).start()

            return carry

        lax.fori_loop(0, zs, one, 0)

    kv_begin()
    for i in range(2):
        half_ref[:, i * half : (i + 1) * half] = dat_ref[i].T
    col_wo.fill(wo_part)
    for k in runs[0] + runs[1]:
        kv_step(k)
    line_tick(2)
    col_wo.after_sib()

    def back(v, at):
        return v * cos_ref[at] - pltpu.roll(v, HEAD_SIZE // 2, 1) * sin_ref[at]

    for sub in range(2):
        at = slice(sub * half, (sub + 1) * half)
        for h in range(heads):
            v = acc_ref[sub, :, h * half : (h + 1) * half].T * scale
            dqkv_ref[at, h * HEAD_SIZE : (h + 1) * HEAD_SIZE] = back(v, at).astype(BF)
    half_ref[...] = h1_ref[...].T
    for k in runs[2]:
        kv_step(k)

    def part(first, last):
        def make(core):
            rows = width // 2
            at = pl.ds(pl.multiple_of(core * rows, rows), rows)
            return dot(half_ref[at], dqkv_ref[:, first:last])

        return make

    for sub in range(2):
        at = slice(sub * half, (sub + 1) * half)
        dk = dkv_ref[me + sub, :, :HEAD_SIZE].astype(F32)
        dqkv_ref[at, q_cols : q_cols + HEAD_SIZE] = back(dk, at).astype(BF)
        dqkv_ref[at, q_cols + HEAD_SIZE :] = dkv_ref[me + sub, :, HEAD_SIZE:]

    dh_s, dh_r = pool.take(), pool.take()
    dh_copy = remote(dh_send, dh_recv, dh_s(), dh_r(), {"tensor": 1 - t})
    theirs = pl.ds(pl.multiple_of((1 - t) * half, half), half)
    own = pl.ds(pl.multiple_of(t * half, half), half)

    def d_first(at):
        q_part = dot_nt(dqkv_ref[at, :q_cols], merge_rows(wq_ref[...]))
        return q_part + dot_nt(dqkv_ref[at, q_cols:], merge_rows(wkv_ref[...]))

    dh_send[...] = d_first(theirs).astype(BF)
    dh_copy.start()
    dh1 = d_first(own)
    sq_y.turn()
    col_kv.fill(part(q_cols, q_cols + 2 * HEAD_SIZE))
    col_q.fill(part(0, q_cols))
    line_tick(3)
    col_q.after_sib()
    col_kv.after_sib()

    dh_copy.wait_recv()
    dh1 = dh1 + dh_recv[...].astype(F32)
    x_load.wait()
    xv = x_ref[...].astype(F32)
    d_norm, g_norm_attn = norm_backward(xv, norm_factor(xv), gain_attn, dh1)

    g_bias = jnp.sum(dqkv_ref[...].astype(F32), axis=0, keepdims=True)
    row = jnp.concatenate([g_bias, g_norm_attn, g_norm_mlp], axis=1)
    lane = vec_ref.shape[1]
    vec_own[...] = jnp.concatenate(
        [row[:, i * lane : (i + 1) * lane] for i in range(vec_ref.shape[0])], axis=0
    )
    v_s, v_r = pool.take(3), pool.take(3)
    vz_s, vz_r = pool.take(zs), pool.take(zs)
    norms = (lax.broadcasted_iota(jnp.int32, vec_ref.shape, 0) >= 4).astype(F32)

    def v_side(i):
        axis, index = (("tensor", t), ("x", x), ("batch", b))[i]
        return remote(vec_own, vec_recv.at[i], v_s(i), v_r(i), {axis: 1 - index})

    def v_add(i):
        v_side(i).wait()
        other = vec_recv[i]
        vec_own[...] = vec_own[...] + (other * norms if i == 0 else other)

    v_side(0).start()
    line_tick(4)
    dat_copy(t).wait_send()
    dat_ref[t] = (dmid_ref[...] + d_norm).astype(BF)
    gh_s, gh_r, gh_l = (pool.take() for _ in range(3))
    gh_copy = remote(dat_ref.at[t], gh_all.at[t], gh_s(), gh_r(), {"tensor": 1 - t})
    gh_own = pltpu.make_async_copy(dat_ref.at[t], gh_all.at[t], gh_l())
    gh_copy.start()
    gh_own.start()
    v_add(0)
    v_side(1).start()
    col_wo.after_side()
    far_s, far_r = pool.take(), pool.take()
    far_copy = remote(
        g_mlp.at[:, 1 - x],
        g_far.at[pl.ds(0, g_mlp.shape[0])],
        far_s(),
        far_r(),
        {"x": 1 - x},
    )
    far_copy.start()
    line_tick(5)
    for k in runs[0]:
        col_wo.step(k)
    col_q.after_side()
    v_add(1)
    v_side(2).start()
    col_kv.after_side()
    y_sum = sq_y.result()
    sq_y.drain()
    total = mid_ref[...] + y_sum
    cut = width // 2
    o_s, o_r, o_l = pool.take(2), pool.take(2), pool.take(2)
    sends, locals_ = [], []
    for i in range(2):
        y_own[i] = total[:, i * cut : (i + 1) * cut].astype(BF)
        dst = out_all.at[t, :, pl.ds(i * cut, cut)]
        sends.append(remote(y_own.at[i], dst, o_s(i), o_r(i), {"tensor": 1 - t}))
        locals_.append(pltpu.make_async_copy(y_own.at[i], dst, o_l(i)))
    for copy in sends + locals_:
        copy.start()
    for tick in range(6, nl + 3):
        line_tick(tick)
    v_add(2)
    for k in runs[0]:
        col_q.step(k)
    for k in runs[1]:
        col_wo.step(k)
    if nl:
        lf_s, lf_r, lf_l = (pool.take() for _ in range(3))
        rows = g_far.shape[1]

        def left_rows(col):
            return left_acc.at[:, z, pl.ds(pl.multiple_of(col * rows, rows), rows)]

        left_far = remote(
            left_rows(1 - x),
            g_far.at[pl.ds(g_mlp.shape[0], nl)],
            lf_s(),
            lf_r(),
            {"x": 1 - x},
        )
        left_own = pltpu.make_async_copy(left_rows(x), left_out, lf_l())
        left_far.start()
        left_own.start()
    for k in runs[0]:
        col_kv.step(k)

    def v_copy(to):
        return remote(vec_own, vec_z.at[z], vz_s(to), vz_r(z), {"z": to})

    for to in range(zs):

        @pl.when(to != z)
        def _():
            v_copy(to).start()

    for k in runs[1]:
        col_q.step(k)
    for k in runs[1]:
        col_kv.step(k)
    for item in (col_wo, col_q, col_kv):
        for k in runs[2]:
            item.step(k)
    total = jnp.zeros(vec_ref.shape, F32)
    for frm in range(zs):

        @pl.when(frm != z)
        def _():
            remote(vec_own, vec_z.at[frm], vz_s(frm), vz_r(frm), {"z": frm}).wait_recv()

        @pl.when(frm == z)
        def _():
            vec_z[frm] = vec_own[...]

        total = total + vec_z[frm]
    g_vec[...] = total

    for to in range(zs):

        @pl.when(to != z)
        def _():
            v_copy(to).wait_send()

    def dkv_drain(s, carry):
        @pl.when((s < z) | ((s == z) & (x == 1)))
        def _():
            side(s, 0).wait_send()

        @pl.when((s > z) | ((s == z) & (x == 0)))
        def _():
            side(s, 1).wait_send()

        @pl.when(s < z)
        def _():
            chain(s, 0).wait_send()

        @pl.when(s > z)
        def _():
            chain(s, 1).wait_send()

        return carry

    lax.fori_loop(0, zs, dkv_drain, 0)
    for item in (col_wo, col_q, col_kv):
        item.drain()
    dh_copy.wait_send()
    far_copy.wait()
    gh_own.wait()
    gh_copy.wait()
    for copy in sends + locals_:
        copy.wait()
    if nl:
        for item in lines:
            item.drain()
        left_far.wait()
        left_own.wait()


def backward_call(zs, heads, left, big, small):
    mid, vec = small[1:3]
    wq = small[9]
    half, width = mid.shape
    tok = 2 * half
    _, rows, q_cols = wq.shape
    qkv_cols = q_cols + 2 * HEAD_SIZE
    n2, _, _, three = big[1].shape
    nl = left[0].shape[0] if left else 0
    shape = jax.ShapeDtypeStruct
    any_spec = pl.BlockSpec(memory_space=pl.ANY)
    vm = pltpu.VMEM
    cut = width // 2

    def collect(cols):
        return [
            vm((2, zs, rows, cols), BF),
            vm((2, zs, rows, cols), BF),
            vm((2, zs, rows, cols), BF),
            vm((zs, rows, cols), BF),
            vm((zs + 1, rows, cols), BF),
        ]

    square = [vm((4, half, cut), BF), vm((4, half, cut), BF), vm((2, half, cut), BF)]
    lines = [vm(left[0].shape, BF), vm((nl, zs + 1) + left[0].shape[2:], BF)] if nl else []
    return pl.pallas_call(
        functools.partial(backward_kernel, zs, heads, nl, HEAD_SIZE ** (-0.5)),
        out_shape=[
            shape((2, half, width), BF),
            shape((2, half, width), BF),
            shape((rows, q_cols), BF),
            shape((rows, 2 * HEAD_SIZE), BF),
            shape((rows, q_cols), BF),
            shape(vec.shape, F32),
            shape((n2 + nl, rows, three), BF),
        ]
        + ([shape((nl, rows, three), BF)] if nl else []),
        in_specs=[any_spec] * (4 + len(left)) + [VMEM] * len(small),
        out_specs=[any_spec] * 5 + [VMEM, any_spec] + [any_spec] * len(left),
        scratch_shapes=square
        + [
            vm((half, width), F32),
            vm((2, half, width), BF),
            vm((width, tok), BF),
            vm((2, heads * half, HEAD_SIZE), BF),
            vm((2, heads * half, HEAD_SIZE), BF),
            vm((2, HEAD_SIZE, heads * half), BF),
            vm((2, HEAD_SIZE, heads * half), BF),
            vm((2, 1, heads * half), F32),
            vm((2 * zs + 1, half, 2 * HEAD_SIZE), BF),
            vm((zs + 1, half, 2 * HEAD_SIZE), BF),
            vm((zs + 1, half, 2 * HEAD_SIZE), BF),
            vm((2, HEAD_SIZE, heads * half), F32),
            vm((tok, qkv_cols), BF),
            vm((half, width), BF),
            vm((half, width), BF),
        ]
        + collect(q_cols)
        + collect(2 * HEAD_SIZE)
        + collect(q_cols)
        + [
            vm(vec.shape, F32),
            vm((3,) + vec.shape, F32),
            vm((zs,) + vec.shape, F32),
            vm((half, width), BF),
            vm((half, width), BF),
            pltpu.SemaphoreType.DMA(((22 + 4 * nl) * zs + 90,)),
        ]
        + lines,
        compiler_params=pltpu.CompilerParams(
            collective_id=2, has_side_effects=True, vmem_limit_bytes=63 * 2**20
        ),
        cost_estimate=pl.CostEstimate(
            flops=4 * tok * width * (qkv_cols + q_cols) + 2**32,
            bytes_accessed=32 * 2**20,
            transcendentals=0,
        ),
    )(*big, *left, *small)


def remote(src, dst, send, recv, to):
    return pltpu.make_async_remote_copy(
        src_ref=src,
        dst_ref=dst,
        send_sem=send,
        recv_sem=recv,
        device_id=to,
        device_id_type=pl.DeviceIdType.MESH,
    )


def greet(z, zs):
    barrier = pltpu.get_barrier_semaphore()
    for axis in ("batch", "x", "tensor"):
        other = {axis: 1 - lax.axis_index(axis)}
        pl.semaphore_signal(barrier, inc=1, device_id=other, device_id_type=pl.DeviceIdType.MESH)

    @pl.when(z > 0)
    def _():
        pl.semaphore_signal(
            barrier, inc=1, device_id={"z": z - 1}, device_id_type=pl.DeviceIdType.MESH
        )

    @pl.when(z < zs - 1)
    def _():
        pl.semaphore_signal(
            barrier, inc=1, device_id={"z": z + 1}, device_id_type=pl.DeviceIdType.MESH
        )

    pl.semaphore_wait(barrier, 5 - (z == 0).astype(jnp.int32) - (z == zs - 1).astype(jnp.int32))


def in_range(c, count):
    return (c >= 0) & (c < count)


class Exchange:
    def __init__(self, mats, full, first, zs, skip, sems):
        self.mats, self.full, self.first = mats, full, first
        self.x = lax.axis_index("x")
        home = (lax.axis_index("batch") * zs + lax.axis_index("z")) * 2 + self.x
        self.rows, self.cols = mats[0].shape[0], full.shape[2] // 3
        self.at = pl.ds(pl.multiple_of(home * self.rows, self.rows), self.rows)
        self.shift = mats[0].shape[1] // 2 - skip // 2
        self.send, self.recv, self.loc = sems

    def pieces(self, c):
        for w, mat in enumerate(self.mats):
            dst = self.full.at[c, self.at, pl.ds(w * self.cols, self.cols)]
            yield mat, dst

    def source(self, mat, c, x):
        first = pl.multiple_of(x * self.shift + (self.first + c) * self.cols, 128)
        return mat.at[:, pl.ds(first, self.cols)]

    def ship(self, c, i):
        for mat, dst in self.pieces(c):
            src = self.source(mat, c, 1 - self.x)
            remote(src, dst, self.send(i), self.recv(i), {"x": 1 - self.x}).start()

    def keep(self, c, i):
        for mat, dst in self.pieces(c):
            pltpu.make_async_copy(self.source(mat, c, self.x), dst, self.loc(i)).start()

    def fetch(self, c, other, buf, sem):
        x = 1 - self.x if other else self.x
        for w, mat in enumerate(self.mats):
            dst = buf.at[pl.ds(c * self.rows, self.rows), pl.ds(w * self.cols, self.cols)]
            pltpu.make_async_copy(self.source(mat, c, x), dst, sem).start()

    def both(self, c, i):
        spot = self.full.at[c, self.at]
        return remote(spot, spot, self.send(i), self.recv(i), {"x": 1 - self.x})

    def arrived(self, c, i):
        self.both(c, i).wait_recv()
        spot = self.full.at[c, self.at]
        pltpu.make_async_copy(spot, spot, self.loc(i)).wait()

    def sent(self, c, i):
        self.both(c, i).wait_send()


class Gather:
    def __init__(self, zs, mine, full, sems):
        self.zs, self.mine, self.full = zs, mine, full
        self.loc, self.up, self.dn, self.zr, self.ss, self.sr = sems
        self.b, self.z = lax.axis_index("batch"), lax.axis_index("z")
        self.size = full.shape[1] // (2 * zs)

    def at(self, c, b, z):
        rows = pl.ds(pl.multiple_of((b * self.zs + z) * self.size, self.size), self.size)
        return self.full.at[:, rows] if c is None else self.full.at[c, rows]

    def sems(self, c, s):
        i = 0 if c is None else c
        return (ref.at[i, s] for ref in (self.up, self.dn, self.zr, self.ss, self.sr))

    def up_copy(self, c, s, src=None):
        dst = self.at(c, self.b, s)
        up, _, zr, _, _ = self.sems(c, s)
        return remote(dst if src is None else src, dst, up, zr, {"z": self.z + 1})

    def dn_copy(self, c, s, src=None):
        dst = self.at(c, self.b, s)
        _, dn, zr, _, _ = self.sems(c, s)
        return remote(dst if src is None else src, dst, dn, zr, {"z": self.z - 1})

    def sib_copy(self, c, s, src=None):
        dst = self.at(c, self.b, s)
        _, _, _, ss, sr = self.sems(c, s)
        return remote(dst if src is None else src, dst, ss, sr, {"batch": 1 - self.b})

    def local(self, c):
        return pltpu.make_async_copy(self.mine.at[c], self.at(c, self.b, self.z), self.loc.at[c])

    def start(self, c):
        src = None if self.mine is None else self.mine.at[c]

        @pl.when(self.z < self.zs - 1)
        def _():
            self.up_copy(c, self.z, src).start()

        @pl.when(self.z > 0)
        def _():
            self.dn_copy(c, self.z, src).start()

        self.sib_copy(c, self.z, src).start()
        if self.mine is not None:
            self.local(c).start()

    def hop(self, c, k):
        low, high = self.z - k, self.z + k

        @pl.when(low >= 0)
        def _():
            self.dn_copy(c, low).wait_recv()

            @pl.when(self.z < self.zs - 1)
            def _():
                self.up_copy(c, low).start()

            self.sib_copy(c, low).start()

        @pl.when(high < self.zs)
        def _():
            self.dn_copy(c, high).wait_recv()

            @pl.when(self.z > 0)
            def _():
                self.dn_copy(c, high).start()

            self.sib_copy(c, high).start()

    def finish(self, c):
        if self.mine is not None:
            self.local(c).wait()
        for s in range(self.zs):
            dst = self.at(c, 1 - self.b, s)
            _, _, _, ss, sr = self.sems(c, s)
            remote(dst, dst, ss, sr, {"batch": 1 - self.b}).wait_recv()

    def drain(self, c):
        for s in range(self.zs):

            @pl.when((s <= self.z) & (self.z < self.zs - 1))
            def _():
                self.up_copy(c, s).wait_send()

            @pl.when((s >= self.z) & (self.z > 0))
            def _():
                self.dn_copy(c, s).wait_send()

            self.sib_copy(c, s).wait_send()


class Reduce:
    def __init__(self, zs, ends, ring, to_sib, r_sib, r_dn, r_up, tmp, out, left, sems):
        self.zs, self.ring, self.to_sib, self.out = zs, ring, to_sib, out
        self.ends, self.left = ends, left
        self.r_sib, self.r_dn, self.r_up = r_sib, r_dn, r_up
        self.tmp_s, self.tmp_d, self.tmp_u = tmp
        self.s_s, self.s_r, self.d_s, self.d_r, self.u_s, self.u_r, self.load, self.o_s, self.l_s = sems
        self.b, self.z = lax.axis_index("batch"), lax.axis_index("z")
        self.slots = ring.shape[0]
        self.size = ring.shape[1] // zs

    def rows(self, h):
        return pl.ds(pl.multiple_of(h * self.size, self.size), self.size)

    def sib(self, c):
        return remote(
            self.to_sib, self.r_sib.at[c], self.s_s.at[c], self.s_r.at[c], {"batch": 1 - self.b}
        )

    def dn(self, c, h):
        src = self.ring.at[lax.rem(c, self.slots), self.rows(h)]
        dst = self.r_dn.at[c, self.rows(h)]
        return remote(src, dst, self.d_s.at[c, h], self.d_r.at[c, h], {"z": self.z - 1})

    def up(self, c, h):
        src = self.ring.at[lax.rem(c, self.slots), self.rows(h)]
        dst = self.r_up.at[c, self.rows(h)]
        return remote(src, dst, self.u_s.at[c, h], self.u_r.at[c, h], {"z": self.z + 1})

    def load_sib(self, c):
        return pltpu.make_async_copy(self.r_sib.at[c], self.tmp_s, self.load.at[0])

    def load_dn(self, c, h):
        rows = self.rows(h)
        return pltpu.make_async_copy(self.r_dn.at[c, rows], self.tmp_d.at[rows], self.load.at[1 + h])

    def load_up(self, c, h):
        rows = self.rows(h)
        return pltpu.make_async_copy(
            self.r_up.at[c, rows], self.tmp_u.at[rows], self.load.at[1 + self.zs + h]
        )

    def arrive(self, c_sib, c_dn, c_up, count):
        @pl.when(in_range(c_sib, count))
        def _():
            self.sib(c_sib).wait_recv()
            self.load_sib(c_sib).start()

        for h in range(self.zs):

            @pl.when(in_range(c_dn, self.ends) & (self.z < self.zs - 1) & (h <= self.z))
            def _():
                self.dn(c_dn, h).wait_recv()
                self.load_dn(c_dn, h).start()

            @pl.when(in_range(c_up, self.ends) & (self.z > 0) & (h >= self.z))
            def _():
                self.up(c_up, h).wait_recv()
                self.load_up(c_up, h).start()

    def add(self, slot, rows, tmp):
        self.ring[slot, rows] = self.ring[slot, rows] + tmp[rows]

    def pass_on(self, c_sib, c_dn, c_up, count):
        @pl.when(in_range(c_sib, count))
        def _():
            self.load_sib(c_sib).wait()
            slot = lax.rem(c_sib, self.slots)
            for h in range(self.zs):
                self.add(slot, pl.ds(h * self.size, self.size), self.tmp_s)
            for h in range(self.zs - 1):

                @pl.when((self.z == self.zs - 1) & (c_sib < self.ends))
                def _():
                    self.dn(c_sib, h).start()

            for h in range(1, self.zs):

                @pl.when((self.z == 0) & (c_sib < self.ends))
                def _():
                    self.up(c_sib, h).start()

            if self.left is not None:

                @pl.when(c_sib >= self.ends)
                def _():
                    self.leave(c_sib).start()

        for h in range(self.zs):

            @pl.when(in_range(c_dn, self.ends) & (self.z < self.zs - 1) & (h <= self.z))
            def _():
                self.load_dn(c_dn, h).wait()
                self.add(lax.rem(c_dn, self.slots), pl.ds(h * self.size, self.size), self.tmp_d)

                @pl.when(h < self.z)
                def _():
                    self.dn(c_dn, h).start()

            @pl.when(in_range(c_up, self.ends) & (self.z > 0) & (h >= self.z))
            def _():
                self.load_up(c_up, h).wait()
                self.add(lax.rem(c_up, self.slots), pl.ds(h * self.size, self.size), self.tmp_u)

                @pl.when(h > self.z)
                def _():
                    self.up(c_up, h).start()

    def leave(self, c):
        src = self.ring.at[lax.rem(c, self.slots)]
        return pltpu.make_async_copy(src, self.left.at[c - self.ends], self.l_s.at[c - self.ends])

    def result(self, c):
        src = self.ring.at[lax.rem(c, self.slots), self.rows(self.z)]
        return pltpu.make_async_copy(src, self.out.at[c], self.o_s.at[0])

    def finish(self, c):
        for h in range(self.zs):

            @pl.when(h < self.z)
            def _():
                self.dn(c, h).wait_send()

            @pl.when(h > self.z)
            def _():
                self.up(c, h).wait_send()

        self.result(c).start()


def mlp_kernel(zs, nc, n1, n2, fc, skip, *refs):
    refs = list(refs)

    def take(count):
        out = refs[:count]
        del refs[:count]
        return out

    if n1:
        mats, full_one = take(3), take(1)[0]
        mine = None
    else:
        (mine,) = take(1)
    h2, dy, dh2_out, y_out, g_out, full, r_sib, r_dn, r_up = take(9)
    left = take(1)[0] if n2 < nc else None
    acc_y, acc_d, h2t, dyt, wbuf, hid_s, dgu_s, ring, to_sib, tmp_s, tmp_d, tmp_u = take(12)
    d_src, d_own, d_one, d_two = take(4)
    w_sem, x_s, x_r, k_s, sq_sem, st_sem = take(6)
    sems = refs
    b, z, x = lax.axis_index("batch"), lax.axis_index("z"), lax.axis_index("x")
    greet(z, zs)
    rest = nc - n1
    lag = 0 if n1 else zs
    ahead = n1 - zs + 1 if n1 else 0
    gather = Gather(zs, mine, full, sems[:6])
    reduce = Reduce(
        zs, n2, ring, to_sib, r_sib, r_dn, r_up, (tmp_s, tmp_d, tmp_u), g_out, left, sems[6:]
    )
    slots = ring.shape[0]
    half = ring.shape[1]
    toks = h2.shape[0]
    part = toks // 4
    square = Square(d_src, d_own, d_one, d_two, Pool(sq_sem))

    if n1:
        trade = Exchange(
            mats, full, n1, zs, skip, [lambda i, r=r: r.at[i] for r in (x_s, x_r, k_s)]
        )
        stage = [ring.at[ring.shape[0] - 1], ring.at[ring.shape[0] - 2]]
        for c in range(rest):
            for side in range(2):
                trade.fetch(c, side, stage[side], st_sem.at[2 * c + side])

        def slices(c):
            rows = pl.ds(c * trade.rows, trade.rows)
            dst = full.at[c, trade.at]
            return (
                pltpu.make_async_copy(stage[0].at[rows], dst, k_s.at[c]),
                remote(stage[1].at[rows], dst, x_s.at[c], x_r.at[c], {"x": 1 - x}),
            )

        for c in range(rest):
            for side in range(2):
                rows = stage[side].at[pl.ds(c * trade.rows, trade.rows)]
                pltpu.make_async_copy(rows, rows, st_sem.at[2 * c + side]).wait()
                slices(c)[side].start()

    def weights(c):
        return pltpu.make_async_copy(full.at[c - n1], wbuf, w_sem.at[0])

    def weights_one(c):
        return pltpu.make_async_copy(full_one.at[c], wbuf, w_sem.at[0])

    if n1:
        weights_one(0).start()
    acc_y[...] = jnp.zeros_like(acc_y)
    acc_d[...] = jnp.zeros_like(acc_d)
    for m in range(4):
        at = slice(m * part, (m + 1) * part)
        h2t[:, at] = h2[at].T
        dyt[:, at] = dy[at].T

    nl = nc - n2

    def keep_slot(c):
        return jnp.maximum(c - n2, 0) if nl else 0

    def compute(c):
        k = keep_slot(c)
        col = lax.broadcasted_iota(jnp.int32, (1, fc), 1) + c * fc
        live = jnp.where((col >= skip) | (x == 0), 1.0, 0.0).astype(F32)
        gate_up = dot(h2[...], wbuf[:, : 2 * fc])
        d_hidden = dot(dy[...], wbuf[:, 2 * fc :]) * live
        gate, up = gate_up[:, :fc], gate_up[:, fc:]
        sig = 1.0 / (1.0 + jnp.exp(-gate))
        silu = gate * sig
        hid_s[k] = (silu * up * live).astype(BF)
        dgu_s[k, :, :fc] = (d_hidden * up * sig * (1.0 + gate * (1.0 - sig))).astype(BF)
        dgu_s[k, :, fc:] = (d_hidden * silu).astype(BF)
        acc_y[...] += dot_nt(hid_s[k], wbuf[:, 2 * fc :])
        acc_d[...] += dot_nt(dgu_s[k], wbuf[:, : 2 * fc])

        @pl.when(c == nc - 1)
        def _():
            for i in range(4):
                d_src[i] = acc_d[i * part : (i + 1) * part].astype(BF)
            square.start()

    def products(c):
        k = keep_slot(c)

        @pl.when(c > 0)
        def _():
            reduce.sib(c - 1).wait_send()

        theirs = pl.ds(pl.multiple_of((1 - b) * half, half), half)
        own = pl.ds(pl.multiple_of(b * half, half), half)
        to_sib[:, : 2 * fc] = dot(h2t[theirs], dgu_s[k]).astype(BF)
        to_sib[:, 2 * fc :] = dot(dyt[theirs], hid_s[k]).astype(BF)
        reduce.sib(c).start()
        slot = lax.rem(c, slots)
        ring[slot, :, : 2 * fc] = dot(h2t[own], dgu_s[k]).astype(BF)
        ring[slot, :, 2 * fc :] = dot(dyt[own], hid_s[k]).astype(BF)

    def begin(i):
        @pl.when(in_range(i, rest))
        def _():
            if n1:
                trade.arrived(i, i)
            gather.start(i)

    def tick(t, carry):
        if n1:
            @pl.when(t == slots - 3)
            def _():
                for c in range(rest):
                    trade.sent(c, c)

        g = t + ahead
        begin(g)
        for k in range(1, zs):

            @pl.when(in_range(g - k, rest))
            def _():
                gather.hop(g - k, k)

        @pl.when(in_range(g - zs, rest))
        def _():
            gather.finish(g - zs)

        c = t - lag
        c_dn = c - 1 - 2 * (zs - 1 - z)
        c_up = c - 1 - 2 * z
        c_end = c - 2 * zs

        def product_at(step):
            late = step - nl
            return jnp.where(
                in_range(step, n2), step, jnp.where((step >= nc) & (late < nc), late, -1)
            )

        c_sib = product_at(c - 1)

        @pl.when(in_range(c - n1, rest))
        def _():
            weights(c).start()

        if n1:

            @pl.when((c > 0) & (c < n1))
            def _():
                weights_one(c).start()

        reduce.arrive(c_sib, c_dn, c_up, nc)
        reduce.pass_on(c_sib, c_dn, c_up, nc)

        @pl.when(in_range(c_end, n2))
        def _():
            reduce.finish(c_end)
            reduce.result(c_end).wait()

        @pl.when(in_range(c, nc))
        def _():
            weights(n1).wait()
            compute(c)

        c_prod = product_at(c)

        @pl.when(c_prod >= 0)
        def _():
            products(c_prod)

        return carry

    for i in range(ahead):
        begin(i)
    lax.fori_loop(0, nc + lag, tick, 0)

    end = max(nc + nl + 1, n2 + 2 * zs) + lag
    turn = min(nc + lag + 3, end)
    lax.fori_loop(nc + lag, turn, tick, 0)
    square.turn()
    for copy in square.first():
        copy.wait_send()
    for i in range(4):
        d_src[i] = acc_y[i * part : (i + 1) * part].astype(BF)
    y_copy = pltpu.make_async_copy(d_src, y_out, w_sem.at[0])
    y_copy.start()
    lax.fori_loop(turn, end, tick, 0)
    dh2_out[...] = square.result()
    for copy in square.second():
        copy.wait_send()
    y_copy.wait()
    reduce.sib(nc - 1).wait_send()
    for c in range(n2, nc):
        reduce.leave(c).wait()

    def drain(c, carry):
        gather.drain(c)
        return carry

    lax.fori_loop(0, rest, drain, 0)


def mlp_call(zs, nc, n1, n2, fc, skip, weights, h2, dy):
    toks, width = h2.shape
    half = width // 2
    slots = min(2 * zs, nc)
    rest = nc - n1
    dma = pltpu.SemaphoreType.DMA
    vm = pltpu.VMEM
    shape = jax.ShapeDtypeStruct
    any_spec = pl.BlockSpec(memory_space=pl.ANY)
    out = [
        shape((toks // 4, width), F32),
        shape((4, toks // 4, width), BF),
        shape((n2, half // zs, 3 * fc), BF),
        shape((rest, width, 3 * fc), BF),
        shape((nc, half, 3 * fc), BF),
        shape((n2, half, 3 * fc), BF),
        shape((n2, half, 3 * fc), BF),
    ]
    if n2 < nc:
        out.append(shape((nc - n2, half, 3 * fc), BF))
    result = pl.pallas_call(
        functools.partial(mlp_kernel, zs, nc, n1, n2, fc, skip),
        out_shape=out,
        in_specs=[any_spec] * len(weights) + [VMEM, VMEM],
        out_specs=[VMEM] + [any_spec] * (len(out) - 1),
        scratch_shapes=[
            vm((toks, width), F32),
            vm((toks, width), F32),
            vm((width, toks), BF),
            vm((width, toks), BF),
            vm((width, 3 * fc), BF),
            vm((max(nc - n2, 1), toks, fc), BF),
            vm((max(nc - n2, 1), toks, 2 * fc), BF),
            vm((slots, half, 3 * fc), BF),
            vm((half, 3 * fc), BF),
            vm((half, 3 * fc), BF),
            vm((half, 3 * fc), BF),
            vm((half, 3 * fc), BF),
            vm((4, toks // 4, width), BF),
            vm((4, toks // 4, half), BF),
            vm((4, toks // 4, half), BF),
            vm((2, toks // 4, half), BF),
            dma((1,)),
        ]
        + [dma((rest,))] * 3
        + [dma((13,)), dma((2 * rest,)), dma((rest,))]
        + [dma((rest, zs))] * 5
        + [dma((nc,))] * 2
        + [dma((nc, zs))] * 4
        + [dma((1 + 2 * zs,)), dma((1,)), dma((nc,))],
        compiler_params=pltpu.CompilerParams(
            collective_id=0, has_side_effects=True, vmem_limit_bytes=62 * 2**20
        ),
        cost_estimate=pl.CostEstimate(
            flops=18 * toks * width * fc * nc, bytes_accessed=80 * 2**20, transcendentals=0
        ),
    )(*weights, h2, dy)
    return list(result[:3]) + list(result[7:])


def final_kernel(skip, *refs):
    refs = list(refs)
    inputs = refs[:8]
    d_hidden, g_query, g_key, g_value, g_out, g_gate, g_up, g_down, output = refs[8:17]
    bufs, sem = refs[17:24] + [output], refs[24]
    x = lax.axis_index("x")
    copies = [
        pltpu.make_async_copy(src, dst, sem.at[i])
        for i, (src, dst) in enumerate(zip(inputs, bufs))
    ]
    for copy in copies:
        copy.start()
    near, left, far, gh, s_q, s_kv, s_wo, _ = bufs
    n2, nl = near.shape[0], left.shape[0]
    half = gh.shape[1]
    fc = far.shape[2] // 3
    split = (n2 + nl) * fc
    for i in (0, 2, 1):
        copies[i].wait()
    for c in range(n2 + nl):
        own = (near[c, x] if c < n2 else left[c - n2]).astype(F32)
        other = far[c].astype(F32)
        low = jnp.where(x == 0, own, other)
        high = jnp.where(x == 0, other, own)
        for w, out in enumerate((g_gate, g_up, g_down)):
            b = high[:, w * fc : (w + 1) * fc]
            first = split - skip + c * fc
            if c == 0:
                b = b[:, skip:]
                first = split
            out[:, c * fc : (c + 1) * fc] = low[:, w * fc : (w + 1) * fc]
            out[:, first : first + b.shape[1]] = b
    for i in (3, 4, 5, 6):
        copies[i].wait()
    for i in range(2):
        d_hidden[i * half : (i + 1) * half] = gh[i].astype(F32)
    g_query[...] = s_q[...].astype(F32)
    g_key[...] = s_kv[:, :HEAD_SIZE].astype(F32)
    g_value[...] = s_kv[:, HEAD_SIZE:].astype(F32)
    g_out[...] = s_wo[...].astype(F32)
    copies[7].wait()


def final_call(skip, ff, inputs):
    rows, three = inputs[2].shape[1:]
    _, half, width = inputs[3].shape
    q_cols = inputs[4].shape[1]
    shape = jax.ShapeDtypeStruct
    any_spec = pl.BlockSpec(memory_space=pl.ANY)
    out = [
        shape((2 * half, width), F32),
        shape((rows, q_cols), F32),
        shape((rows, HEAD_SIZE), F32),
        shape((rows, HEAD_SIZE), F32),
        shape((rows, q_cols), F32),
        shape((rows, ff), F32),
        shape((rows, ff), F32),
        shape((rows, ff), F32),
        shape(inputs[7].shape, BF),
    ]
    return pl.pallas_call(
        functools.partial(final_kernel, skip),
        out_shape=out,
        in_specs=[any_spec] * len(inputs),
        out_specs=[VMEM] * 9,
        scratch_shapes=[pltpu.VMEM(v.shape, BF) for v in inputs[:7]]
        + [pltpu.SemaphoreType.DMA((8,))],
        compiler_params=pltpu.CompilerParams(vmem_limit_bytes=60 * 2**20),
    )(*inputs)


def on_device(
    hidden,
    lengths,
    norm_attn,
    w_query,
    key_weight_matrix,
    value_weight_matrix,
    b_query,
    key_bias_rows,
    value_bias_rows,
    w_out,
    norm_mlp,
    w_gate,
    w_up,
    w_down,
    cotangent,
):
    homes = lax.axis_size("batch") * lax.axis_size("z") * lax.axis_size("x")
    shards = lax.axis_size("z") * lax.axis_size("x")
    z_i, x_i = lax.axis_index("z"), lax.axis_index("x")
    me = z_i * lax.axis_size("x") + x_i
    tok = hidden.shape[1]
    width = hidden.shape[2]
    half = tok // 2
    doc_lengths = lengths[0]
    heads = b_query.shape[0]
    heads_all = heads + 2
    q_cols = heads * HEAD_SIZE
    rows = norm_attn.shape[0]
    ff = w_gate.shape[1]
    ffh = -(-ff // 512) * 256
    fc = FC
    nc = ffh // fc

    home = (lax.axis_index("batch") * lax.axis_size("z") + z_i) * 2 + x_i
    per_home = HEAD_SIZE // homes

    def spot(value):
        here = jnp.arange(homes, dtype=jnp.int32)[None, :, None] == home
        return jnp.where(here, value[:, None, :], 0).reshape(-1)

    biases = jnp.concatenate([b_query, key_bias_rows, value_bias_rows], axis=0)
    small = jnp.concatenate(
        [spot(biases), spot(norm_attn[None]), spot(norm_mlp[None])]
    ).reshape(16, -1)

    zs = lax.axis_size("z")
    n1, n2 = (zs, nc - zs) if rows % 16 == 0 and 2 * zs < nc else (0, nc)
    three = (w_gate, w_up, w_down.T)
    skip = 2 * ffh - ff

    stored = me * tok + jnp.arange(tok, dtype=jnp.int32)
    q_rows = row_positions(stored, shards, half)
    doc_start = doc_starts_of(q_rows, doc_lengths)
    cosine_table, sine_table = rotary(q_rows - doc_start, HEAD_SIZE)
    cos2 = jnp.concatenate([cosine_table, cosine_table], axis=1)
    sin2 = jnp.concatenate([-sine_table, sine_table], axis=1)
    start_row = doc_start[None, :]

    x_in = hidden[0]
    (
        h_first,
        q_mat,
        out_low,
        lse,
        mid,
        vec,
        wkv,
        wq,
        wo_t,
        kv_all,
        h2,
        dy,
        *full_one,
    ) = forward_call(
        zs,
        heads,
        n1,
        skip,
        fc,
        x_in,
        jnp.concatenate([key_weight_matrix, value_weight_matrix], axis=1),
        w_query,
        w_out.T,
        small,
        cos2,
        sin2,
        start_row,
        cotangent[0].reshape(2, half, width),
        three if n1 else (),
    )
    h2 = h2.reshape(4 * half, width)
    dy = dy.reshape(4 * half, width)
    if n1:
        mlp_w = (*three, *full_one)
    else:

        def stacked(x_at):
            halves = [
                lax.dynamic_slice_in_dim(mat, x_at * (ff - ffh), ffh, axis=1).reshape(rows, nc, fc)
                for mat in three
            ]
            return jnp.transpose(jnp.concatenate(halves, axis=2), (1, 0, 2))

        keep = stacked(x_i)
        other = lax.ppermute(stacked(1 - x_i), "x", [(0, 1), (1, 0)])
        low = jnp.where(x_i == 0, keep, other)
        high = jnp.where(x_i == 0, other, keep)
        mlp_w = (jnp.concatenate([low, high], axis=1),)
    dh2, y_sum, mlp_g, *left = mlp_call(zs, nc, n1, n2, fc, skip, mlp_w, h2, dy)
    mlp_g = mlp_g.reshape(n2, 2, rows, 3 * fc)
    left = [v.reshape(nc - n2, zs, 2 * rows, 3 * fc) for v in left]

    output, d_hidden, s_q, s_kv, s_wo, g_vec, other, *left_own = backward_call(
        zs,
        heads,
        left,
        (y_sum, mlp_g, x_in, cotangent[0]),
        (
            dh2,
            mid,
            vec,
            h_first,
            q_mat,
            out_low,
            lse[:, None],
            kv_all,
            wkv,
            wq,
            wo_t,
            cos2,
            sin2,
            start_row.reshape(2, 1, half),
        ),
    )
    g_vec = g_vec.reshape(-1)
    g_bias = lax.dynamic_slice_in_dim(
        g_vec[: heads_all * HEAD_SIZE].reshape(heads_all, HEAD_SIZE), home * per_home, per_home, 1
    )
    g_norms = g_vec[heads_all * HEAD_SIZE :].reshape(2, width)
    g_norms = lax.dynamic_slice_in_dim(g_norms, home * rows, rows, 1)

    if n1:
        grads = final_call(skip, ff, (mlp_g, *left_own, other, d_hidden, s_q, s_kv, s_wo, output))
    else:
        keep = lax.dynamic_index_in_dim(mlp_g, x_i, 1, False)
        low = jnp.where(x_i == 0, keep, other)
        high = jnp.where(x_i == 0, other, keep)

        def whole(k):
            def cols(value):
                piece = value[:, :, k * fc : (k + 1) * fc]
                return jnp.transpose(piece, (1, 0, 2)).reshape(rows, ffh)

            return jnp.concatenate([cols(low), cols(high)[:, skip:]], axis=1).astype(F32)

        grads = (
            d_hidden.astype(F32).reshape(tok, width),
            s_q.astype(F32),
            s_kv[:, :HEAD_SIZE].astype(F32),
            s_kv[:, HEAD_SIZE:].astype(F32),
            s_wo.astype(F32),
            whole(0),
            whole(1),
            whole(2),
            output,
        )
    d_hidden, g_query, g_key, g_value, g_out, g_gate, g_up, g_down, output = grads
    return (
        output.reshape(1, tok, width),
        d_hidden[None],
        g_norms[0],
        g_query,
        g_key,
        g_value,
        g_bias[:heads],
        g_bias[heads : heads + 1],
        g_bias[heads + 1 :],
        g_out.T,
        g_norms[1],
        g_gate,
        g_up,
        g_down.T,
    )


def solution(mesh):
    seq = mesh.shape["seq"]
    fine = Mesh(
        mesh.devices.reshape(mesh.shape["batch"], seq // 2, 2, mesh.shape["tensor"]),
        ("batch", "z", "x", "tensor"),
    )
    toks = P("batch", ("z", "x"), None)
    home = ("batch", "z", "x")
    down = P(home, "tensor")
    across = P("tensor", home)
    return jax.shard_map(
        on_device,
        mesh=fine,
        in_specs=(
            toks,
            P("batch", None),
            P(home),
            down,
            down,
            down,
            across,
            across,
            across,
            across,
            P(home),
            down,
            down,
            across,
            toks,
        ),
        out_specs=(
            toks,
            toks,
            P(home),
            down,
            down,
            down,
            across,
            across,
            across,
            across,
            P(home),
            down,
            down,
            across,
        ),
        check_vma=False,
    )
```

```python
import functools

import jax
import jax.numpy as jnp
from jax import lax
from jax.experimental import pallas as pl
from jax.experimental.pallas import tpu as pltpu
from jax.sharding import Mesh
from jax.sharding import PartitionSpec as P

HEAD_SIZE = 128
NORM_EPS = 1e-06
ROPE_BASE = 10000.0
MASKED = -1e30
FLOOR = -1e29
FC = 256
BF = jnp.bfloat16
F32 = jnp.float32
VMEM = pl.BlockSpec(memory_space=pltpu.VMEM)


def row_positions(stored, shards, half_rows):
    slot_id = stored // half_rows
    inner = stored % half_rows
    shard_id = slot_id // 2
    row_block = jnp.where(slot_id % 2 == 0, shard_id, 2 * shards - 1 - shard_id)
    return row_block * half_rows + inner


def doc_starts_of(row_pos, doc_lengths):
    doc_ends = jnp.cumsum(doc_lengths)
    doc_starts = doc_ends - doc_lengths
    inside = (row_pos[:, None] >= doc_starts[None, :]) & (row_pos[:, None] < doc_ends[None, :])
    return jnp.sum(jnp.where(inside, doc_starts[None, :], 0), axis=1).astype(jnp.int32)


def rotary(doc_pos, head_dim):
    half_dim = head_dim // 2
    freqs = ROPE_BASE ** (-2.0 * jnp.arange(half_dim, dtype=jnp.float32) / head_dim)
    angles = doc_pos.astype(jnp.float32)[:, None] * freqs[None, :]
    return (jnp.cos(angles), jnp.sin(angles))


def norm_factor(resid):
    return lax.rsqrt(jnp.mean(resid * resid, axis=-1, keepdims=True) + NORM_EPS)


def norm_backward(resid, factor, gain, grad_in):
    weighted = grad_in * gain
    grad_resid = factor * weighted - resid * factor**3 * jnp.mean(
        weighted * resid, axis=-1, keepdims=True
    )
    grad_gain = jnp.sum(grad_in * resid * factor, axis=0, keepdims=True)
    return (grad_resid, grad_gain)


def dot(a, b):
    return jnp.dot(a, b, preferred_element_type=F32)


def dot_nt(a, b):
    return lax.dot_general(a, b, (((1,), (1,)), ((), ())), preferred_element_type=F32)


def block_mask(sub, block, me, shards, half, start_row, heads):
    key_blk = jnp.where(sub == 0, block, 2 * shards - 1 - block)
    query_blk = jnp.where(sub == 0, me, 2 * shards - 1 - me)
    key_pos = key_blk * half + lax.broadcasted_iota(jnp.int32, (half, half), 0)
    query_pos = query_blk * half + lax.broadcasted_iota(jnp.int32, (half, half), 1)
    allowed = (key_pos <= query_pos) & (key_pos >= start_row)
    return jnp.concatenate([jnp.where(allowed, 0.0, MASKED).astype(F32)] * heads, axis=1)


def stack_heads(ref, sub, half, heads):
    return jnp.concatenate(
        [
            ref[sub * half : (sub + 1) * half, h * HEAD_SIZE : (h + 1) * HEAD_SIZE]
            for h in range(heads)
        ],
        axis=0,
    )


class Pool:
    def __init__(self, ref):
        self.ref, self.used = ref, 0

    def take(self, count=1):
        base = self.used
        self.used += count
        assert self.used <= self.ref.shape[0], self.used
        return lambda i=0: self.ref.at[base + i]


def merge_rows(value):
    homes, rows, cols = value.shape
    if rows % 16:
        return value.astype(F32).reshape(homes * rows, cols).astype(BF)
    return value.reshape(homes * rows, cols)


class Spread:
    def __init__(self, zs, src, buf, pool):
        self.zs, self.src, self.buf = zs, src, buf
        self.b, self.z, self.x = (lax.axis_index(a) for a in ("batch", "z", "x"))
        self.up_s, self.dn_s, self.z_r, self.x_s, self.x_r = (pool.take(zs) for _ in range(5))
        self.s_s, self.s_r = pool.take(2 * zs), pool.take(2 * zs)
        self.loc = pool.take()

    def at(self, b, z, x):
        return self.buf.at[(b * self.zs + z) * 2 + x]

    def up(self, s, src=None):
        dst = self.at(self.b, s, self.x)
        src = dst if src is None else src
        return remote(src, dst, self.up_s(s), self.z_r(s), {"z": self.z + 1})

    def dn(self, s, src=None):
        dst = self.at(self.b, s, self.x)
        src = dst if src is None else src
        return remote(src, dst, self.dn_s(s), self.z_r(s), {"z": self.z - 1})

    def side(self, s, src=None):
        dst = self.at(self.b, s, self.x)
        src = dst if src is None else src
        return remote(src, dst, self.x_s(s), self.x_r(s), {"x": 1 - self.x})

    def sib(self, s, far=0, src=None):
        dst = self.at(self.b, s, self.x if far == 0 else 1 - self.x)
        src = dst if src is None else src
        i = far * self.zs + s
        return remote(src, dst, self.s_s(i), self.s_r(i), {"batch": 1 - self.b})

    def local(self):
        return pltpu.make_async_copy(self.src, self.at(self.b, self.z, self.x), self.loc())

    def start(self):
        @pl.when(self.z < self.zs - 1)
        def _():
            self.up(self.z, self.src).start()

        @pl.when(self.z > 0)
        def _():
            self.dn(self.z, self.src).start()

        self.side(self.z, self.src).start()
        self.sib(self.z, 0, self.src).start()
        self.local().start()

    def hop(self, k):
        low, high = self.z - k, self.z + k

        @pl.when(low >= 0)
        def _():
            self.dn(low).wait_recv()

            @pl.when(self.z < self.zs - 1)
            def _():
                self.up(low).start()

            self.side(low).start()
            self.sib(low).start()

        @pl.when(high < self.zs)
        def _():
            self.dn(high).wait_recv()

            @pl.when(self.z > 0)
            def _():
                self.dn(high).start()

            self.side(high).start()
            self.sib(high).start()

    def cross(self):
        for s in range(self.zs):
            dst = self.at(self.b, s, 1 - self.x)
            remote(dst, dst, self.x_s(s), self.x_r(s), {"x": 1 - self.x}).wait_recv()
            self.sib(s, 1).start()

    def finish(self):
        self.local().wait()
        for far in range(2):
            for s in range(self.zs):
                dst = self.at(1 - self.b, s, self.x if far == 0 else 1 - self.x)
                i = far * self.zs + s
                remote(dst, dst, self.s_s(i), self.s_r(i), {"batch": 1 - self.b}).wait_recv()

    def drain(self):
        for s in range(self.zs):

            @pl.when((s <= self.z) & (self.z < self.zs - 1))
            def _():
                self.up(s).wait_send()

            @pl.when((s >= self.z) & (self.z > 0))
            def _():
                self.dn(s).wait_send()

            self.side(s).wait_send()
            self.sib(s, 0).wait_send()
            self.sib(s, 1).wait_send()


def lanes(vec, first, count):
    return jnp.concatenate([vec[r : r + 1, :] for r in range(first, first + count)], axis=1)


def thirds(zs):
    hops = list(range(1, zs))
    per = -(-len(hops) // 3)
    return [hops[i * per : (i + 1) * per] for i in range(3)]


def forward_kernel(
    zs,
    heads,
    n1,
    skip,
    scale,
    x_ref,
    wkv_in,
    wq_in,
    wo_in,
    small_in,
    cos_ref,
    sin_ref,
    start_ref,
    dy_in,
    *refs,
):
    refs = list(refs)
    if n1:
        mats = refs[:3]
        del refs[:3]
    h1_out, q_out, attn_out, lse_out, mid_out, vec_out = refs[:6]
    wkv_all, wq_all, wo_all, kv_all, h2_all, dy_all = refs[6:12]
    del refs[:12]
    if n1:
        full = refs.pop(0)
    small_buf, wkv_buf, wq_buf, wo_buf, kv_buf, q_t, acc_ref, max_ref, sum_ref = refs[:9]
    att_send, att_recv, h2_half, xn_ref, sem_ref = refs[9:14]
    g_sems = refs[14:]
    b, z, x, t = (lax.axis_index(a) for a in ("batch", "z", "x", "tensor"))
    shards = 2 * zs
    me = 2 * z + x
    tok, width = x_ref.shape
    half = tok // 2
    q_cols = heads * HEAD_SIZE
    pool = Pool(sem_ref)
    greet(z, zs)

    small = Spread(zs, small_in, small_buf, pool)
    wkv = Spread(zs, wkv_in, wkv_buf, pool)
    wq = Spread(zs, wq_in, wq_buf, pool)
    wo = Spread(zs, wo_in, wo_buf, pool)
    small.start()
    wkv.start()
    wq.start()

    runs = thirds(zs)
    if n1:
        trade = Exchange(mats, full, 0, zs, skip, [pool.take(n1) for _ in range(3)])
        gather = Gather(zs, None, full, [None] + list(g_sems))
        for c in range(n1):
            trade.keep(c, c)

    def ship(first, last):
        if n1:
            for c in range(first, last):
                trade.ship(c, c)

    def prefetch(tick):
        if n1:
            for c in range(n1):
                hops = [k for k in range(1, zs) if min(k, 3) == tick - c]
                if tick == c:
                    trade.arrived(c, c)
                    gather.start(c)
                for k in hops:
                    gather.hop(c, k)

    quarter = half // 2
    dy_l, dyy_s, dyy_r = (pool.take() for _ in range(3))
    dyx_s, dyx_r = pool.take(3), pool.take(3)
    dy_own = pltpu.make_async_copy(dy_in, dy_all.at[pl.ds(2 * x, 2)], dy_l())
    dy_own.start()

    def dy_side(i):
        rows = pl.ds((i % 3 > 0) * quarter, quarter)
        block = t if i < 2 else 1 - t
        dst = dy_all.at[2 * x + block, rows]
        return remote(dy_in.at[block, rows], dst, dyx_s(i), dyx_r(i), {"x": 1 - x})

    dy_piece = dy_all.at[2 * (1 - x) + t, pl.ds(0, quarter)]
    dy_across = remote(dy_piece, dy_piece, dyy_s(), dyy_r(), {"tensor": 1 - t})

    for m in range(2):
        at = slice(m * half, (m + 1) * half)
        xv = x_ref[at].astype(F32)
        xn_ref[at] = xv * norm_factor(xv)
    for k in range(1, zs):
        small.hop(k)
        wkv.hop(k)
        if k == 1:
            ship(0, 1)
    for k in runs[0]:
        wq.hop(k)
    wo.start()
    prefetch(0)
    small.cross()
    small.finish()
    vec = jnp.sum(small_buf[...].astype(F32), axis=0)
    vec_out[...] = vec
    bias = lanes(vec, 0, 4)
    gain_attn = lanes(vec, 4, 6)
    gain_mlp = lanes(vec, 10, 6)
    for m in range(2):
        at = slice(m * half, (m + 1) * half)
        h1_out[at] = (xn_ref[at] * gain_attn).astype(BF)

    def turned(value, at):
        return value * cos_ref[at] + pltpu.roll(value, HEAD_SIZE // 2, 1) * sin_ref[at]

    wkv.cross()
    ship(1, 2)
    wkv.finish()
    for k in runs[1]:
        wq.hop(k)
    wkv_m = merge_rows(wkv_buf[...])
    for m in range(2):
        at = slice(m * half, (m + 1) * half)
        lin = dot(h1_out[at], wkv_m) + bias[:, q_cols:]
        kv_buf[me + m, :, :HEAD_SIZE] = turned(lin[:, :HEAD_SIZE], at).astype(BF)
        kv_buf[me + m, :, HEAD_SIZE:] = lin[:, HEAD_SIZE:].astype(BF)

    ku_s, kd_s, k0_r, k1_r, x0_s, x1_s, x0_r, x1_r = (pool.take(zs) for _ in range(8))

    def kv_up(s):
        piece = kv_buf.at[2 * s + x]
        return remote(piece, piece, ku_s(s), k0_r(s), {"z": z + 1})

    def kv_dn(s):
        piece = kv_buf.at[2 * s + x + 1]
        return remote(piece, piece, kd_s(s), k1_r(s), {"z": z - 1})

    def kv_side(s, sub, col):
        piece = kv_buf.at[2 * s + col + sub]
        send, recv = (x0_s, x0_r) if sub == 0 else (x1_s, x1_r)
        return remote(piece, piece, send(s), recv(s), {"x": 1 - x})

    def kv_hop(k):
        low, high = z - k, z + k

        @pl.when(low >= 0)
        def _():
            kv_up(low).wait_recv()

            @pl.when(z < zs - 1)
            def _():
                kv_up(low).start()

            kv_side(low, 0, x).start()

        @pl.when(high < zs)
        def _():
            kv_dn(high).wait_recv()

            @pl.when(z > 0)
            def _():
                kv_dn(high).start()

            kv_side(high, 1, x).start()

    @pl.when(z < zs - 1)
    def _():
        kv_up(z).start()

    @pl.when(z > 0)
    def _():
        kv_dn(z).start()

    @pl.when(x == 0)
    def _():
        kv_side(z, 0, x).start()

    @pl.when(x == 1)
    def _():
        kv_side(z, 1, x).start()

    for k in runs[2]:
        wq.hop(k)
    for k in runs[0]:
        wo.hop(k)
    for k in runs[0]:
        kv_hop(k)
    wq.cross()
    for k in runs[1]:
        kv_hop(k)
    for k in runs[1]:
        wo.hop(k)
    ship(2, 3)
    prefetch(1)
    wq.finish()
    wq_m = merge_rows(wq_buf[...])
    for m in range(2):
        at = slice(m * half, (m + 1) * half)
        lin = dot(h1_out[at], wq_m) + bias[:, :q_cols]
        for h in range(heads):
            cols = slice(h * HEAD_SIZE, (h + 1) * HEAD_SIZE)
            q_out[at, cols] = turned(lin[:, cols], at).astype(BF)
    for sub in range(2):
        q_t[sub] = stack_heads(q_out, sub, half, heads).T
    acc_ref[...] = jnp.zeros_like(acc_ref)
    max_ref[...] = jnp.full_like(max_ref, FLOOR)
    sum_ref[...] = jnp.zeros_like(sum_ref)

    def fold(sub, block):
        keys = kv_buf[block + sub, :, :HEAD_SIZE]
        vals = kv_buf[block + sub, :, HEAD_SIZE:]
        start_row = start_ref[:, sub * half : (sub + 1) * half]
        scores = dot(keys, q_t[sub]) * scale + block_mask(
            sub, block, me, shards, half, start_row, heads
        )
        old_max = max_ref[sub]
        new_max = jnp.maximum(old_max, jnp.max(scores, axis=0, keepdims=True))
        weights = jnp.exp(scores - new_max)
        shrink = jnp.exp(old_max - new_max)
        max_ref[sub] = new_max
        sum_ref[sub] = sum_ref[sub] * shrink + jnp.sum(weights, axis=0, keepdims=True)
        acc_ref[sub] = acc_ref[sub] * shrink + dot(vals.T, weights.astype(BF))

    def attend(k, carry):
        low, high = z - k, z + k

        @pl.when((low >= 0) & (k < zs))
        def _():
            fold(0, 2 * low + x)

        @pl.when((high < zs) & (k < zs))
        def _():
            fold(1, 2 * high + x)

        far_low, far_high = low + 1, high - 1

        @pl.when((k > 0) & (far_low >= 0) & ((k > 1) | (x == 1)))
        def _():
            kv_side(far_low, 0, 1 - x).wait_recv()
            fold(0, 2 * far_low + 1 - x)

        @pl.when((k > 0) & (far_high < zs) & ((k > 1) | (x == 0)))
        def _():
            kv_side(far_high, 1, 1 - x).wait_recv()
            fold(1, 2 * far_high + 1 - x)

        @pl.when(k == 0)
        def _():
            for hop in runs[2]:
                kv_hop(hop)

        @pl.when(k == 1)
        def _():
            for hop in runs[2]:
                wo.hop(hop)

        @pl.when(k == 2)
        def _():
            dy_side(1).start()

        @pl.when(k == zs - 1)
        def _():
            prefetch(2)

        return carry

    lax.fori_loop(0, zs + 1, attend, 0)
    dy_side(0).start()
    ship(3, n1)
    wo.cross()
    for sub in range(2):
        lse_out[sub : sub + 1, :] = max_ref[sub] + jnp.log(sum_ref[sub])
        out_t = acc_ref[sub] / sum_ref[sub]
        for h in range(heads):
            attn_out[sub * half : (sub + 1) * half, h * HEAD_SIZE : (h + 1) * HEAD_SIZE] = (
                out_t[:, h * half : (h + 1) * half].T.astype(BF)
            )

    wo.finish()
    att_s, att_r = pool.take(2), pool.take(2)
    h_l, hx_s, hx_r, hy_s, hy_r = (pool.take(2) for _ in range(5))
    hxx_s, hxx_r, hyy_s, hyy_r = (pool.take() for _ in range(4))

    def rows(i):
        return pl.ds(i * quarter, quarter)

    def att_copy(i):
        to = {"tensor": 1 - t}
        return remote(att_send.at[rows(i)], att_recv.at[rows(i)], att_s(i), att_r(i), to)

    def h_copies(i):
        src, dst = h2_half.at[rows(i)], h2_all.at[2 * x + t, rows(i)]
        return (
            pltpu.make_async_copy(src, dst, h_l(i)),
            remote(src, dst, hx_s(i), hx_r(i), {"x": 1 - x}),
            remote(src, dst, hy_s(i), hy_r(i), {"tensor": 1 - t}),
        )

    wo_m = merge_rows(wo_buf[...])
    for i in range(2):
        at = pl.ds(pl.multiple_of((1 - t) * half + i * quarter, quarter), quarter)
        att_send[rows(i)] = dot_nt(attn_out[at], wo_m).astype(BF)
        att_copy(i).start()
    for i in range(2):
        at = pl.ds(pl.multiple_of(t * half + i * quarter, quarter), quarter)
        mid_out[rows(i)] = dot_nt(attn_out[at], wo_m) + x_ref[at].astype(F32)
    prefetch(3)
    for i in range(2):
        att_copy(i).wait_recv()
        mid = mid_out[rows(i)] + att_recv[rows(i)].astype(F32)
        mid_out[rows(i)] = mid
        h2_half[rows(i)] = (mid * norm_factor(mid) * gain_mlp).astype(BF)
        for copy in h_copies(i):
            copy.start()
    from_side = h2_all.at[2 * (1 - x) + t, rows(0)]
    from_across = h2_all.at[2 * x + 1 - t, rows(1)]
    relay_across = remote(from_side, from_side, hyy_s(), hyy_r(), {"tensor": 1 - t})
    relay_side = remote(from_across, from_across, hxx_s(), hxx_r(), {"x": 1 - x})
    dy_side(2).start()
    h_copies(0)[1].wait_recv()
    relay_across.start()
    prefetch(4)
    h_copies(1)[2].wait_recv()
    relay_side.start()
    dy_side(0).wait_recv()
    dy_across.start()
    for tick in range(5, n1 + 3):
        prefetch(tick)

    save = pool.take(4)
    saves = [
        pltpu.make_async_copy(src, dst, save(i))
        for i, (src, dst) in enumerate(
            ((wkv_buf, wkv_all), (wq_buf, wq_all), (wo_buf, wo_all), (kv_buf, kv_all))
        )
    ]
    for copy in saves:
        copy.start()

    for item in (small, wkv, wq, wo):
        item.drain()

    def kv_drain(s, carry):
        @pl.when((s <= z) & (z < zs - 1))
        def _():
            kv_up(s).wait_send()

        @pl.when((s >= z) & (z > 0))
        def _():
            kv_dn(s).wait_send()

        @pl.when((s < z) | ((s == z) & (x == 0)))
        def _():
            kv_side(s, 0, x).wait_send()

        @pl.when((s > z) | ((s == z) & (x == 1)))
        def _():
            kv_side(s, 1, x).wait_send()

        return carry

    lax.fori_loop(0, zs, kv_drain, 0)
    relay_across.wait()
    relay_side.wait()
    dy_across.wait()
    for i in range(3):
        dy_side(i).wait_send()
        if i > 0:
            dy_side(i).wait_recv()
    for i in range(2):
        att_copy(i).wait_send()
        own, side, across = h_copies(i)
        own.wait()
        side.wait_send()
        across.wait_send()
    h_copies(1)[1].wait_recv()
    h_copies(0)[2].wait_recv()
    if n1:
        for c in range(n1):
            trade.sent(c, c)
            gather.finish(c)
            gather.drain(c)
    for copy in saves + [dy_own]:
        copy.wait()


def forward_call(
    zs, heads, n1, skip, fc, x_in, wkv_in, wq_in, wo_in, small_in, cos, sin, start, dy_in, first
):
    tok, width = x_in.shape
    half = tok // 2
    homes = 4 * zs
    rows, q_cols = wq_in.shape
    shape = jax.ShapeDtypeStruct
    any_spec = pl.BlockSpec(memory_space=pl.ANY)
    out = [
        shape((tok, width), BF),
        shape((tok, q_cols), BF),
        shape((tok, q_cols), BF),
        shape((2, heads * half), F32),
        shape((half, width), F32),
        shape(small_in.shape, F32),
        shape((homes, rows, 2 * HEAD_SIZE), BF),
        shape((homes, rows, q_cols), BF),
        shape((homes, rows, q_cols), BF),
        shape((2 * zs + 1, half, 2 * HEAD_SIZE), BF),
        shape((4, half, width), BF),
        shape((4, half, width), BF),
    ]
    sems = [pltpu.SemaphoreType.DMA((4 * (9 * zs + 1) + 8 * zs + 3 * n1 + 40,))]
    if n1:
        out.append(shape((n1, width, 3 * fc), BF))
        sems += [pltpu.SemaphoreType.DMA((n1, zs))] * 5
    return pl.pallas_call(
        functools.partial(forward_kernel, zs, heads, n1, skip, HEAD_SIZE ** (-0.5)),
        out_shape=out,
        in_specs=[VMEM] + [any_spec] * 4 + [VMEM] * (4 + len(first)),
        out_specs=[VMEM] * 6 + [any_spec] * (len(out) - 6),
        scratch_shapes=[
            pltpu.VMEM((homes,) + small_in.shape, BF),
            pltpu.VMEM((homes, rows, 2 * HEAD_SIZE), BF),
            pltpu.VMEM((homes, rows, q_cols), BF),
            pltpu.VMEM((homes, rows, q_cols), BF),
            pltpu.VMEM((2 * zs + 1, half, 2 * HEAD_SIZE), BF),
            pltpu.VMEM((2, HEAD_SIZE, heads * half), BF),
            pltpu.VMEM((2, HEAD_SIZE, heads * half), F32),
            pltpu.VMEM((2, 1, heads * half), F32),
            pltpu.VMEM((2, 1, heads * half), F32),
            pltpu.VMEM((half, width), BF),
            pltpu.VMEM((half, width), BF),
            pltpu.VMEM((half, width), BF),
            pltpu.VMEM((tok, width), F32),
        ]
        + sems,
        compiler_params=pltpu.CompilerParams(
            collective_id=1, has_side_effects=True, vmem_limit_bytes=60 * 2**20
        ),
        cost_estimate=pl.CostEstimate(
            flops=4 * tok * width * (q_cols + HEAD_SIZE) + 2**31,
            bytes_accessed=32 * 2**20,
            transcendentals=0,
        ),
    )(x_in, wkv_in, wq_in, wo_in, small_in, cos, sin, start, dy_in, *first)


class Square:
    def __init__(self, src, own, r_one, r_two, pool):
        self.src, self.own, self.r_one, self.r_two = src, own, r_one, r_two
        self.x, self.t = lax.axis_index("x"), lax.axis_index("tensor")
        self.cut = src.shape[2] // 2
        self.one_s, self.one_r = pool.take(3), pool.take(3)
        self.two_s, self.two_r = pool.take(2), pool.take(2)
        self.load = pool.take(3)

    def first(self):
        x, t, cut, src = self.x, self.t, self.cut, self.src
        left, right = pl.ds(0, cut), pl.ds(cut, cut)
        sends = [
            remote(
                src.at[pl.ds(2 * (1 - x), 2), :, left],
                self.r_one.at[pl.ds(0, 2)],
                self.one_s(0),
                self.one_r(0),
                {"x": 1 - x},
            )
        ]
        for i in range(2):
            sends.append(
                remote(
                    src.at[2 * i + 1 - t, :, right],
                    self.r_one.at[2 + i],
                    self.one_s(1 + i),
                    self.one_r(1 + i),
                    {"tensor": 1 - t},
                )
            )
        return sends

    def loads(self):
        x, t, cut, src = self.x, self.t, self.cut, self.src
        left, right = pl.ds(0, cut), pl.ds(cut, cut)
        loads = [
            pltpu.make_async_copy(
                src.at[pl.ds(2 * x, 2), :, left], self.own.at[pl.ds(0, 2)], self.load(0)
            )
        ]
        for i in range(2):
            loads.append(
                pltpu.make_async_copy(
                    src.at[2 * i + t, :, right], self.own.at[2 + i], self.load(1 + i)
                )
            )
        return loads

    def second(self):
        x, t = self.x, self.t
        return [
            remote(
                self.own.at[1 - t],
                self.r_two.at[0],
                self.two_s(0),
                self.two_r(0),
                {"tensor": 1 - t},
            ),
            remote(
                self.own.at[3 - x],
                self.r_two.at[1],
                self.two_s(1),
                self.two_r(1),
                {"x": 1 - x},
            ),
        ]

    def start(self):
        for copy in self.first() + self.loads():
            copy.start()

    def turn(self):
        for copy in self.loads():
            copy.wait()
        for copy in self.first():
            copy.wait_recv()
        for i in range(4):
            self.own[i] = self.own[i] + self.r_one[i]
        for copy in self.second():
            copy.start()

    def result(self):
        for copy in self.second():
            copy.wait_recv()
        left = self.own[self.t].astype(F32) + self.r_two[0].astype(F32)
        right = self.own[2 + self.x].astype(F32) + self.r_two[1].astype(F32)
        return jnp.concatenate([left, right], axis=1)

    def drain(self):
        for copy in self.first() + self.second():
            copy.wait_send()


class Collect:
    def __init__(self, zs, acc, to_sib, r_sib, r_x, r_z, out, pool):
        self.zs, self.acc, self.to_sib, self.r_sib = zs, acc, to_sib, r_sib
        self.r_x, self.r_z, self.out = r_x, r_z, out
        self.b, self.z, self.x = (lax.axis_index(a) for a in ("batch", "z", "x"))
        self.s_s, self.s_r, self.x_s, self.x_r, self.loc = (pool.take() for _ in range(5))
        self.d_s, self.d_r, self.u_s, self.u_r = (pool.take(zs) for _ in range(4))

    def sib(self):
        return remote(self.to_sib, self.r_sib, self.s_s(), self.s_r(), {"batch": 1 - self.b})

    def side(self):
        return remote(
            self.acc.at[1 - self.x], self.r_x, self.x_s(), self.x_r(), {"x": 1 - self.x}
        )

    def dn(self, h):
        return remote(
            self.acc.at[self.x, h], self.r_z.at[h], self.d_s(h), self.d_r(h), {"z": self.z - 1}
        )

    def up(self, h):
        return remote(
            self.acc.at[self.x, h], self.r_z.at[h + 1], self.u_s(h), self.u_r(h), {"z": self.z + 1}
        )

    def fill(self, make):
        rows = self.acc.shape[2]
        for buf, core in ((self.to_sib, 1 - self.b), (self.acc, self.b)):
            value = make(core)
            for h in range(self.zs):
                for col in range(2):
                    i = 2 * h + col
                    buf[col, h] = value[i * rows : (i + 1) * rows].astype(BF)
            if buf is self.to_sib:
                self.sib().start()

    def add(self, dst, src):
        dst[...] = dst[...] + src[...]

    def after_sib(self):
        self.sib().wait_recv()

        def one(h, carry):
            self.add(self.acc.at[1 - self.x, h], self.r_sib.at[1 - self.x, h])
            return carry

        lax.fori_loop(0, self.zs, one, 0)
        self.side().start()

        def other(h, carry):
            self.add(self.acc.at[self.x, h], self.r_sib.at[self.x, h])
            return carry

        lax.fori_loop(0, self.zs, other, 0)

    def after_side(self):
        self.side().wait_recv()

        def one(h, carry):
            self.add(self.acc.at[self.x, h], self.r_x.at[h])
            return carry

        lax.fori_loop(0, self.zs, one, 0)

        def ends(h, carry):
            @pl.when((self.z == self.zs - 1) & (h < self.z))
            def _():
                self.dn(h).start()

            @pl.when((self.z == 0) & (h > 0))
            def _():
                self.up(h).start()

            return carry

        lax.fori_loop(0, self.zs, ends, 0)

    def step(self, k):
        def one(i, carry):
            @pl.when((self.z == self.zs - 1 - k) & (i <= self.z))
            def _():
                self.dn(i).wait_recv()
                self.add(self.acc.at[self.x, i], self.r_z.at[i])

                @pl.when(i < self.z)
                def _():
                    self.dn(i).start()

            j = self.zs - 1 - i

            @pl.when((self.z == k) & (j >= self.z))
            def _():
                self.up(j).wait_recv()
                self.add(self.acc.at[self.x, j], self.r_z.at[j + 1])

                @pl.when(j > self.z)
                def _():
                    self.up(j).start()

            return carry

        lax.fori_loop(0, self.zs, one, 0)
        if k == self.zs - 1:
            self.result().start()

    def result(self):
        return pltpu.make_async_copy(self.acc.at[self.x, self.z], self.out, self.loc())

    def drain(self):
        self.sib().wait_send()
        self.side().wait_send()
        self.result().wait()

        def one(h, carry):
            @pl.when(h < self.z)
            def _():
                self.dn(h).wait_send()

            @pl.when(h > self.z)
            def _():
                self.up(h).wait_send()

            return carry

        lax.fori_loop(0, self.zs, one, 0)


class LineSum:
    def __init__(self, zs, acc, r_z, pool):
        self.zs, self.acc, self.r_z = zs, acc, r_z
        self.z = lax.axis_index("z")
        self.d_s, self.d_r, self.u_s, self.u_r = (pool.take(zs) for _ in range(4))

    def dn(self, h):
        to = {"z": self.z - 1}
        return remote(self.acc.at[:, h], self.r_z.at[:, h], self.d_s(h), self.d_r(h), to)

    def up(self, h):
        to = {"z": self.z + 1}
        return remote(self.acc.at[:, h], self.r_z.at[:, h + 1], self.u_s(h), self.u_r(h), to)

    def start(self):
        for h in range(self.zs):
            if h < self.zs - 1:

                @pl.when(self.z == self.zs - 1)
                def _():
                    self.dn(h).start()

            if h > 0:

                @pl.when(self.z == 0)
                def _():
                    self.up(self.zs - h).start()

    def plus(self, h, slot):
        for c in range(self.acc.shape[0]):
            self.acc[c, h] = self.acc[c, h] + self.r_z[c, slot]

    def step(self, k):
        def one(i, carry):
            @pl.when((self.z == self.zs - 1 - k) & (i <= self.z))
            def _():
                self.dn(i).wait_recv()
                self.plus(i, i)

                @pl.when(i < self.z)
                def _():
                    self.dn(i).start()

            j = self.zs - 1 - i

            @pl.when((self.z == k) & (j >= self.z))
            def _():
                self.up(j).wait_recv()
                self.plus(j, j + 1)

                @pl.when(j > self.z)
                def _():
                    self.up(j).start()

            return carry

        lax.fori_loop(0, self.zs, one, 0)

    def drain(self):
        def one(h, carry):
            @pl.when(h < self.z)
            def _():
                self.dn(h).wait_send()

            @pl.when(h > self.z)
            def _():
                self.up(h).wait_send()

            return carry

        lax.fori_loop(0, self.zs, one, 0)


def backward_kernel(zs, heads, nl, scale, *refs):
    refs = list(refs)

    def take(count):
        out = refs[:count]
        del refs[:count]
        return out

    y_in, g_mlp, x_in, dy_in = take(4)
    if nl:
        (left_in,) = take(1)
    dh2_ref, mid_ref, vec_ref, h1_ref, q_ref, attn_ref, lse_ref, kv_ref = take(8)
    wkv_ref, wq_ref, wo_ref, cos_ref, sin_ref, start_ref = take(6)
    out_all, gh_all, g_q, g_kv, g_wo, g_vec, g_far = take(7)
    if nl:
        (left_out,) = take(1)
    y_own, y_one, y_two, dmid_ref, dat_ref, half_ref = take(6)
    q_s, do_s, q_t, do_t, delta_ref = take(5)
    dkv_ref, rx_ref, rz_ref, acc_ref, dqkv_ref, dh_send, dh_recv = take(7)
    bufs_q, bufs_kv, bufs_wo = take(5), take(5), take(5)
    vec_own, vec_recv, vec_z, x_ref, dy_ref, sem_ref = take(6)
    if nl:
        left_acc, left_z = take(2)

    b, z, x, t = (lax.axis_index(a) for a in ("batch", "z", "x", "tensor"))
    shards = 2 * zs
    me = 2 * z + x
    half, width = mid_ref.shape
    q_cols = heads * HEAD_SIZE
    pool = Pool(sem_ref)
    greet(z, zs)

    sq_y = Square(y_in, y_own, y_one, y_two, pool)
    col_q = Collect(zs, *bufs_q, g_q, pool)
    col_kv = Collect(zs, *bufs_kv, g_kv, pool)
    col_wo = Collect(zs, *bufs_wo, g_wo, pool)
    runs = thirds(zs)
    mine = pl.ds(pl.multiple_of(t * half, half), half)
    fetch = pool.take(2)
    x_load = pltpu.make_async_copy(x_in.at[mine], x_ref, fetch(0))
    dy_load = pltpu.make_async_copy(dy_in.at[mine], dy_ref, fetch(1))
    x_load.start()
    dy_load.start()
    if nl:
        lines = [
            LineSum(zs, left_acc.at[pl.ds(c, 1)], left_z.at[pl.ds(c, 1)], pool) for c in range(nl)
        ]
        left_l = pool.take()
        left_load = pltpu.make_async_copy(left_in, left_acc, left_l())
        left_load.start()

    def line_tick(tick):
        for c in range(nl):
            if tick == c:
                lines[c].start()
            for k in range(1, zs):
                if min(k, 3) == tick - c:
                    lines[c].step(k)

    vec = vec_ref[...]
    gain_attn = lanes(vec, 4, 6)
    gain_mlp = lanes(vec, 10, 6)

    mid = mid_ref[...]
    d_norm, g_norm_mlp = norm_backward(mid, norm_factor(mid), gain_mlp, dh2_ref[...])
    dy_load.wait()
    dmid_ref[...] = dy_ref[...].astype(F32) + d_norm
    dat_ref[t] = dmid_ref[...].astype(BF)
    dat_s, dat_r = pool.take(), pool.take()

    def dat_copy(i):
        return remote(dat_ref.at[i], dat_ref.at[i], dat_s(), dat_r(), {"tensor": 1 - t})

    dat_copy(t).start()
    if nl:
        left_load.wait()
        line_tick(0)

    x0_s, x0_r, x1_s, x1_r = (pool.take(zs) for _ in range(4))
    c0_s, c0_r, c1_s, c1_r = (pool.take(zs) for _ in range(4))

    def side(s, sub):
        src = dkv_ref.at[2 * s + 1 - x + sub]
        send, recv = (x0_s, x0_r) if sub == 0 else (x1_s, x1_r)
        return remote(src, rx_ref.at[s + sub], send(s), recv(s), {"x": 1 - x})

    def chain(s, sub):
        src = dkv_ref.at[2 * s + x + sub]
        send, recv = (c0_s, c0_r) if sub == 0 else (c1_s, c1_r)
        to = z - 1 if sub == 0 else z + 1
        return remote(src, rz_ref.at[s + sub], send(s), recv(s), {"z": to})

    acc_ref[...] = jnp.zeros_like(acc_ref)

    def prepare(sub):
        d_out = dot(dat_ref[sub], merge_rows(wo_ref[...])).astype(BF)
        rows = pl.ds(pl.multiple_of(sub * half, half), half)
        out = attn_ref[rows]
        q = q_ref[rows]
        for h in range(heads):
            cols = slice(h * HEAD_SIZE, (h + 1) * HEAD_SIZE)
            at = slice(h * half, (h + 1) * half)
            q_s[sub, at] = q[:, cols]
            do_s[sub, at] = d_out[:, cols]
            q_t[sub, :, at] = q[:, cols].T
            do_h = d_out[:, cols].T
            do_t[sub, :, at] = do_h
            delta_ref[sub, :, at] = jnp.sum(
                do_h.astype(F32) * out[:, cols].T.astype(F32), axis=0, keepdims=True
            )

    def fold(sub, block):
        slot = block + sub
        keys = kv_ref[slot, :, :HEAD_SIZE]
        vals = kv_ref[slot, :, HEAD_SIZE:]
        scores = dot(keys, q_t[sub]) * scale + block_mask(
            sub, block, me, shards, half, start_ref[sub], heads
        )
        probs = jnp.exp(scores - lse_ref[sub])
        d_scores = (probs * (dot(vals, do_t[sub]) - delta_ref[sub])).astype(BF)
        dkv_ref[slot, :, HEAD_SIZE:] = dot(probs.astype(BF), do_s[sub]).astype(BF)
        dkv_ref[slot, :, :HEAD_SIZE] = (dot(d_scores, q_s[sub]) * scale).astype(BF)
        acc_ref[sub] += dot(keys.T, d_scores)

    def far_blocks(sub):
        def one(k, carry):
            s = jnp.where(sub == 0, z - k, z + k)

            @pl.when(in_range(s, zs) & ((k > 0) | (x != sub)))
            def _():
                fold(sub, 2 * s + 1 - x)

                @pl.when(sub == 0)
                def _():
                    side(s, 0).start()

                @pl.when(sub == 1)
                def _():
                    side(s, 1).start()

            return carry

        lax.fori_loop(0, zs, one, 0)

    def near_blocks(sub):
        def one(i, carry):
            k = zs - 1 - i
            s = jnp.where(sub == 0, z - k, z + k)

            @pl.when(in_range(s, zs))
            def _():
                fold(sub, 2 * s + x)

            return carry

        lax.fori_loop(0, zs, one, 0)

    def tokens(i, carry):
        sub = jnp.where(i == 0, t, 1 - t)

        @pl.when(i == 1)
        def _():
            line_tick(1)
            dat_copy(1 - t).wait_recv()

        prepare(sub)
        far_blocks(sub)
        near_blocks(sub)
        return carry

    lax.fori_loop(0, 2, tokens, 0)
    sq_y.start()

    def wo_part(core):
        rows = width // 2
        at = pl.ds(pl.multiple_of(core * rows, rows), rows)
        return dot(half_ref[at], attn_ref[...])

    def plus(slot, src):
        dkv_ref[slot] = dkv_ref[slot] + src[...]

    def kv_begin():
        def one(i, carry):
            j = zs - 1 - i

            @pl.when((i < z) | ((i == z) & (x == 0)))
            def _():
                side(i, 0).wait_recv()
                plus(2 * i + x, rx_ref.at[i])

            @pl.when((z == zs - 1) & (i < z))
            def _():
                chain(i, 0).start()

            @pl.when((j > z) | ((j == z) & (x == 1)))
            def _():
                side(j, 1).wait_recv()
                plus(2 * j + x + 1, rx_ref.at[j + 1])

            @pl.when((z == 0) & (j > z))
            def _():
                chain(j, 1).start()

            return carry

        lax.fori_loop(0, zs, one, 0)

    def kv_step(k):
        def one(i, carry):
            j = zs - 1 - i

            @pl.when((z == zs - 1 - k) & (i <= z))
            def _():
                chain(i, 0).wait_recv()
                plus(2 * i + x, rz_ref.at[i])

                @pl.when(i < z)
                def _():
                    chain(i, 0).start()

            @pl.when((z == k) & (j >= z))
            def _():
                chain(j, 1).wait_recv()
                plus(2 * j + x + 1, rz_ref.at[j + 1])

                @pl.when(j > z)
                def _():
                    chain(j, 1).start()

            return carry

        lax.fori_loop(0, zs, one, 0)

    kv_begin()
    for i in range(2):
        half_ref[:, i * half : (i + 1) * half] = dat_ref[i].T
    col_wo.fill(wo_part)
    for k in runs[0] + runs[1]:
        kv_step(k)
    line_tick(2)
    col_wo.after_sib()

    def back(v, at):
        return v * cos_ref[at] - pltpu.roll(v, HEAD_SIZE // 2, 1) * sin_ref[at]

    for sub in range(2):
        at = slice(sub * half, (sub + 1) * half)
        for h in range(heads):
            v = acc_ref[sub, :, h * half : (h + 1) * half].T * scale
            dqkv_ref[at, h * HEAD_SIZE : (h + 1) * HEAD_SIZE] = back(v, at).astype(BF)
    half_ref[...] = h1_ref[...].T
    for k in runs[2]:
        kv_step(k)

    def part(first, last):
        def make(core):
            rows = width // 2
            at = pl.ds(pl.multiple_of(core * rows, rows), rows)
            return dot(half_ref[at], dqkv_ref[:, first:last])

        return make

    for sub in range(2):
        at = slice(sub * half, (sub + 1) * half)
        dk = dkv_ref[me + sub, :, :HEAD_SIZE].astype(F32)
        dqkv_ref[at, q_cols : q_cols + HEAD_SIZE] = back(dk, at).astype(BF)
        dqkv_ref[at, q_cols + HEAD_SIZE :] = dkv_ref[me + sub, :, HEAD_SIZE:]

    dh_s, dh_r = pool.take(), pool.take()
    dh_copy = remote(dh_send, dh_recv, dh_s(), dh_r(), {"tensor": 1 - t})
    theirs = pl.ds(pl.multiple_of((1 - t) * half, half), half)
    own = pl.ds(pl.multiple_of(t * half, half), half)

    def d_first(at):
        q_part = dot_nt(dqkv_ref[at, :q_cols], merge_rows(wq_ref[...]))
        return q_part + dot_nt(dqkv_ref[at, q_cols:], merge_rows(wkv_ref[...]))

    dh_send[...] = d_first(theirs).astype(BF)
    dh_copy.start()
    dh1 = d_first(own)
    sq_y.turn()
    col_kv.fill(part(q_cols, q_cols + 2 * HEAD_SIZE))
    col_q.fill(part(0, q_cols))
    line_tick(3)
    col_q.after_sib()
    col_kv.after_sib()

    dh_copy.wait_recv()
    dh1 = dh1 + dh_recv[...].astype(F32)
    x_load.wait()
    xv = x_ref[...].astype(F32)
    d_norm, g_norm_attn = norm_backward(xv, norm_factor(xv), gain_attn, dh1)

    g_bias = jnp.sum(dqkv_ref[...].astype(F32), axis=0, keepdims=True)
    row = jnp.concatenate([g_bias, g_norm_attn, g_norm_mlp], axis=1)
    lane = vec_ref.shape[1]
    vec_own[...] = jnp.concatenate(
        [row[:, i * lane : (i + 1) * lane] for i in range(vec_ref.shape[0])], axis=0
    )
    v_s, v_r = pool.take(3), pool.take(3)
    vz_s, vz_r = pool.take(zs), pool.take(zs)
    norms = (lax.broadcasted_iota(jnp.int32, vec_ref.shape, 0) >= 4).astype(F32)

    def v_side(i):
        axis, index = (("tensor", t), ("x", x), ("batch", b))[i]
        return remote(vec_own, vec_recv.at[i], v_s(i), v_r(i), {axis: 1 - index})

    def v_add(i):
        v_side(i).wait()
        other = vec_recv[i]
        vec_own[...] = vec_own[...] + (other * norms if i == 0 else other)

    v_side(0).start()
    line_tick(4)
    dat_copy(t).wait_send()
    dat_ref[t] = (dmid_ref[...] + d_norm).astype(BF)
    gh_s, gh_r, gh_l = (pool.take() for _ in range(3))
    gh_copy = remote(dat_ref.at[t], gh_all.at[t], gh_s(), gh_r(), {"tensor": 1 - t})
    gh_own = pltpu.make_async_copy(dat_ref.at[t], gh_all.at[t], gh_l())
    gh_copy.start()
    gh_own.start()
    v_add(0)
    v_side(1).start()
    col_wo.after_side()
    far_s, far_r = pool.take(), pool.take()
    far_copy = remote(
        g_mlp.at[:, 1 - x],
        g_far.at[pl.ds(0, g_mlp.shape[0])],
        far_s(),
        far_r(),
        {"x": 1 - x},
    )
    far_copy.start()
    line_tick(5)
    for k in runs[0]:
        col_wo.step(k)
    col_q.after_side()
    v_add(1)
    v_side(2).start()
    col_kv.after_side()
    y_sum = sq_y.result()
    sq_y.drain()
    total = mid_ref[...] + y_sum
    cut = width // 2
    o_s, o_r, o_l = pool.take(2), pool.take(2), pool.take(2)
    sends, locals_ = [], []
    for i in range(2):
        y_own[i] = total[:, i * cut : (i + 1) * cut].astype(BF)
        dst = out_all.at[t, :, pl.ds(i * cut, cut)]
        sends.append(remote(y_own.at[i], dst, o_s(i), o_r(i), {"tensor": 1 - t}))
        locals_.append(pltpu.make_async_copy(y_own.at[i], dst, o_l(i)))
    for copy in sends + locals_:
        copy.start()
    for tick in range(6, nl + 3):
        line_tick(tick)
    v_add(2)
    for k in runs[0]:
        col_q.step(k)
    for k in runs[1]:
        col_wo.step(k)
    if nl:
        lf_s, lf_r, lf_l = (pool.take() for _ in range(3))
        rows = g_far.shape[1]

        def left_rows(col):
            return left_acc.at[:, z, pl.ds(pl.multiple_of(col * rows, rows), rows)]

        left_far = remote(
            left_rows(1 - x),
            g_far.at[pl.ds(g_mlp.shape[0], nl)],
            lf_s(),
            lf_r(),
            {"x": 1 - x},
        )
        left_own = pltpu.make_async_copy(left_rows(x), left_out, lf_l())
        left_far.start()
        left_own.start()
    for k in runs[0]:
        col_kv.step(k)

    def v_copy(to):
        return remote(vec_own, vec_z.at[z], vz_s(to), vz_r(z), {"z": to})

    for to in range(zs):

        @pl.when(to != z)
        def _():
            v_copy(to).start()

    for k in runs[1]:
        col_q.step(k)
    for k in runs[1]:
        col_kv.step(k)
    for item in (col_wo, col_q, col_kv):
        for k in runs[2]:
            item.step(k)
    total = jnp.zeros(vec_ref.shape, F32)
    for frm in range(zs):

        @pl.when(frm != z)
        def _():
            remote(vec_own, vec_z.at[frm], vz_s(frm), vz_r(frm), {"z": frm}).wait_recv()

        @pl.when(frm == z)
        def _():
            vec_z[frm] = vec_own[...]

        total = total + vec_z[frm]
    g_vec[...] = total

    for to in range(zs):

        @pl.when(to != z)
        def _():
            v_copy(to).wait_send()

    def dkv_drain(s, carry):
        @pl.when((s < z) | ((s == z) & (x == 1)))
        def _():
            side(s, 0).wait_send()

        @pl.when((s > z) | ((s == z) & (x == 0)))
        def _():
            side(s, 1).wait_send()

        @pl.when(s < z)
        def _():
            chain(s, 0).wait_send()

        @pl.when(s > z)
        def _():
            chain(s, 1).wait_send()

        return carry

    lax.fori_loop(0, zs, dkv_drain, 0)
    for item in (col_wo, col_q, col_kv):
        item.drain()
    dh_copy.wait_send()
    far_copy.wait()
    gh_own.wait()
    gh_copy.wait()
    for copy in sends + locals_:
        copy.wait()
    if nl:
        for item in lines:
            item.drain()
        left_far.wait()
        left_own.wait()


def backward_call(zs, heads, left, big, small):
    mid, vec = small[1:3]
    wq = small[9]
    half, width = mid.shape
    tok = 2 * half
    _, rows, q_cols = wq.shape
    qkv_cols = q_cols + 2 * HEAD_SIZE
    n2, _, _, three = big[1].shape
    nl = left[0].shape[0] if left else 0
    shape = jax.ShapeDtypeStruct
    any_spec = pl.BlockSpec(memory_space=pl.ANY)
    vm = pltpu.VMEM
    cut = width // 2

    def collect(cols):
        return [
            vm((2, zs, rows, cols), BF),
            vm((2, zs, rows, cols), BF),
            vm((2, zs, rows, cols), BF),
            vm((zs, rows, cols), BF),
            vm((zs + 1, rows, cols), BF),
        ]

    square = [vm((4, half, cut), BF), vm((4, half, cut), BF), vm((2, half, cut), BF)]
    lines = [vm(left[0].shape, BF), vm((nl, zs + 1) + left[0].shape[2:], BF)] if nl else []
    return pl.pallas_call(
        functools.partial(backward_kernel, zs, heads, nl, HEAD_SIZE ** (-0.5)),
        out_shape=[
            shape((2, half, width), BF),
            shape((2, half, width), BF),
            shape((rows, q_cols), BF),
            shape((rows, 2 * HEAD_SIZE), BF),
            shape((rows, q_cols), BF),
            shape(vec.shape, F32),
            shape((n2 + nl, rows, three), BF),
        ]
        + ([shape((nl, rows, three), BF)] if nl else []),
        in_specs=[any_spec] * (4 + len(left)) + [VMEM] * len(small),
        out_specs=[any_spec] * 5 + [VMEM, any_spec] + [any_spec] * len(left),
        scratch_shapes=square
        + [
            vm((half, width), F32),
            vm((2, half, width), BF),
            vm((width, tok), BF),
            vm((2, heads * half, HEAD_SIZE), BF),
            vm((2, heads * half, HEAD_SIZE), BF),
            vm((2, HEAD_SIZE, heads * half), BF),
            vm((2, HEAD_SIZE, heads * half), BF),
            vm((2, 1, heads * half), F32),
            vm((2 * zs + 1, half, 2 * HEAD_SIZE), BF),
            vm((zs + 1, half, 2 * HEAD_SIZE), BF),
            vm((zs + 1, half, 2 * HEAD_SIZE), BF),
            vm((2, HEAD_SIZE, heads * half), F32),
            vm((tok, qkv_cols), BF),
            vm((half, width), BF),
            vm((half, width), BF),
        ]
        + collect(q_cols)
        + collect(2 * HEAD_SIZE)
        + collect(q_cols)
        + [
            vm(vec.shape, F32),
            vm((3,) + vec.shape, F32),
            vm((zs,) + vec.shape, F32),
            vm((half, width), BF),
            vm((half, width), BF),
            pltpu.SemaphoreType.DMA(((22 + 4 * nl) * zs + 90,)),
        ]
        + lines,
        compiler_params=pltpu.CompilerParams(
            collective_id=2, has_side_effects=True, vmem_limit_bytes=63 * 2**20
        ),
        cost_estimate=pl.CostEstimate(
            flops=4 * tok * width * (qkv_cols + q_cols) + 2**32,
            bytes_accessed=32 * 2**20,
            transcendentals=0,
        ),
    )(*big, *left, *small)


def remote(src, dst, send, recv, to):
    return pltpu.make_async_remote_copy(
        src_ref=src,
        dst_ref=dst,
        send_sem=send,
        recv_sem=recv,
        device_id=to,
        device_id_type=pl.DeviceIdType.MESH,
    )


def greet(z, zs):
    barrier = pltpu.get_barrier_semaphore()
    for axis in ("batch", "x", "tensor"):
        other = {axis: 1 - lax.axis_index(axis)}
        pl.semaphore_signal(barrier, inc=1, device_id=other, device_id_type=pl.DeviceIdType.MESH)

    @pl.when(z > 0)
    def _():
        pl.semaphore_signal(
            barrier, inc=1, device_id={"z": z - 1}, device_id_type=pl.DeviceIdType.MESH
        )

    @pl.when(z < zs - 1)
    def _():
        pl.semaphore_signal(
            barrier, inc=1, device_id={"z": z + 1}, device_id_type=pl.DeviceIdType.MESH
        )

    pl.semaphore_wait(barrier, 5 - (z == 0).astype(jnp.int32) - (z == zs - 1).astype(jnp.int32))


def in_range(c, count):
    return (c >= 0) & (c < count)


class Exchange:
    def __init__(self, mats, full, first, zs, skip, sems):
        self.mats, self.full, self.first = mats, full, first
        self.x = lax.axis_index("x")
        home = (lax.axis_index("batch") * zs + lax.axis_index("z")) * 2 + self.x
        self.rows, self.cols = mats[0].shape[0], full.shape[2] // 3
        self.at = pl.ds(pl.multiple_of(home * self.rows, self.rows), self.rows)
        self.shift = mats[0].shape[1] // 2 - skip // 2
        self.send, self.recv, self.loc = sems

    def pieces(self, c):
        for w, mat in enumerate(self.mats):
            dst = self.full.at[c, self.at, pl.ds(w * self.cols, self.cols)]
            yield mat, dst

    def source(self, mat, c, x):
        first = pl.multiple_of(x * self.shift + (self.first + c) * self.cols, 128)
        return mat.at[:, pl.ds(first, self.cols)]

    def ship(self, c, i):
        for mat, dst in self.pieces(c):
            src = self.source(mat, c, 1 - self.x)
            remote(src, dst, self.send(i), self.recv(i), {"x": 1 - self.x}).start()

    def keep(self, c, i):
        for mat, dst in self.pieces(c):
            pltpu.make_async_copy(self.source(mat, c, self.x), dst, self.loc(i)).start()

    def fetch(self, c, other, buf, sem):
        x = 1 - self.x if other else self.x
        for w, mat in enumerate(self.mats):
            dst = buf.at[pl.ds(c * self.rows, self.rows), pl.ds(w * self.cols, self.cols)]
            pltpu.make_async_copy(self.source(mat, c, x), dst, sem).start()

    def both(self, c, i):
        spot = self.full.at[c, self.at]
        return remote(spot, spot, self.send(i), self.recv(i), {"x": 1 - self.x})

    def arrived(self, c, i):
        self.both(c, i).wait_recv()
        spot = self.full.at[c, self.at]
        pltpu.make_async_copy(spot, spot, self.loc(i)).wait()

    def sent(self, c, i):
        self.both(c, i).wait_send()


class Gather:
    def __init__(self, zs, mine, full, sems):
        self.zs, self.mine, self.full = zs, mine, full
        self.loc, self.up, self.dn, self.zr, self.ss, self.sr = sems
        self.b, self.z = lax.axis_index("batch"), lax.axis_index("z")
        self.size = full.shape[1] // (2 * zs)

    def at(self, c, b, z):
        rows = pl.ds(pl.multiple_of((b * self.zs + z) * self.size, self.size), self.size)
        return self.full.at[:, rows] if c is None else self.full.at[c, rows]

    def sems(self, c, s):
        i = 0 if c is None else c
        return (ref.at[i, s] for ref in (self.up, self.dn, self.zr, self.ss, self.sr))

    def up_copy(self, c, s, src=None):
        dst = self.at(c, self.b, s)
        up, _, zr, _, _ = self.sems(c, s)
        return remote(dst if src is None else src, dst, up, zr, {"z": self.z + 1})

    def dn_copy(self, c, s, src=None):
        dst = self.at(c, self.b, s)
        _, dn, zr, _, _ = self.sems(c, s)
        return remote(dst if src is None else src, dst, dn, zr, {"z": self.z - 1})

    def sib_copy(self, c, s, src=None):
        dst = self.at(c, self.b, s)
        _, _, _, ss, sr = self.sems(c, s)
        return remote(dst if src is None else src, dst, ss, sr, {"batch": 1 - self.b})

    def local(self, c):
        return pltpu.make_async_copy(self.mine.at[c], self.at(c, self.b, self.z), self.loc.at[c])

    def start(self, c):
        src = None if self.mine is None else self.mine.at[c]

        @pl.when(self.z < self.zs - 1)
        def _():
            self.up_copy(c, self.z, src).start()

        @pl.when(self.z > 0)
        def _():
            self.dn_copy(c, self.z, src).start()

        self.sib_copy(c, self.z, src).start()
        if self.mine is not None:
            self.local(c).start()

    def hop(self, c, k):
        low, high = self.z - k, self.z + k

        @pl.when(low >= 0)
        def _():
            self.dn_copy(c, low).wait_recv()

            @pl.when(self.z < self.zs - 1)
            def _():
                self.up_copy(c, low).start()

            self.sib_copy(c, low).start()

        @pl.when(high < self.zs)
        def _():
            self.dn_copy(c, high).wait_recv()

            @pl.when(self.z > 0)
            def _():
                self.dn_copy(c, high).start()

            self.sib_copy(c, high).start()

    def finish(self, c):
        if self.mine is not None:
            self.local(c).wait()
        for s in range(self.zs):
            dst = self.at(c, 1 - self.b, s)
            _, _, _, ss, sr = self.sems(c, s)
            remote(dst, dst, ss, sr, {"batch": 1 - self.b}).wait_recv()

    def drain(self, c):
        for s in range(self.zs):

            @pl.when((s <= self.z) & (self.z < self.zs - 1))
            def _():
                self.up_copy(c, s).wait_send()

            @pl.when((s >= self.z) & (self.z > 0))
            def _():
                self.dn_copy(c, s).wait_send()

            self.sib_copy(c, s).wait_send()


class Reduce:
    def __init__(self, zs, ends, ring, to_sib, r_sib, r_dn, r_up, tmp, out, left, sems):
        self.zs, self.ring, self.to_sib, self.out = zs, ring, to_sib, out
        self.ends, self.left = ends, left
        self.r_sib, self.r_dn, self.r_up = r_sib, r_dn, r_up
        self.tmp_s, self.tmp_d, self.tmp_u = tmp
        self.s_s, self.s_r, self.d_s, self.d_r, self.u_s, self.u_r, self.load, self.o_s, self.l_s = sems
        self.b, self.z = lax.axis_index("batch"), lax.axis_index("z")
        self.slots = ring.shape[0]
        self.size = ring.shape[1] // zs

    def rows(self, h):
        return pl.ds(pl.multiple_of(h * self.size, self.size), self.size)

    def sib(self, c):
        return remote(
            self.to_sib, self.r_sib.at[c], self.s_s.at[c], self.s_r.at[c], {"batch": 1 - self.b}
        )

    def dn(self, c, h):
        src = self.ring.at[lax.rem(c, self.slots), self.rows(h)]
        dst = self.r_dn.at[c, self.rows(h)]
        return remote(src, dst, self.d_s.at[c, h], self.d_r.at[c, h], {"z": self.z - 1})

    def up(self, c, h):
        src = self.ring.at[lax.rem(c, self.slots), self.rows(h)]
        dst = self.r_up.at[c, self.rows(h)]
        return remote(src, dst, self.u_s.at[c, h], self.u_r.at[c, h], {"z": self.z + 1})

    def load_sib(self, c):
        return pltpu.make_async_copy(self.r_sib.at[c], self.tmp_s, self.load.at[0])

    def load_dn(self, c, h):
        rows = self.rows(h)
        return pltpu.make_async_copy(self.r_dn.at[c, rows], self.tmp_d.at[rows], self.load.at[1 + h])

    def load_up(self, c, h):
        rows = self.rows(h)
        return pltpu.make_async_copy(
            self.r_up.at[c, rows], self.tmp_u.at[rows], self.load.at[1 + self.zs + h]
        )

    def arrive(self, c_sib, c_dn, c_up, count):
        @pl.when(in_range(c_sib, count))
        def _():
            self.sib(c_sib).wait_recv()
            self.load_sib(c_sib).start()

        for h in range(self.zs):

            @pl.when(in_range(c_dn, self.ends) & (self.z < self.zs - 1) & (h <= self.z))
            def _():
                self.dn(c_dn, h).wait_recv()
                self.load_dn(c_dn, h).start()

            @pl.when(in_range(c_up, self.ends) & (self.z > 0) & (h >= self.z))
            def _():
                self.up(c_up, h).wait_recv()
                self.load_up(c_up, h).start()

    def add(self, slot, rows, tmp):
        self.ring[slot, rows] = self.ring[slot, rows] + tmp[rows]

    def pass_on(self, c_sib, c_dn, c_up, count):
        @pl.when(in_range(c_sib, count))
        def _():
            self.load_sib(c_sib).wait()
            slot = lax.rem(c_sib, self.slots)
            for h in range(self.zs):
                self.add(slot, pl.ds(h * self.size, self.size), self.tmp_s)
            for h in range(self.zs - 1):

                @pl.when((self.z == self.zs - 1) & (c_sib < self.ends))
                def _():
                    self.dn(c_sib, h).start()

            for h in range(1, self.zs):

                @pl.when((self.z == 0) & (c_sib < self.ends))
                def _():
                    self.up(c_sib, h).start()

            if self.left is not None:

                @pl.when(c_sib >= self.ends)
                def _():
                    self.leave(c_sib).start()

        for h in range(self.zs):

            @pl.when(in_range(c_dn, self.ends) & (self.z < self.zs - 1) & (h <= self.z))
            def _():
                self.load_dn(c_dn, h).wait()
                self.add(lax.rem(c_dn, self.slots), pl.ds(h * self.size, self.size), self.tmp_d)

                @pl.when(h < self.z)
                def _():
                    self.dn(c_dn, h).start()

            @pl.when(in_range(c_up, self.ends) & (self.z > 0) & (h >= self.z))
            def _():
                self.load_up(c_up, h).wait()
                self.add(lax.rem(c_up, self.slots), pl.ds(h * self.size, self.size), self.tmp_u)

                @pl.when(h > self.z)
                def _():
                    self.up(c_up, h).start()

    def leave(self, c):
        src = self.ring.at[lax.rem(c, self.slots)]
        return pltpu.make_async_copy(src, self.left.at[c - self.ends], self.l_s.at[c - self.ends])

    def result(self, c):
        src = self.ring.at[lax.rem(c, self.slots), self.rows(self.z)]
        return pltpu.make_async_copy(src, self.out.at[c], self.o_s.at[0])

    def finish(self, c):
        for h in range(self.zs):

            @pl.when(h < self.z)
            def _():
                self.dn(c, h).wait_send()

            @pl.when(h > self.z)
            def _():
                self.up(c, h).wait_send()

        self.result(c).start()


def mlp_kernel(zs, nc, n1, n2, fc, skip, *refs):
    refs = list(refs)

    def take(count):
        out = refs[:count]
        del refs[:count]
        return out

    if n1:
        mats, full_one = take(3), take(1)[0]
        mine = None
    else:
        (mine,) = take(1)
    h2, dy, dh2_out, y_out, g_out, full, r_sib, r_dn, r_up = take(9)
    left = take(1)[0] if n2 < nc else None
    acc_y, acc_d, h2t, dyt, wbuf, hid_s, dgu_s, ring, to_sib, tmp_s, tmp_d, tmp_u = take(12)
    d_src, d_own, d_one, d_two = take(4)
    w_sem, x_s, x_r, k_s, sq_sem, st_sem = take(6)
    sems = refs
    b, z, x = lax.axis_index("batch"), lax.axis_index("z"), lax.axis_index("x")
    greet(z, zs)
    rest = nc - n1
    lag = 0 if n1 else zs + 1
    ahead = n1 - zs + 1 if n1 else 0
    gather = Gather(zs, mine, full, sems[:6])
    reduce = Reduce(
        zs, n2, ring, to_sib, r_sib, r_dn, r_up, (tmp_s, tmp_d, tmp_u), g_out, left, sems[6:]
    )
    slots = ring.shape[0]
    half = ring.shape[1]
    toks = h2.shape[0]
    part = toks // 4
    square = Square(d_src, d_own, d_one, d_two, Pool(sq_sem))

    if n1:
        trade = Exchange(
            mats, full, n1, zs, skip, [lambda i, r=r: r.at[i] for r in (x_s, x_r, k_s)]
        )
        stage = [ring.at[ring.shape[0] - 1], ring.at[ring.shape[0] - 2]]
        for c in range(rest):
            for side in range(2):
                trade.fetch(c, side, stage[side], st_sem.at[2 * c + side])

        def slices(c):
            rows = pl.ds(c * trade.rows, trade.rows)
            dst = full.at[c, trade.at]
            return (
                pltpu.make_async_copy(stage[0].at[rows], dst, k_s.at[c]),
                remote(stage[1].at[rows], dst, x_s.at[c], x_r.at[c], {"x": 1 - x}),
            )

        for c in range(rest):
            for side in range(2):
                rows = stage[side].at[pl.ds(c * trade.rows, trade.rows)]
                pltpu.make_async_copy(rows, rows, st_sem.at[2 * c + side]).wait()
                slices(c)[side].start()

    def weights(c):
        return pltpu.make_async_copy(full.at[c - n1], wbuf, w_sem.at[0])

    def weights_one(c):
        return pltpu.make_async_copy(full_one.at[c], wbuf, w_sem.at[0])

    if n1:
        weights_one(0).start()
    acc_y[...] = jnp.zeros_like(acc_y)
    acc_d[...] = jnp.zeros_like(acc_d)
    for m in range(4):
        at = slice(m * part, (m + 1) * part)
        h2t[:, at] = h2[at].T
        dyt[:, at] = dy[at].T

    nl = nc - n2

    def keep_slot(c):
        return jnp.maximum(c - n2, 0) if nl else 0

    def compute(c):
        k = keep_slot(c)
        col = lax.broadcasted_iota(jnp.int32, (1, fc), 1) + c * fc
        live = jnp.where((col >= skip) | (x == 0), 1.0, 0.0).astype(F32)
        gate_up = dot(h2[...], wbuf[:, : 2 * fc])
        d_hidden = dot(dy[...], wbuf[:, 2 * fc :]) * live
        gate, up = gate_up[:, :fc], gate_up[:, fc:]
        sig = 1.0 / (1.0 + jnp.exp(-gate))
        silu = gate * sig
        hid_s[k] = (silu * up * live).astype(BF)
        dgu_s[k, :, :fc] = (d_hidden * up * sig * (1.0 + gate * (1.0 - sig))).astype(BF)
        dgu_s[k, :, fc:] = (d_hidden * silu).astype(BF)
        acc_y[...] += dot_nt(hid_s[k], wbuf[:, 2 * fc :])
        acc_d[...] += dot_nt(dgu_s[k], wbuf[:, : 2 * fc])

        @pl.when(c == nc - 1)
        def _():
            for i in range(4):
                d_src[i] = acc_d[i * part : (i + 1) * part].astype(BF)
            square.start()

    def products(c):
        k = keep_slot(c)

        @pl.when(c > 0)
        def _():
            reduce.sib(c - 1).wait_send()

        theirs = pl.ds(pl.multiple_of((1 - b) * half, half), half)
        own = pl.ds(pl.multiple_of(b * half, half), half)
        to_sib[:, : 2 * fc] = dot(h2t[theirs], dgu_s[k]).astype(BF)
        to_sib[:, 2 * fc :] = dot(dyt[theirs], hid_s[k]).astype(BF)
        reduce.sib(c).start()
        slot = lax.rem(c, slots)
        ring[slot, :, : 2 * fc] = dot(h2t[own], dgu_s[k]).astype(BF)
        ring[slot, :, 2 * fc :] = dot(dyt[own], hid_s[k]).astype(BF)

    def begin(i):
        @pl.when(in_range(i, rest))
        def _():
            if n1:
                trade.arrived(i, i)
            gather.start(i)

    def tick(t, carry):
        if n1:
            @pl.when(t == slots - 3)
            def _():
                for c in range(rest):
                    trade.sent(c, c)

        c = t - lag

        @pl.when(in_range(c, nc))
        def _():
            weights(n1).wait()
            compute(c)

        g = t + ahead
        begin(g)
        for k in range(1, zs):

            @pl.when(in_range(g - k, rest))
            def _():
                gather.hop(g - k, k)

        @pl.when(in_range(g - zs, rest))
        def _():
            gather.finish(g - zs)
            weights(g - zs + n1).start()

        if n1:

            @pl.when(c + 1 < n1)
            def _():
                weights_one(c + 1).start()

        c_dn = c - 1 - 3 * (zs - 1 - z)
        c_up = c - 1 - 3 * z
        c_end = c - 3 * zs + 1

        def product_at(step):
            late = step - nl
            return jnp.where(
                in_range(step, n2), step, jnp.where((step >= nc) & (late < nc), late, -1)
            )

        c_sib = product_at(c - 1)
        reduce.arrive(c_sib, c_dn, c_up, nc)
        reduce.pass_on(c_sib, c_dn, c_up, nc)

        @pl.when(in_range(c_end, n2))
        def _():
            reduce.finish(c_end)
            reduce.result(c_end).wait()

        c_prod = product_at(c)

        @pl.when(c_prod >= 0)
        def _():
            products(c_prod)

        return carry

    for i in range(ahead):
        begin(i)
    lax.fori_loop(0, nc + lag, tick, 0)

    end = max(nc + nl + 1, n2 + 3 * zs - 1) + lag
    turn = min(nc + lag + 3, end)
    lax.fori_loop(nc + lag, turn, tick, 0)
    square.turn()
    for copy in square.first():
        copy.wait_send()
    for i in range(4):
        d_src[i] = acc_y[i * part : (i + 1) * part].astype(BF)
    y_copy = pltpu.make_async_copy(d_src, y_out, w_sem.at[0])
    y_copy.start()
    lax.fori_loop(turn, end, tick, 0)
    dh2_out[...] = square.result()
    for copy in square.second():
        copy.wait_send()
    y_copy.wait()
    reduce.sib(nc - 1).wait_send()
    for c in range(n2, nc):
        reduce.leave(c).wait()

    def drain(c, carry):
        gather.drain(c)
        return carry

    lax.fori_loop(0, rest, drain, 0)


def mlp_call(zs, nc, n1, n2, fc, skip, weights, h2, dy):
    toks, width = h2.shape
    half = width // 2
    slots = min(2 * zs, nc)
    rest = nc - n1
    dma = pltpu.SemaphoreType.DMA
    vm = pltpu.VMEM
    shape = jax.ShapeDtypeStruct
    any_spec = pl.BlockSpec(memory_space=pl.ANY)
    out = [
        shape((toks // 4, width), F32),
        shape((4, toks // 4, width), BF),
        shape((n2, half // zs, 3 * fc), BF),
        shape((rest, width, 3 * fc), BF),
        shape((nc, half, 3 * fc), BF),
        shape((n2, half, 3 * fc), BF),
        shape((n2, half, 3 * fc), BF),
    ]
    if n2 < nc:
        out.append(shape((nc - n2, half, 3 * fc), BF))
    result = pl.pallas_call(
        functools.partial(mlp_kernel, zs, nc, n1, n2, fc, skip),
        out_shape=out,
        in_specs=[any_spec] * len(weights) + [VMEM, VMEM],
        out_specs=[VMEM] + [any_spec] * (len(out) - 1),
        scratch_shapes=[
            vm((toks, width), F32),
            vm((toks, width), F32),
            vm((width, toks), BF),
            vm((width, toks), BF),
            vm((width, 3 * fc), BF),
            vm((max(nc - n2, 1), toks, fc), BF),
            vm((max(nc - n2, 1), toks, 2 * fc), BF),
            vm((slots, half, 3 * fc), BF),
            vm((half, 3 * fc), BF),
            vm((half, 3 * fc), BF),
            vm((half, 3 * fc), BF),
            vm((half, 3 * fc), BF),
            vm((4, toks // 4, width), BF),
            vm((4, toks // 4, half), BF),
            vm((4, toks // 4, half), BF),
            vm((2, toks // 4, half), BF),
            dma((1,)),
        ]
        + [dma((rest,))] * 3
        + [dma((13,)), dma((2 * rest,)), dma((rest,))]
        + [dma((rest, zs))] * 5
        + [dma((nc,))] * 2
        + [dma((nc, zs))] * 4
        + [dma((1 + 2 * zs,)), dma((1,)), dma((nc,))],
        compiler_params=pltpu.CompilerParams(
            collective_id=0, has_side_effects=True, vmem_limit_bytes=62 * 2**20
        ),
        cost_estimate=pl.CostEstimate(
            flops=18 * toks * width * fc * nc, bytes_accessed=80 * 2**20, transcendentals=0
        ),
    )(*weights, h2, dy)
    return list(result[:3]) + list(result[7:])


def final_kernel(skip, *refs):
    refs = list(refs)
    inputs = refs[:8]
    d_hidden, g_query, g_key, g_value, g_out, g_gate, g_up, g_down, output = refs[8:17]
    bufs, sem = refs[17:24] + [output], refs[24]
    x = lax.axis_index("x")
    copies = [
        pltpu.make_async_copy(src, dst, sem.at[i])
        for i, (src, dst) in enumerate(zip(inputs, bufs))
    ]
    for copy in copies:
        copy.start()
    near, left, far, gh, s_q, s_kv, s_wo, _ = bufs
    n2, nl = near.shape[0], left.shape[0]
    half = gh.shape[1]
    fc = far.shape[2] // 3
    split = (n2 + nl) * fc
    for i in (0, 2, 1):
        copies[i].wait()
    for c in range(n2 + nl):
        own = (near[c, x] if c < n2 else left[c - n2]).astype(F32)
        other = far[c].astype(F32)
        low = jnp.where(x == 0, own, other)
        high = jnp.where(x == 0, other, own)
        for w, out in enumerate((g_gate, g_up, g_down)):
            b = high[:, w * fc : (w + 1) * fc]
            first = split - skip + c * fc
            if c == 0:
                b = b[:, skip:]
                first = split
            out[:, c * fc : (c + 1) * fc] = low[:, w * fc : (w + 1) * fc]
            out[:, first : first + b.shape[1]] = b
    for i in (3, 4, 5, 6):
        copies[i].wait()
    for i in range(2):
        d_hidden[i * half : (i + 1) * half] = gh[i].astype(F32)
    g_query[...] = s_q[...].astype(F32)
    g_key[...] = s_kv[:, :HEAD_SIZE].astype(F32)
    g_value[...] = s_kv[:, HEAD_SIZE:].astype(F32)
    g_out[...] = s_wo[...].astype(F32)
    copies[7].wait()


def final_call(skip, ff, inputs):
    rows, three = inputs[2].shape[1:]
    _, half, width = inputs[3].shape
    q_cols = inputs[4].shape[1]
    shape = jax.ShapeDtypeStruct
    any_spec = pl.BlockSpec(memory_space=pl.ANY)
    out = [
        shape((2 * half, width), F32),
        shape((rows, q_cols), F32),
        shape((rows, HEAD_SIZE), F32),
        shape((rows, HEAD_SIZE), F32),
        shape((rows, q_cols), F32),
        shape((rows, ff), F32),
        shape((rows, ff), F32),
        shape((rows, ff), F32),
        shape(inputs[7].shape, BF),
    ]
    return pl.pallas_call(
        functools.partial(final_kernel, skip),
        out_shape=out,
        in_specs=[any_spec] * len(inputs),
        out_specs=[VMEM] * 9,
        scratch_shapes=[pltpu.VMEM(v.shape, BF) for v in inputs[:7]]
        + [pltpu.SemaphoreType.DMA((8,))],
        compiler_params=pltpu.CompilerParams(vmem_limit_bytes=60 * 2**20),
    )(*inputs)


def on_device(
    hidden,
    lengths,
    norm_attn,
    w_query,
    key_weight_matrix,
    value_weight_matrix,
    b_query,
    key_bias_rows,
    value_bias_rows,
    w_out,
    norm_mlp,
    w_gate,
    w_up,
    w_down,
    cotangent,
):
    homes = lax.axis_size("batch") * lax.axis_size("z") * lax.axis_size("x")
    shards = lax.axis_size("z") * lax.axis_size("x")
    z_i, x_i = lax.axis_index("z"), lax.axis_index("x")
    me = z_i * lax.axis_size("x") + x_i
    tok = hidden.shape[1]
    width = hidden.shape[2]
    half = tok // 2
    doc_lengths = lengths[0]
    heads = b_query.shape[0]
    heads_all = heads + 2
    q_cols = heads * HEAD_SIZE
    rows = norm_attn.shape[0]
    ff = w_gate.shape[1]
    ffh = -(-ff // 512) * 256
    fc = FC
    nc = ffh // fc

    home = (lax.axis_index("batch") * lax.axis_size("z") + z_i) * 2 + x_i
    per_home = HEAD_SIZE // homes

    def spot(value):
        here = jnp.arange(homes, dtype=jnp.int32)[None, :, None] == home
        return jnp.where(here, value[:, None, :], 0).reshape(-1)

    biases = jnp.concatenate([b_query, key_bias_rows, value_bias_rows], axis=0)
    small = jnp.concatenate(
        [spot(biases), spot(norm_attn[None]), spot(norm_mlp[None])]
    ).reshape(16, -1)

    zs = lax.axis_size("z")
    n1, n2 = (zs, nc - zs) if rows % 16 == 0 and 2 * zs < nc else (0, nc)
    three = (w_gate, w_up, w_down.T)
    skip = 2 * ffh - ff

    stored = me * tok + jnp.arange(tok, dtype=jnp.int32)
    q_rows = row_positions(stored, shards, half)
    doc_start = doc_starts_of(q_rows, doc_lengths)
    cosine_table, sine_table = rotary(q_rows - doc_start, HEAD_SIZE)
    cos2 = jnp.concatenate([cosine_table, cosine_table], axis=1)
    sin2 = jnp.concatenate([-sine_table, sine_table], axis=1)
    start_row = doc_start[None, :]

    x_in = hidden[0]
    (
        h_first,
        q_mat,
        out_low,
        lse,
        mid,
        vec,
        wkv,
        wq,
        wo_t,
        kv_all,
        h2,
        dy,
        *full_one,
    ) = forward_call(
        zs,
        heads,
        n1,
        skip,
        fc,
        x_in,
        jnp.concatenate([key_weight_matrix, value_weight_matrix], axis=1),
        w_query,
        w_out.T,
        small,
        cos2,
        sin2,
        start_row,
        cotangent[0].reshape(2, half, width),
        three if n1 else (),
    )
    h2 = h2.reshape(4 * half, width)
    dy = dy.reshape(4 * half, width)
    if n1:
        mlp_w = (*three, *full_one)
    else:

        def stacked(x_at):
            halves = [
                lax.dynamic_slice_in_dim(mat, x_at * (ff - ffh), ffh, axis=1).reshape(rows, nc, fc)
                for mat in three
            ]
            return jnp.transpose(jnp.concatenate(halves, axis=2), (1, 0, 2))

        keep = stacked(x_i)
        other = lax.ppermute(stacked(1 - x_i), "x", [(0, 1), (1, 0)])
        low = jnp.where(x_i == 0, keep, other)
        high = jnp.where(x_i == 0, other, keep)
        mlp_w = (jnp.concatenate([low, high], axis=1),)
    dh2, y_sum, mlp_g, *left = mlp_call(zs, nc, n1, n2, fc, skip, mlp_w, h2, dy)
    mlp_g = mlp_g.reshape(n2, 2, rows, 3 * fc)
    left = [v.reshape(nc - n2, zs, 2 * rows, 3 * fc) for v in left]

    output, d_hidden, s_q, s_kv, s_wo, g_vec, other, *left_own = backward_call(
        zs,
        heads,
        left,
        (y_sum, mlp_g, x_in, cotangent[0]),
        (
            dh2,
            mid,
            vec,
            h_first,
            q_mat,
            out_low,
            lse[:, None],
            kv_all,
            wkv,
            wq,
            wo_t,
            cos2,
            sin2,
            start_row.reshape(2, 1, half),
        ),
    )
    g_vec = g_vec.reshape(-1)
    g_bias = lax.dynamic_slice_in_dim(
        g_vec[: heads_all * HEAD_SIZE].reshape(heads_all, HEAD_SIZE), home * per_home, per_home, 1
    )
    g_norms = g_vec[heads_all * HEAD_SIZE :].reshape(2, width)
    g_norms = lax.dynamic_slice_in_dim(g_norms, home * rows, rows, 1)

    if n1:
        grads = final_call(skip, ff, (mlp_g, *left_own, other, d_hidden, s_q, s_kv, s_wo, output))
    else:
        keep = lax.dynamic_index_in_dim(mlp_g, x_i, 1, False)
        low = jnp.where(x_i == 0, keep, other)
        high = jnp.where(x_i == 0, other, keep)

        def whole(k):
            def cols(value):
                piece = value[:, :, k * fc : (k + 1) * fc]
                return jnp.transpose(piece, (1, 0, 2)).reshape(rows, ffh)

            return jnp.concatenate([cols(low), cols(high)[:, skip:]], axis=1).astype(F32)

        grads = (
            d_hidden.astype(F32).reshape(tok, width),
            s_q.astype(F32),
            s_kv[:, :HEAD_SIZE].astype(F32),
            s_kv[:, HEAD_SIZE:].astype(F32),
            s_wo.astype(F32),
            whole(0),
            whole(1),
            whole(2),
            output,
        )
    d_hidden, g_query, g_key, g_value, g_out, g_gate, g_up, g_down, output = grads
    return (
        output.reshape(1, tok, width),
        d_hidden[None],
        g_norms[0],
        g_query,
        g_key,
        g_value,
        g_bias[:heads],
        g_bias[heads : heads + 1],
        g_bias[heads + 1 :],
        g_out.T,
        g_norms[1],
        g_gate,
        g_up,
        g_down.T,
    )


def solution(mesh):
    seq = mesh.shape["seq"]
    fine = Mesh(
        mesh.devices.reshape(mesh.shape["batch"], seq // 2, 2, mesh.shape["tensor"]),
        ("batch", "z", "x", "tensor"),
    )
    toks = P("batch", ("z", "x"), None)
    home = ("batch", "z", "x")
    down = P(home, "tensor")
    across = P("tensor", home)
    return jax.shard_map(
        on_device,
        mesh=fine,
        in_specs=(
            toks,
            P("batch", None),
            P(home),
            down,
            down,
            down,
            across,
            across,
            across,
            across,
            P(home),
            down,
            down,
            across,
            toks,
        ),
        out_specs=(
            toks,
            toks,
            P(home),
            down,
            down,
            down,
            across,
            across,
            across,
            across,
            P(home),
            down,
            down,
            across,
        ),
        check_vma=False,
    )
```

```python
import functools

import jax
import jax.numpy as jnp
from jax import lax
from jax.experimental import pallas as pl
from jax.experimental.pallas import tpu as pltpu
from jax.sharding import Mesh
from jax.sharding import PartitionSpec as P

HEAD_SIZE = 128
NORM_EPS = 1e-06
ROPE_BASE = 10000.0
MASKED = -1e30
FLOOR = -1e29
FC = 256
BF = jnp.bfloat16
F32 = jnp.float32
VMEM = pl.BlockSpec(memory_space=pltpu.VMEM)


def row_positions(stored, shards, half_rows):
    slot_id = stored // half_rows
    inner = stored % half_rows
    shard_id = slot_id // 2
    row_block = jnp.where(slot_id % 2 == 0, shard_id, 2 * shards - 1 - shard_id)
    return row_block * half_rows + inner


def doc_starts_of(row_pos, doc_lengths):
    doc_ends = jnp.cumsum(doc_lengths)
    doc_starts = doc_ends - doc_lengths
    inside = (row_pos[:, None] >= doc_starts[None, :]) & (row_pos[:, None] < doc_ends[None, :])
    return jnp.sum(jnp.where(inside, doc_starts[None, :], 0), axis=1).astype(jnp.int32)


def rotary(doc_pos, head_dim):
    half_dim = head_dim // 2
    freqs = ROPE_BASE ** (-2.0 * jnp.arange(half_dim, dtype=jnp.float32) / head_dim)
    angles = doc_pos.astype(jnp.float32)[:, None] * freqs[None, :]
    return (jnp.cos(angles), jnp.sin(angles))


def norm_factor(resid):
    return lax.rsqrt(jnp.mean(resid * resid, axis=-1, keepdims=True) + NORM_EPS)


def norm_backward(resid, factor, gain, grad_in):
    weighted = grad_in * gain
    grad_resid = factor * weighted - resid * factor**3 * jnp.mean(
        weighted * resid, axis=-1, keepdims=True
    )
    grad_gain = jnp.sum(grad_in * resid * factor, axis=0, keepdims=True)
    return (grad_resid, grad_gain)


def dot(a, b):
    return jnp.dot(a, b, preferred_element_type=F32)


def dot_nt(a, b):
    return lax.dot_general(a, b, (((1,), (1,)), ((), ())), preferred_element_type=F32)


def block_mask(sub, block, me, shards, half, start_row, heads):
    key_blk = jnp.where(sub == 0, block, 2 * shards - 1 - block)
    query_blk = jnp.where(sub == 0, me, 2 * shards - 1 - me)
    key_pos = key_blk * half + lax.broadcasted_iota(jnp.int32, (half, half), 0)
    query_pos = query_blk * half + lax.broadcasted_iota(jnp.int32, (half, half), 1)
    allowed = (key_pos <= query_pos) & (key_pos >= start_row)
    return jnp.concatenate([jnp.where(allowed, 0.0, MASKED).astype(F32)] * heads, axis=1)


def stack_heads(ref, sub, half, heads):
    return jnp.concatenate(
        [
            ref[sub * half : (sub + 1) * half, h * HEAD_SIZE : (h + 1) * HEAD_SIZE]
            for h in range(heads)
        ],
        axis=0,
    )


class Pool:
    def __init__(self, ref):
        self.ref, self.used = ref, 0

    def take(self, count=1):
        base = self.used
        self.used += count
        assert self.used <= self.ref.shape[0], self.used
        return lambda i=0: self.ref.at[base + i]


def merge_rows(value):
    homes, rows, cols = value.shape
    if rows % 16:
        return value.astype(F32).reshape(homes * rows, cols).astype(BF)
    return value.reshape(homes * rows, cols)


class Spread:
    def __init__(self, zs, src, buf, pool):
        self.zs, self.src, self.buf = zs, src, buf
        self.b, self.z, self.x = (lax.axis_index(a) for a in ("batch", "z", "x"))
        self.up_s, self.dn_s, self.z_r, self.x_s, self.x_r = (pool.take(zs) for _ in range(5))
        self.s_s, self.s_r = pool.take(2 * zs), pool.take(2 * zs)
        self.loc = pool.take()

    def at(self, b, z, x):
        return self.buf.at[(b * self.zs + z) * 2 + x]

    def up(self, s, src=None):
        dst = self.at(self.b, s, self.x)
        src = dst if src is None else src
        return remote(src, dst, self.up_s(s), self.z_r(s), {"z": self.z + 1})

    def dn(self, s, src=None):
        dst = self.at(self.b, s, self.x)
        src = dst if src is None else src
        return remote(src, dst, self.dn_s(s), self.z_r(s), {"z": self.z - 1})

    def side(self, s, src=None):
        dst = self.at(self.b, s, self.x)
        src = dst if src is None else src
        return remote(src, dst, self.x_s(s), self.x_r(s), {"x": 1 - self.x})

    def sib(self, s, far=0, src=None):
        dst = self.at(self.b, s, self.x if far == 0 else 1 - self.x)
        src = dst if src is None else src
        i = far * self.zs + s
        return remote(src, dst, self.s_s(i), self.s_r(i), {"batch": 1 - self.b})

    def local(self):
        return pltpu.make_async_copy(self.src, self.at(self.b, self.z, self.x), self.loc())

    def start(self):
        @pl.when(self.z < self.zs - 1)
        def _():
            self.up(self.z, self.src).start()

        @pl.when(self.z > 0)
        def _():
            self.dn(self.z, self.src).start()

        self.side(self.z, self.src).start()
        self.sib(self.z, 0, self.src).start()
        self.local().start()

    def hop(self, k):
        low, high = self.z - k, self.z + k

        @pl.when(low >= 0)
        def _():
            self.dn(low).wait_recv()

            @pl.when(self.z < self.zs - 1)
            def _():
                self.up(low).start()

            self.side(low).start()
            self.sib(low).start()

        @pl.when(high < self.zs)
        def _():
            self.dn(high).wait_recv()

            @pl.when(self.z > 0)
            def _():
                self.dn(high).start()

            self.side(high).start()
            self.sib(high).start()

    def cross(self):
        for s in range(self.zs):
            dst = self.at(self.b, s, 1 - self.x)
            remote(dst, dst, self.x_s(s), self.x_r(s), {"x": 1 - self.x}).wait_recv()
            self.sib(s, 1).start()

    def finish(self):
        self.local().wait()
        for far in range(2):
            for s in range(self.zs):
                dst = self.at(1 - self.b, s, self.x if far == 0 else 1 - self.x)
                i = far * self.zs + s
                remote(dst, dst, self.s_s(i), self.s_r(i), {"batch": 1 - self.b}).wait_recv()

    def drain(self):
        for s in range(self.zs):

            @pl.when((s <= self.z) & (self.z < self.zs - 1))
            def _():
                self.up(s).wait_send()

            @pl.when((s >= self.z) & (self.z > 0))
            def _():
                self.dn(s).wait_send()

            self.side(s).wait_send()
            self.sib(s, 0).wait_send()
            self.sib(s, 1).wait_send()


def lanes(vec, first, count):
    return jnp.concatenate([vec[r : r + 1, :] for r in range(first, first + count)], axis=1)


def thirds(zs):
    hops = list(range(1, zs))
    per = -(-len(hops) // 3)
    return [hops[i * per : (i + 1) * per] for i in range(3)]


def forward_kernel(
    zs,
    heads,
    n1,
    skip,
    scale,
    x_ref,
    wkv_in,
    wq_in,
    wo_in,
    small_in,
    cos_ref,
    sin_ref,
    start_ref,
    dy_in,
    *refs,
):
    refs = list(refs)
    if n1:
        mats = refs[:3]
        del refs[:3]
    h1_out, q_out, attn_out, lse_out, mid_out, vec_out = refs[:6]
    wkv_all, wq_all, wo_all, kv_all, h2_all, dy_all = refs[6:12]
    del refs[:12]
    if n1:
        full = refs.pop(0)
    small_buf, wkv_buf, wq_buf, wo_buf, kv_buf, q_t, acc_ref, max_ref, sum_ref = refs[:9]
    att_send, att_recv, h2_half, xn_ref, sem_ref, dy_buf = refs[9:15]
    mat_bufs = refs[15:18] if n1 else []
    g_sems = refs[15 + len(mat_bufs) :]
    b, z, x, t = (lax.axis_index(a) for a in ("batch", "z", "x", "tensor"))
    shards = 2 * zs
    me = 2 * z + x
    tok, width = x_ref.shape
    half = tok // 2
    q_cols = heads * HEAD_SIZE
    pool = Pool(sem_ref)
    late = [(dy_in, dy_buf)] + (list(zip(mats, mat_bufs)) if n1 else [])
    late_sem = pool.take(len(late))
    loads = [
        pltpu.make_async_copy(src, dst, late_sem(i)) for i, (src, dst) in enumerate(late)
    ]
    for copy in loads[1:] + loads[:1]:
        copy.start()
    greet(z, zs)

    small = Spread(zs, small_in, small_buf, pool)
    wkv = Spread(zs, wkv_in, wkv_buf, pool)
    wq = Spread(zs, wq_in, wq_buf, pool)
    wo = Spread(zs, wo_in, wo_buf, pool)
    small.start()
    wkv.start()
    wq.start()

    runs = thirds(zs)
    if n1:
        trade = Exchange(mat_bufs, full, 0, zs, skip, [pool.take(n1) for _ in range(3)])
        gather = Gather(zs, None, full, [None] + list(g_sems))

    def ship(first, last):
        if n1:
            for c in range(first, last):
                trade.ship(c, c)

    def prefetch(tick):
        if n1:
            for c in range(n1):
                hops = [k for k in range(1, zs) if min(k, 3) == tick - c]
                if tick == c:
                    trade.arrived(c, c)
                    gather.start(c)
                for k in hops:
                    gather.hop(c, k)

    quarter = half // 2
    dy_l, dyy_s, dyy_r = (pool.take() for _ in range(3))
    dyx_s, dyx_r = pool.take(3), pool.take(3)
    dy_own = pltpu.make_async_copy(dy_buf, dy_all.at[pl.ds(2 * x, 2)], dy_l())

    def dy_side(i):
        rows = pl.ds((i % 3 > 0) * quarter, quarter)
        block = t if i < 2 else 1 - t
        dst = dy_all.at[2 * x + block, rows]
        return remote(dy_buf.at[block, rows], dst, dyx_s(i), dyx_r(i), {"x": 1 - x})

    dy_piece = dy_all.at[2 * (1 - x) + t, pl.ds(0, quarter)]
    dy_across = remote(dy_piece, dy_piece, dyy_s(), dyy_r(), {"tensor": 1 - t})

    for m in range(2):
        at = slice(m * half, (m + 1) * half)
        xv = x_ref[at].astype(F32)
        xn_ref[at] = xv * norm_factor(xv)
    for copy in loads:
        copy.wait()
    dy_own.start()
    if n1:
        for c in range(n1):
            trade.keep(c, c)
    for k in range(1, zs):
        small.hop(k)
        wkv.hop(k)
        if k == 1:
            ship(0, 1)
    for k in runs[0]:
        wq.hop(k)
    wo.start()
    prefetch(0)
    small.cross()
    small.finish()
    vec = jnp.sum(small_buf[...].astype(F32), axis=0)
    vec_out[...] = vec
    bias = lanes(vec, 0, 4)
    gain_attn = lanes(vec, 4, 6)
    gain_mlp = lanes(vec, 10, 6)
    for m in range(2):
        at = slice(m * half, (m + 1) * half)
        h1_out[at] = (xn_ref[at] * gain_attn).astype(BF)

    def turned(value, at):
        return value * cos_ref[at] + pltpu.roll(value, HEAD_SIZE // 2, 1) * sin_ref[at]

    wkv.cross()
    ship(1, 2)
    wkv.finish()
    for k in runs[1]:
        wq.hop(k)
    wkv_m = merge_rows(wkv_buf[...])
    for m in range(2):
        at = slice(m * half, (m + 1) * half)
        lin = dot(h1_out[at], wkv_m) + bias[:, q_cols:]
        kv_buf[me + m, :, :HEAD_SIZE] = turned(lin[:, :HEAD_SIZE], at).astype(BF)
        kv_buf[me + m, :, HEAD_SIZE:] = lin[:, HEAD_SIZE:].astype(BF)

    ku_s, kd_s, k0_r, k1_r, x0_s, x1_s, x0_r, x1_r = (pool.take(zs) for _ in range(8))

    def kv_up(s):
        piece = kv_buf.at[2 * s + x]
        return remote(piece, piece, ku_s(s), k0_r(s), {"z": z + 1})

    def kv_dn(s):
        piece = kv_buf.at[2 * s + x + 1]
        return remote(piece, piece, kd_s(s), k1_r(s), {"z": z - 1})

    def kv_side(s, sub, col):
        piece = kv_buf.at[2 * s + col + sub]
        send, recv = (x0_s, x0_r) if sub == 0 else (x1_s, x1_r)
        return remote(piece, piece, send(s), recv(s), {"x": 1 - x})

    def kv_hop(k):
        low, high = z - k, z + k

        @pl.when(low >= 0)
        def _():
            kv_up(low).wait_recv()

            @pl.when(z < zs - 1)
            def _():
                kv_up(low).start()

            kv_side(low, 0, x).start()

        @pl.when(high < zs)
        def _():
            kv_dn(high).wait_recv()

            @pl.when(z > 0)
            def _():
                kv_dn(high).start()

            kv_side(high, 1, x).start()

    @pl.when(z < zs - 1)
    def _():
        kv_up(z).start()

    @pl.when(z > 0)
    def _():
        kv_dn(z).start()

    @pl.when(x == 0)
    def _():
        kv_side(z, 0, x).start()

    @pl.when(x == 1)
    def _():
        kv_side(z, 1, x).start()

    for k in runs[2]:
        wq.hop(k)
    for k in runs[0]:
        wo.hop(k)
    for k in runs[0]:
        kv_hop(k)
    wq.cross()
    for k in runs[1]:
        kv_hop(k)
    for k in runs[1]:
        wo.hop(k)
    ship(2, 3)
    prefetch(1)
    wq.finish()
    wq_m = merge_rows(wq_buf[...])
    for m in range(2):
        at = slice(m * half, (m + 1) * half)
        lin = dot(h1_out[at], wq_m) + bias[:, :q_cols]
        for h in range(heads):
            cols = slice(h * HEAD_SIZE, (h + 1) * HEAD_SIZE)
            q_out[at, cols] = turned(lin[:, cols], at).astype(BF)
    for sub in range(2):
        q_t[sub] = stack_heads(q_out, sub, half, heads).T
    acc_ref[...] = jnp.zeros_like(acc_ref)
    max_ref[...] = jnp.full_like(max_ref, FLOOR)
    sum_ref[...] = jnp.zeros_like(sum_ref)

    def fold(sub, block):
        keys = kv_buf[block + sub, :, :HEAD_SIZE]
        vals = kv_buf[block + sub, :, HEAD_SIZE:]
        start_row = start_ref[:, sub * half : (sub + 1) * half]
        scores = dot(keys, q_t[sub]) * scale + block_mask(
            sub, block, me, shards, half, start_row, heads
        )
        old_max = max_ref[sub]
        new_max = jnp.maximum(old_max, jnp.max(scores, axis=0, keepdims=True))
        weights = jnp.exp(scores - new_max)
        shrink = jnp.exp(old_max - new_max)
        max_ref[sub] = new_max
        sum_ref[sub] = sum_ref[sub] * shrink + jnp.sum(weights, axis=0, keepdims=True)
        acc_ref[sub] = acc_ref[sub] * shrink + dot(vals.T, weights.astype(BF))

    def attend(k, carry):
        low, high = z - k, z + k

        @pl.when((low >= 0) & (k < zs))
        def _():
            fold(0, 2 * low + x)

        @pl.when((high < zs) & (k < zs))
        def _():
            fold(1, 2 * high + x)

        far_low, far_high = low + 1, high - 1

        @pl.when((k > 0) & (far_low >= 0) & ((k > 1) | (x == 1)))
        def _():
            kv_side(far_low, 0, 1 - x).wait_recv()
            fold(0, 2 * far_low + 1 - x)

        @pl.when((k > 0) & (far_high < zs) & ((k > 1) | (x == 0)))
        def _():
            kv_side(far_high, 1, 1 - x).wait_recv()
            fold(1, 2 * far_high + 1 - x)

        @pl.when(k == 0)
        def _():
            for hop in runs[2]:
                kv_hop(hop)

        @pl.when(k == 1)
        def _():
            for hop in runs[2]:
                wo.hop(hop)

        @pl.when(k == 2)
        def _():
            dy_side(1).start()

        @pl.when(k == zs - 1)
        def _():
            prefetch(2)

        return carry

    lax.fori_loop(0, zs + 1, attend, 0)
    dy_side(0).start()
    ship(3, n1)
    wo.cross()
    for sub in range(2):
        lse_out[sub : sub + 1, :] = max_ref[sub] + jnp.log(sum_ref[sub])
        out_t = acc_ref[sub] / sum_ref[sub]
        for h in range(heads):
            attn_out[sub * half : (sub + 1) * half, h * HEAD_SIZE : (h + 1) * HEAD_SIZE] = (
                out_t[:, h * half : (h + 1) * half].T.astype(BF)
            )

    wo.finish()
    att_s, att_r = pool.take(2), pool.take(2)
    h_l, hx_s, hx_r, hy_s, hy_r = (pool.take(2) for _ in range(5))
    hxx_s, hxx_r, hyy_s, hyy_r = (pool.take() for _ in range(4))

    def rows(i):
        return pl.ds(i * quarter, quarter)

    def att_copy(i):
        to = {"tensor": 1 - t}
        return remote(att_send.at[rows(i)], att_recv.at[rows(i)], att_s(i), att_r(i), to)

    def h_copies(i):
        src, dst = h2_half.at[rows(i)], h2_all.at[2 * x + t, rows(i)]
        return (
            pltpu.make_async_copy(src, dst, h_l(i)),
            remote(src, dst, hx_s(i), hx_r(i), {"x": 1 - x}),
            remote(src, dst, hy_s(i), hy_r(i), {"tensor": 1 - t}),
        )

    wo_m = merge_rows(wo_buf[...])
    for i in range(2):
        at = pl.ds(pl.multiple_of((1 - t) * half + i * quarter, quarter), quarter)
        att_send[rows(i)] = dot_nt(attn_out[at], wo_m).astype(BF)
        att_copy(i).start()
    for i in range(2):
        at = pl.ds(pl.multiple_of(t * half + i * quarter, quarter), quarter)
        mid_out[rows(i)] = dot_nt(attn_out[at], wo_m) + x_ref[at].astype(F32)
    prefetch(3)
    for i in range(2):
        att_copy(i).wait_recv()
        mid = mid_out[rows(i)] + att_recv[rows(i)].astype(F32)
        mid_out[rows(i)] = mid
        h2_half[rows(i)] = (mid * norm_factor(mid) * gain_mlp).astype(BF)
        for copy in h_copies(i):
            copy.start()
    from_side = h2_all.at[2 * (1 - x) + t, rows(0)]
    from_across = h2_all.at[2 * x + 1 - t, rows(1)]
    relay_across = remote(from_side, from_side, hyy_s(), hyy_r(), {"tensor": 1 - t})
    relay_side = remote(from_across, from_across, hxx_s(), hxx_r(), {"x": 1 - x})
    dy_side(2).start()
    h_copies(0)[1].wait_recv()
    relay_across.start()
    prefetch(4)
    h_copies(1)[2].wait_recv()
    relay_side.start()
    dy_side(0).wait_recv()
    dy_across.start()
    for tick in range(5, n1 + 3):
        prefetch(tick)

    save = pool.take(4)
    saves = [
        pltpu.make_async_copy(src, dst, save(i))
        for i, (src, dst) in enumerate(
            ((wkv_buf, wkv_all), (wq_buf, wq_all), (wo_buf, wo_all), (kv_buf, kv_all))
        )
    ]
    for copy in saves:
        copy.start()

    for item in (small, wkv, wq, wo):
        item.drain()

    def kv_drain(s, carry):
        @pl.when((s <= z) & (z < zs - 1))
        def _():
            kv_up(s).wait_send()

        @pl.when((s >= z) & (z > 0))
        def _():
            kv_dn(s).wait_send()

        @pl.when((s < z) | ((s == z) & (x == 0)))
        def _():
            kv_side(s, 0, x).wait_send()

        @pl.when((s > z) | ((s == z) & (x == 1)))
        def _():
            kv_side(s, 1, x).wait_send()

        return carry

    lax.fori_loop(0, zs, kv_drain, 0)
    relay_across.wait()
    relay_side.wait()
    dy_across.wait()
    for i in range(3):
        dy_side(i).wait_send()
        if i > 0:
            dy_side(i).wait_recv()
    for i in range(2):
        att_copy(i).wait_send()
        own, side, across = h_copies(i)
        own.wait()
        side.wait_send()
        across.wait_send()
    h_copies(1)[1].wait_recv()
    h_copies(0)[2].wait_recv()
    if n1:
        for c in range(n1):
            trade.sent(c, c)
            gather.finish(c)
            gather.drain(c)
    for copy in saves + [dy_own]:
        copy.wait()


def forward_call(
    zs, heads, n1, skip, fc, x_in, wkv_in, wq_in, wo_in, small_in, cos, sin, start, dy_in, first
):
    tok, width = x_in.shape
    half = tok // 2
    homes = 4 * zs
    rows, q_cols = wq_in.shape
    shape = jax.ShapeDtypeStruct
    any_spec = pl.BlockSpec(memory_space=pl.ANY)
    out = [
        shape((tok, width), BF),
        shape((tok, q_cols), BF),
        shape((tok, q_cols), BF),
        shape((2, heads * half), F32),
        shape((half, width), F32),
        shape(small_in.shape, F32),
        shape((homes, rows, 2 * HEAD_SIZE), BF),
        shape((homes, rows, q_cols), BF),
        shape((homes, rows, q_cols), BF),
        shape((2 * zs + 1, half, 2 * HEAD_SIZE), BF),
        shape((4, half, width), BF),
        shape((4, half, width), BF),
    ]
    sems = [pltpu.SemaphoreType.DMA((4 * (9 * zs + 1) + 8 * zs + 3 * n1 + 44,))]
    sems += [pltpu.VMEM(v.shape, BF) for v in (dy_in, *first)]
    if n1:
        out.append(shape((n1, width, 3 * fc), BF))
        sems += [pltpu.SemaphoreType.DMA((n1, zs))] * 5
    return pl.pallas_call(
        functools.partial(forward_kernel, zs, heads, n1, skip, HEAD_SIZE ** (-0.5)),
        out_shape=out,
        in_specs=[VMEM] + [any_spec] * 4 + [VMEM] * 3 + [any_spec] * (1 + len(first)),
        out_specs=[VMEM] * 6 + [any_spec] * (len(out) - 6),
        scratch_shapes=[
            pltpu.VMEM((homes,) + small_in.shape, BF),
            pltpu.VMEM((homes, rows, 2 * HEAD_SIZE), BF),
            pltpu.VMEM((homes, rows, q_cols), BF),
            pltpu.VMEM((homes, rows, q_cols), BF),
            pltpu.VMEM((2 * zs + 1, half, 2 * HEAD_SIZE), BF),
            pltpu.VMEM((2, HEAD_SIZE, heads * half), BF),
            pltpu.VMEM((2, HEAD_SIZE, heads * half), F32),
            pltpu.VMEM((2, 1, heads * half), F32),
            pltpu.VMEM((2, 1, heads * half), F32),
            pltpu.VMEM((half, width), BF),
            pltpu.VMEM((half, width), BF),
            pltpu.VMEM((half, width), BF),
            pltpu.VMEM((tok, width), F32),
        ]
        + sems,
        compiler_params=pltpu.CompilerParams(
            collective_id=1, has_side_effects=True, vmem_limit_bytes=60 * 2**20
        ),
        cost_estimate=pl.CostEstimate(
            flops=4 * tok * width * (q_cols + HEAD_SIZE) + 2**31,
            bytes_accessed=32 * 2**20,
            transcendentals=0,
        ),
    )(x_in, wkv_in, wq_in, wo_in, small_in, cos, sin, start, dy_in, *first)


class Square:
    def __init__(self, src, own, r_one, r_two, pool):
        self.src, self.own, self.r_one, self.r_two = src, own, r_one, r_two
        self.x, self.t = lax.axis_index("x"), lax.axis_index("tensor")
        self.cut = src.shape[2] // 2
        self.one_s, self.one_r = pool.take(3), pool.take(3)
        self.two_s, self.two_r = pool.take(2), pool.take(2)
        self.load = pool.take(3)

    def first(self):
        x, t, cut, src = self.x, self.t, self.cut, self.src
        left, right = pl.ds(0, cut), pl.ds(cut, cut)
        sends = [
            remote(
                src.at[pl.ds(2 * (1 - x), 2), :, left],
                self.r_one.at[pl.ds(0, 2)],
                self.one_s(0),
                self.one_r(0),
                {"x": 1 - x},
            )
        ]
        for i in range(2):
            sends.append(
                remote(
                    src.at[2 * i + 1 - t, :, right],
                    self.r_one.at[2 + i],
                    self.one_s(1 + i),
                    self.one_r(1 + i),
                    {"tensor": 1 - t},
                )
            )
        return sends

    def loads(self):
        x, t, cut, src = self.x, self.t, self.cut, self.src
        left, right = pl.ds(0, cut), pl.ds(cut, cut)
        loads = [
            pltpu.make_async_copy(
                src.at[pl.ds(2 * x, 2), :, left], self.own.at[pl.ds(0, 2)], self.load(0)
            )
        ]
        for i in range(2):
            loads.append(
                pltpu.make_async_copy(
                    src.at[2 * i + t, :, right], self.own.at[2 + i], self.load(1 + i)
                )
            )
        return loads

    def second(self):
        x, t = self.x, self.t
        return [
            remote(
                self.own.at[1 - t],
                self.r_two.at[0],
                self.two_s(0),
                self.two_r(0),
                {"tensor": 1 - t},
            ),
            remote(
                self.own.at[3 - x],
                self.r_two.at[1],
                self.two_s(1),
                self.two_r(1),
                {"x": 1 - x},
            ),
        ]

    def start(self):
        for copy in self.first() + self.loads():
            copy.start()

    def turn(self):
        for copy in self.loads():
            copy.wait()
        for copy in self.first():
            copy.wait_recv()
        for i in range(4):
            self.own[i] = self.own[i] + self.r_one[i]
        for copy in self.second():
            copy.start()

    def result(self):
        for copy in self.second():
            copy.wait_recv()
        left = self.own[self.t].astype(F32) + self.r_two[0].astype(F32)
        right = self.own[2 + self.x].astype(F32) + self.r_two[1].astype(F32)
        return jnp.concatenate([left, right], axis=1)

    def drain(self):
        for copy in self.first() + self.second():
            copy.wait_send()


class Collect:
    def __init__(self, zs, acc, to_sib, r_sib, r_x, r_z, out, pool):
        self.zs, self.acc, self.to_sib, self.r_sib = zs, acc, to_sib, r_sib
        self.r_x, self.r_z, self.out = r_x, r_z, out
        self.b, self.z, self.x = (lax.axis_index(a) for a in ("batch", "z", "x"))
        self.s_s, self.s_r, self.x_s, self.x_r, self.loc = (pool.take() for _ in range(5))
        self.d_s, self.d_r, self.u_s, self.u_r = (pool.take(zs) for _ in range(4))

    def sib(self):
        return remote(self.to_sib, self.r_sib, self.s_s(), self.s_r(), {"batch": 1 - self.b})

    def side(self):
        return remote(
            self.acc.at[1 - self.x], self.r_x, self.x_s(), self.x_r(), {"x": 1 - self.x}
        )

    def dn(self, h):
        return remote(
            self.acc.at[self.x, h], self.r_z.at[h], self.d_s(h), self.d_r(h), {"z": self.z - 1}
        )

    def up(self, h):
        return remote(
            self.acc.at[self.x, h], self.r_z.at[h + 1], self.u_s(h), self.u_r(h), {"z": self.z + 1}
        )

    def fill(self, make):
        rows = self.acc.shape[2]
        for buf, core in ((self.to_sib, 1 - self.b), (self.acc, self.b)):
            value = make(core)
            for h in range(self.zs):
                for col in range(2):
                    i = 2 * h + col
                    buf[col, h] = value[i * rows : (i + 1) * rows].astype(BF)
            if buf is self.to_sib:
                self.sib().start()

    def add(self, dst, src):
        dst[...] = dst[...] + src[...]

    def after_sib(self):
        self.sib().wait_recv()

        def one(h, carry):
            self.add(self.acc.at[1 - self.x, h], self.r_sib.at[1 - self.x, h])
            return carry

        lax.fori_loop(0, self.zs, one, 0)
        self.side().start()

        def other(h, carry):
            self.add(self.acc.at[self.x, h], self.r_sib.at[self.x, h])
            return carry

        lax.fori_loop(0, self.zs, other, 0)

    def after_side(self):
        self.side().wait_recv()

        def one(h, carry):
            self.add(self.acc.at[self.x, h], self.r_x.at[h])
            return carry

        lax.fori_loop(0, self.zs, one, 0)

        def ends(h, carry):
            @pl.when((self.z == self.zs - 1) & (h < self.z))
            def _():
                self.dn(h).start()

            @pl.when((self.z == 0) & (h > 0))
            def _():
                self.up(h).start()

            return carry

        lax.fori_loop(0, self.zs, ends, 0)

    def step(self, k):
        def one(i, carry):
            @pl.when((self.z == self.zs - 1 - k) & (i <= self.z))
            def _():
                self.dn(i).wait_recv()
                self.add(self.acc.at[self.x, i], self.r_z.at[i])

                @pl.when(i < self.z)
                def _():
                    self.dn(i).start()

            j = self.zs - 1 - i

            @pl.when((self.z == k) & (j >= self.z))
            def _():
                self.up(j).wait_recv()
                self.add(self.acc.at[self.x, j], self.r_z.at[j + 1])

                @pl.when(j > self.z)
                def _():
                    self.up(j).start()

            return carry

        lax.fori_loop(0, self.zs, one, 0)
        if k == self.zs - 1:
            self.result().start()

    def result(self):
        return pltpu.make_async_copy(self.acc.at[self.x, self.z], self.out, self.loc())

    def drain(self):
        self.sib().wait_send()
        self.side().wait_send()
        self.result().wait()

        def one(h, carry):
            @pl.when(h < self.z)
            def _():
                self.dn(h).wait_send()

            @pl.when(h > self.z)
            def _():
                self.up(h).wait_send()

            return carry

        lax.fori_loop(0, self.zs, one, 0)


class LineSum:
    def __init__(self, zs, acc, r_z, pool):
        self.zs, self.acc, self.r_z = zs, acc, r_z
        self.z = lax.axis_index("z")
        self.d_s, self.d_r, self.u_s, self.u_r = (pool.take(zs) for _ in range(4))

    def dn(self, h):
        to = {"z": self.z - 1}
        return remote(self.acc.at[:, h], self.r_z.at[:, h], self.d_s(h), self.d_r(h), to)

    def up(self, h):
        to = {"z": self.z + 1}
        return remote(self.acc.at[:, h], self.r_z.at[:, h + 1], self.u_s(h), self.u_r(h), to)

    def start(self):
        for h in range(self.zs):
            if h < self.zs - 1:

                @pl.when(self.z == self.zs - 1)
                def _():
                    self.dn(h).start()

            if h > 0:

                @pl.when(self.z == 0)
                def _():
                    self.up(self.zs - h).start()

    def plus(self, h, slot):
        for c in range(self.acc.shape[0]):
            self.acc[c, h] = self.acc[c, h] + self.r_z[c, slot]

    def step(self, k):
        def one(i, carry):
            @pl.when((self.z == self.zs - 1 - k) & (i <= self.z))
            def _():
                self.dn(i).wait_recv()
                self.plus(i, i)

                @pl.when(i < self.z)
                def _():
                    self.dn(i).start()

            j = self.zs - 1 - i

            @pl.when((self.z == k) & (j >= self.z))
            def _():
                self.up(j).wait_recv()
                self.plus(j, j + 1)

                @pl.when(j > self.z)
                def _():
                    self.up(j).start()

            return carry

        lax.fori_loop(0, self.zs, one, 0)

    def drain(self):
        def one(h, carry):
            @pl.when(h < self.z)
            def _():
                self.dn(h).wait_send()

            @pl.when(h > self.z)
            def _():
                self.up(h).wait_send()

            return carry

        lax.fori_loop(0, self.zs, one, 0)


def backward_kernel(zs, heads, nl, scale, *refs):
    refs = list(refs)

    def take(count):
        out = refs[:count]
        del refs[:count]
        return out

    y_in, g_mlp, x_in, dy_in = take(4)
    if nl:
        (left_in,) = take(1)
    late_in = take(7)
    dh2_ref, mid_ref, vec_ref, lse_ref, cos_ref, sin_ref, start_ref = take(7)
    out_all, gh_all, g_q, g_kv, g_wo, g_vec, g_far = take(7)
    if nl:
        (left_out,) = take(1)
    y_own, y_one, y_two, dmid_ref, dat_ref, half_ref = take(6)
    q_s, do_s, q_t, do_t, delta_ref = take(5)
    dkv_ref, rx_ref, rz_ref, acc_ref, dqkv_ref, dh_send, dh_recv = take(7)
    bufs_q, bufs_kv, bufs_wo = take(5), take(5), take(5)
    vec_own, vec_recv, vec_z, x_ref, dy_ref, sem_ref = take(6)
    late = take(7)
    h1_ref, q_ref, attn_ref, kv_ref, wkv_ref, wq_ref, wo_ref = late
    if nl:
        left_acc, left_z = take(2)

    b, z, x, t = (lax.axis_index(a) for a in ("batch", "z", "x", "tensor"))
    shards = 2 * zs
    me = 2 * z + x
    half, width = mid_ref.shape
    q_cols = heads * HEAD_SIZE
    pool = Pool(sem_ref)
    late_sem = pool.take(7)
    loads = [
        pltpu.make_async_copy(src, dst, late_sem(i))
        for i, (src, dst) in enumerate(zip(late_in, late))
    ]
    for i in (6, 2, 1, 3, 0, 5, 4):
        loads[i].start()
    greet(z, zs)

    sq_y = Square(y_in, y_own, y_one, y_two, pool)
    col_q = Collect(zs, *bufs_q, g_q, pool)
    col_kv = Collect(zs, *bufs_kv, g_kv, pool)
    col_wo = Collect(zs, *bufs_wo, g_wo, pool)
    runs = thirds(zs)
    mine = pl.ds(pl.multiple_of(t * half, half), half)
    fetch = pool.take(2)
    x_load = pltpu.make_async_copy(x_in.at[mine], x_ref, fetch(0))
    dy_load = pltpu.make_async_copy(dy_in.at[mine], dy_ref, fetch(1))
    x_load.start()
    dy_load.start()
    if nl:
        lines = [
            LineSum(zs, left_acc.at[pl.ds(c, 1)], left_z.at[pl.ds(c, 1)], pool) for c in range(nl)
        ]
        left_l = pool.take()
        left_load = pltpu.make_async_copy(left_in, left_acc, left_l())
        left_load.start()

    def line_tick(tick):
        for c in range(nl):
            if tick == c:
                lines[c].start()
            for k in range(1, zs):
                if min(k, 3) == tick - c:
                    lines[c].step(k)

    vec = vec_ref[...]
    gain_attn = lanes(vec, 4, 6)
    gain_mlp = lanes(vec, 10, 6)

    mid = mid_ref[...]
    d_norm, g_norm_mlp = norm_backward(mid, norm_factor(mid), gain_mlp, dh2_ref[...])
    dy_load.wait()
    dmid_ref[...] = dy_ref[...].astype(F32) + d_norm
    dat_ref[t] = dmid_ref[...].astype(BF)
    dat_s, dat_r = pool.take(), pool.take()

    def dat_copy(i):
        return remote(dat_ref.at[i], dat_ref.at[i], dat_s(), dat_r(), {"tensor": 1 - t})

    dat_copy(t).start()
    if nl:
        left_load.wait()
        line_tick(0)
    sq_y.start()

    x0_s, x0_r, x1_s, x1_r = (pool.take(zs) for _ in range(4))
    c0_s, c0_r, c1_s, c1_r = (pool.take(zs) for _ in range(4))

    def side(s, sub):
        src = dkv_ref.at[2 * s + 1 - x + sub]
        send, recv = (x0_s, x0_r) if sub == 0 else (x1_s, x1_r)
        return remote(src, rx_ref.at[s + sub], send(s), recv(s), {"x": 1 - x})

    def chain(s, sub):
        src = dkv_ref.at[2 * s + x + sub]
        send, recv = (c0_s, c0_r) if sub == 0 else (c1_s, c1_r)
        to = z - 1 if sub == 0 else z + 1
        return remote(src, rz_ref.at[s + sub], send(s), recv(s), {"z": to})

    acc_ref[...] = jnp.zeros_like(acc_ref)
    for i in (6, 2, 1, 3):
        loads[i].wait()

    def prepare(sub):
        d_out = dot(dat_ref[sub], merge_rows(wo_ref[...])).astype(BF)
        rows = pl.ds(pl.multiple_of(sub * half, half), half)
        out = attn_ref[rows]
        q = q_ref[rows]
        for h in range(heads):
            cols = slice(h * HEAD_SIZE, (h + 1) * HEAD_SIZE)
            at = slice(h * half, (h + 1) * half)
            q_s[sub, at] = q[:, cols]
            do_s[sub, at] = d_out[:, cols]
            q_t[sub, :, at] = q[:, cols].T
            do_h = d_out[:, cols].T
            do_t[sub, :, at] = do_h
            delta_ref[sub, :, at] = jnp.sum(
                do_h.astype(F32) * out[:, cols].T.astype(F32), axis=0, keepdims=True
            )

    def fold(sub, block):
        slot = block + sub
        keys = kv_ref[slot, :, :HEAD_SIZE]
        vals = kv_ref[slot, :, HEAD_SIZE:]
        scores = dot(keys, q_t[sub]) * scale + block_mask(
            sub, block, me, shards, half, start_ref[sub], heads
        )
        probs = jnp.exp(scores - lse_ref[sub])
        d_scores = (probs * (dot(vals, do_t[sub]) - delta_ref[sub])).astype(BF)
        dkv_ref[slot, :, HEAD_SIZE:] = dot(probs.astype(BF), do_s[sub]).astype(BF)
        dkv_ref[slot, :, :HEAD_SIZE] = (dot(d_scores, q_s[sub]) * scale).astype(BF)
        acc_ref[sub] += dot(keys.T, d_scores)

    def far_blocks(sub):
        def one(k, carry):
            s = jnp.where(sub == 0, z - k, z + k)

            @pl.when(in_range(s, zs) & ((k > 0) | (x != sub)))
            def _():
                fold(sub, 2 * s + 1 - x)

                @pl.when(sub == 0)
                def _():
                    side(s, 0).start()

                @pl.when(sub == 1)
                def _():
                    side(s, 1).start()

            return carry

        lax.fori_loop(0, zs, one, 0)

    def near_blocks(sub):
        def one(i, carry):
            k = zs - 1 - i
            s = jnp.where(sub == 0, z - k, z + k)

            @pl.when(in_range(s, zs))
            def _():
                fold(sub, 2 * s + x)

            return carry

        lax.fori_loop(0, zs, one, 0)

    def tokens(i, carry):
        sub = jnp.where(i == 0, t, 1 - t)

        @pl.when(i == 1)
        def _():
            line_tick(1)
            dat_copy(1 - t).wait_recv()

        prepare(sub)
        far_blocks(sub)
        near_blocks(sub)
        return carry

    lax.fori_loop(0, 2, tokens, 0)

    def wo_part(core):
        rows = width // 2
        at = pl.ds(pl.multiple_of(core * rows, rows), rows)
        return dot(half_ref[at], attn_ref[...])

    def plus(slot, src):
        dkv_ref[slot] = dkv_ref[slot] + src[...]

    def kv_begin():
        def one(i, carry):
            j = zs - 1 - i

            @pl.when((i < z) | ((i == z) & (x == 0)))
            def _():
                side(i, 0).wait_recv()
                plus(2 * i + x, rx_ref.at[i])

            @pl.when((z == zs - 1) & (i < z))
            def _():
                chain(i, 0).start()

            @pl.when((j > z) | ((j == z) & (x == 1)))
            def _():
                side(j, 1).wait_recv()
                plus(2 * j + x + 1, rx_ref.at[j + 1])

            @pl.when((z == 0) & (j > z))
            def _():
                chain(j, 1).start()

            return carry

        lax.fori_loop(0, zs, one, 0)

    def kv_step(k):
        def one(i, carry):
            j = zs - 1 - i

            @pl.when((z == zs - 1 - k) & (i <= z))
            def _():
                chain(i, 0).wait_recv()
                plus(2 * i + x, rz_ref.at[i])

                @pl.when(i < z)
                def _():
                    chain(i, 0).start()

            @pl.when((z == k) & (j >= z))
            def _():
                chain(j, 1).wait_recv()
                plus(2 * j + x + 1, rz_ref.at[j + 1])

                @pl.when(j > z)
                def _():
                    chain(j, 1).start()

            return carry

        lax.fori_loop(0, zs, one, 0)

    kv_begin()
    for i in range(2):
        half_ref[:, i * half : (i + 1) * half] = dat_ref[i].T
    col_wo.fill(wo_part)
    sq_y.turn()
    for k in runs[0] + runs[1]:
        kv_step(k)
    line_tick(2)
    col_wo.after_sib()

    def back(v, at):
        return v * cos_ref[at] - pltpu.roll(v, HEAD_SIZE // 2, 1) * sin_ref[at]

    for sub in range(2):
        at = slice(sub * half, (sub + 1) * half)
        for h in range(heads):
            v = acc_ref[sub, :, h * half : (h + 1) * half].T * scale
            dqkv_ref[at, h * HEAD_SIZE : (h + 1) * HEAD_SIZE] = back(v, at).astype(BF)
    loads[0].wait()
    half_ref[...] = h1_ref[...].T
    for k in runs[2]:
        kv_step(k)

    def part(first, last):
        def make(core):
            rows = width // 2
            at = pl.ds(pl.multiple_of(core * rows, rows), rows)
            return dot(half_ref[at], dqkv_ref[:, first:last])

        return make

    for sub in range(2):
        at = slice(sub * half, (sub + 1) * half)
        dk = dkv_ref[me + sub, :, :HEAD_SIZE].astype(F32)
        dqkv_ref[at, q_cols : q_cols + HEAD_SIZE] = back(dk, at).astype(BF)
        dqkv_ref[at, q_cols + HEAD_SIZE :] = dkv_ref[me + sub, :, HEAD_SIZE:]

    dh_s, dh_r = pool.take(), pool.take()
    dh_copy = remote(dh_send, dh_recv, dh_s(), dh_r(), {"tensor": 1 - t})
    theirs = pl.ds(pl.multiple_of((1 - t) * half, half), half)
    own = pl.ds(pl.multiple_of(t * half, half), half)
    loads[4].wait()
    loads[5].wait()

    def d_first(at):
        q_part = dot_nt(dqkv_ref[at, :q_cols], merge_rows(wq_ref[...]))
        return q_part + dot_nt(dqkv_ref[at, q_cols:], merge_rows(wkv_ref[...]))

    dh_send[...] = d_first(theirs).astype(BF)
    dh_copy.start()
    col_kv.fill(part(q_cols, q_cols + 2 * HEAD_SIZE))
    col_q.fill(part(0, q_cols))
    line_tick(3)
    col_kv.after_sib()
    col_wo.after_side()
    col_q.after_sib()
    dh1 = d_first(own)

    dh_copy.wait_recv()
    dh1 = dh1 + dh_recv[...].astype(F32)
    x_load.wait()
    xv = x_ref[...].astype(F32)
    d_norm, g_norm_attn = norm_backward(xv, norm_factor(xv), gain_attn, dh1)

    g_bias = jnp.sum(dqkv_ref[...].astype(F32), axis=0, keepdims=True)
    row = jnp.concatenate([g_bias, g_norm_attn, g_norm_mlp], axis=1)
    lane = vec_ref.shape[1]
    vec_own[...] = jnp.concatenate(
        [row[:, i * lane : (i + 1) * lane] for i in range(vec_ref.shape[0])], axis=0
    )
    v_s, v_r = pool.take(3), pool.take(3)
    vz_s, vz_r = pool.take(zs), pool.take(zs)
    norms = (lax.broadcasted_iota(jnp.int32, vec_ref.shape, 0) >= 4).astype(F32)

    def v_side(i):
        axis, index = (("tensor", t), ("x", x), ("batch", b))[i]
        return remote(vec_own, vec_recv.at[i], v_s(i), v_r(i), {axis: 1 - index})

    def v_add(i):
        v_side(i).wait()
        other = vec_recv[i]
        vec_own[...] = vec_own[...] + (other * norms if i == 0 else other)

    v_side(0).start()
    dat_copy(t).wait_send()
    dat_ref[t] = (dmid_ref[...] + d_norm).astype(BF)
    gh_s, gh_r, gh_l = (pool.take() for _ in range(3))
    gh_copy = remote(dat_ref.at[t], gh_all.at[t], gh_s(), gh_r(), {"tensor": 1 - t})
    gh_own = pltpu.make_async_copy(dat_ref.at[t], gh_all.at[t], gh_l())
    gh_copy.start()
    gh_own.start()
    line_tick(4)
    v_add(0)
    v_side(1).start()
    far_s, far_r = pool.take(), pool.take()
    far_copy = remote(
        g_mlp.at[:, 1 - x],
        g_far.at[pl.ds(0, g_mlp.shape[0])],
        far_s(),
        far_r(),
        {"x": 1 - x},
    )
    far_copy.start()
    y_sum = sq_y.result()
    sq_y.drain()
    total = mid_ref[...] + y_sum
    cut = width // 2
    o_s, o_r, o_l = pool.take(2), pool.take(2), pool.take(2)
    sends, locals_ = [], []
    for i in range(2):
        y_own[i] = total[:, i * cut : (i + 1) * cut].astype(BF)
        dst = out_all.at[t, :, pl.ds(i * cut, cut)]
        sends.append(remote(y_own.at[i], dst, o_s(i), o_r(i), {"tensor": 1 - t}))
        locals_.append(pltpu.make_async_copy(y_own.at[i], dst, o_l(i)))
    for copy in sends + locals_:
        copy.start()
    v_add(1)
    v_side(2).start()
    col_q.after_side()
    line_tick(5)
    for k in runs[0]:
        col_wo.step(k)
    for tick in range(6, nl + 3):
        line_tick(tick)
    if nl:
        lf_s, lf_r, lf_l = (pool.take() for _ in range(3))
        rows = g_far.shape[1]

        def left_rows(col):
            return left_acc.at[:, z, pl.ds(pl.multiple_of(col * rows, rows), rows)]

        left_far = remote(
            left_rows(1 - x),
            g_far.at[pl.ds(g_mlp.shape[0], nl)],
            lf_s(),
            lf_r(),
            {"x": 1 - x},
        )
        left_own = pltpu.make_async_copy(left_rows(x), left_out, lf_l())
        left_far.start()
        left_own.start()
    for k in runs[0]:
        col_q.step(k)
    for k in runs[1]:
        col_wo.step(k)
    col_kv.after_side()
    for k in runs[0]:
        col_kv.step(k)
    v_add(2)

    def v_copy(to):
        return remote(vec_own, vec_z.at[z], vz_s(to), vz_r(z), {"z": to})

    for to in range(zs):

        @pl.when(to != z)
        def _():
            v_copy(to).start()

    for k in runs[1]:
        col_q.step(k)
    for k in runs[1]:
        col_kv.step(k)
    for item in (col_wo, col_q, col_kv):
        for k in runs[2]:
            item.step(k)
    total = jnp.zeros(vec_ref.shape, F32)
    for frm in range(zs):

        @pl.when(frm != z)
        def _():
            remote(vec_own, vec_z.at[frm], vz_s(frm), vz_r(frm), {"z": frm}).wait_recv()

        @pl.when(frm == z)
        def _():
            vec_z[frm] = vec_own[...]

        total = total + vec_z[frm]
    g_vec[...] = total

    for to in range(zs):

        @pl.when(to != z)
        def _():
            v_copy(to).wait_send()

    def dkv_drain(s, carry):
        @pl.when((s < z) | ((s == z) & (x == 1)))
        def _():
            side(s, 0).wait_send()

        @pl.when((s > z) | ((s == z) & (x == 0)))
        def _():
            side(s, 1).wait_send()

        @pl.when(s < z)
        def _():
            chain(s, 0).wait_send()

        @pl.when(s > z)
        def _():
            chain(s, 1).wait_send()

        return carry

    lax.fori_loop(0, zs, dkv_drain, 0)
    for item in (col_wo, col_q, col_kv):
        item.drain()
    dh_copy.wait_send()
    far_copy.wait()
    gh_own.wait()
    gh_copy.wait()
    for copy in sends + locals_:
        copy.wait()
    if nl:
        for item in lines:
            item.drain()
        left_far.wait()
        left_own.wait()


def backward_call(zs, heads, left, big, late, small):
    mid, vec = small[1:3]
    wq = late[5]
    half, width = mid.shape
    tok = 2 * half
    _, rows, q_cols = wq.shape
    qkv_cols = q_cols + 2 * HEAD_SIZE
    n2, _, _, three = big[1].shape
    nl = left[0].shape[0] if left else 0
    shape = jax.ShapeDtypeStruct
    any_spec = pl.BlockSpec(memory_space=pl.ANY)
    vm = pltpu.VMEM
    cut = width // 2

    def collect(cols):
        return [
            vm((2, zs, rows, cols), BF),
            vm((2, zs, rows, cols), BF),
            vm((2, zs, rows, cols), BF),
            vm((zs, rows, cols), BF),
            vm((zs + 1, rows, cols), BF),
        ]

    square = [vm((4, half, cut), BF), vm((4, half, cut), BF), vm((2, half, cut), BF)]
    lines = [vm(left[0].shape, BF), vm((nl, zs + 1) + left[0].shape[2:], BF)] if nl else []
    return pl.pallas_call(
        functools.partial(backward_kernel, zs, heads, nl, HEAD_SIZE ** (-0.5)),
        out_shape=[
            shape((2, half, width), BF),
            shape((2, half, width), BF),
            shape((rows, q_cols), BF),
            shape((rows, 2 * HEAD_SIZE), BF),
            shape((rows, q_cols), BF),
            shape(vec.shape, F32),
            shape((n2 + nl, rows, three), BF),
        ]
        + ([shape((nl, rows, three), BF)] if nl else []),
        in_specs=[any_spec] * (4 + len(left) + len(late)) + [VMEM] * len(small),
        out_specs=[any_spec] * 5 + [VMEM, any_spec] + [any_spec] * len(left),
        scratch_shapes=square
        + [
            vm((half, width), F32),
            vm((2, half, width), BF),
            vm((width, tok), BF),
            vm((2, heads * half, HEAD_SIZE), BF),
            vm((2, heads * half, HEAD_SIZE), BF),
            vm((2, HEAD_SIZE, heads * half), BF),
            vm((2, HEAD_SIZE, heads * half), BF),
            vm((2, 1, heads * half), F32),
            vm((2 * zs + 1, half, 2 * HEAD_SIZE), BF),
            vm((zs + 1, half, 2 * HEAD_SIZE), BF),
            vm((zs + 1, half, 2 * HEAD_SIZE), BF),
            vm((2, HEAD_SIZE, heads * half), F32),
            vm((tok, qkv_cols), BF),
            vm((half, width), BF),
            vm((half, width), BF),
        ]
        + collect(q_cols)
        + collect(2 * HEAD_SIZE)
        + collect(q_cols)
        + [
            vm(vec.shape, F32),
            vm((3,) + vec.shape, F32),
            vm((zs,) + vec.shape, F32),
            vm((half, width), BF),
            vm((half, width), BF),
            pltpu.SemaphoreType.DMA(((22 + 4 * nl) * zs + 97,)),
        ]
        + [vm(v.shape, BF) for v in late]
        + lines,
        compiler_params=pltpu.CompilerParams(
            collective_id=2, has_side_effects=True, vmem_limit_bytes=63 * 2**20
        ),
        cost_estimate=pl.CostEstimate(
            flops=4 * tok * width * (qkv_cols + q_cols) + 2**32,
            bytes_accessed=32 * 2**20,
            transcendentals=0,
        ),
    )(*big, *left, *late, *small)


def remote(src, dst, send, recv, to):
    return pltpu.make_async_remote_copy(
        src_ref=src,
        dst_ref=dst,
        send_sem=send,
        recv_sem=recv,
        device_id=to,
        device_id_type=pl.DeviceIdType.MESH,
    )


def greet(z, zs):
    barrier = pltpu.get_barrier_semaphore()
    for axis in ("batch", "x", "tensor"):
        other = {axis: 1 - lax.axis_index(axis)}
        pl.semaphore_signal(barrier, inc=1, device_id=other, device_id_type=pl.DeviceIdType.MESH)

    @pl.when(z > 0)
    def _():
        pl.semaphore_signal(
            barrier, inc=1, device_id={"z": z - 1}, device_id_type=pl.DeviceIdType.MESH
        )

    @pl.when(z < zs - 1)
    def _():
        pl.semaphore_signal(
            barrier, inc=1, device_id={"z": z + 1}, device_id_type=pl.DeviceIdType.MESH
        )

    pl.semaphore_wait(barrier, 5 - (z == 0).astype(jnp.int32) - (z == zs - 1).astype(jnp.int32))


def in_range(c, count):
    return (c >= 0) & (c < count)


class Exchange:
    def __init__(self, mats, full, first, zs, skip, sems):
        self.mats, self.full, self.first = mats, full, first
        self.x = lax.axis_index("x")
        home = (lax.axis_index("batch") * zs + lax.axis_index("z")) * 2 + self.x
        self.rows, self.cols = mats[0].shape[0], full.shape[2] // 3
        self.at = pl.ds(pl.multiple_of(home * self.rows, self.rows), self.rows)
        self.shift = mats[0].shape[1] // 2 - skip // 2
        self.send, self.recv, self.loc = sems

    def pieces(self, c):
        for w, mat in enumerate(self.mats):
            dst = self.full.at[c, self.at, pl.ds(w * self.cols, self.cols)]
            yield mat, dst

    def source(self, mat, c, x):
        first = pl.multiple_of(x * self.shift + (self.first + c) * self.cols, 128)
        return mat.at[:, pl.ds(first, self.cols)]

    def ship(self, c, i):
        for mat, dst in self.pieces(c):
            src = self.source(mat, c, 1 - self.x)
            remote(src, dst, self.send(i), self.recv(i), {"x": 1 - self.x}).start()

    def keep(self, c, i):
        for mat, dst in self.pieces(c):
            pltpu.make_async_copy(self.source(mat, c, self.x), dst, self.loc(i)).start()

    def fetch(self, c, other, buf, sem):
        x = 1 - self.x if other else self.x
        for w, mat in enumerate(self.mats):
            dst = buf.at[pl.ds(c * self.rows, self.rows), pl.ds(w * self.cols, self.cols)]
            pltpu.make_async_copy(self.source(mat, c, x), dst, sem).start()

    def both(self, c, i):
        spot = self.full.at[c, self.at]
        return remote(spot, spot, self.send(i), self.recv(i), {"x": 1 - self.x})

    def arrived(self, c, i):
        self.both(c, i).wait_recv()
        spot = self.full.at[c, self.at]
        pltpu.make_async_copy(spot, spot, self.loc(i)).wait()

    def sent(self, c, i):
        self.both(c, i).wait_send()


class Gather:
    def __init__(self, zs, mine, full, sems):
        self.zs, self.mine, self.full = zs, mine, full
        self.loc, self.up, self.dn, self.zr, self.ss, self.sr = sems
        self.b, self.z = lax.axis_index("batch"), lax.axis_index("z")
        self.size = full.shape[1] // (2 * zs)

    def at(self, c, b, z):
        rows = pl.ds(pl.multiple_of((b * self.zs + z) * self.size, self.size), self.size)
        return self.full.at[:, rows] if c is None else self.full.at[c, rows]

    def sems(self, c, s):
        i = 0 if c is None else c
        return (ref.at[i, s] for ref in (self.up, self.dn, self.zr, self.ss, self.sr))

    def up_copy(self, c, s, src=None):
        dst = self.at(c, self.b, s)
        up, _, zr, _, _ = self.sems(c, s)
        return remote(dst if src is None else src, dst, up, zr, {"z": self.z + 1})

    def dn_copy(self, c, s, src=None):
        dst = self.at(c, self.b, s)
        _, dn, zr, _, _ = self.sems(c, s)
        return remote(dst if src is None else src, dst, dn, zr, {"z": self.z - 1})

    def sib_copy(self, c, s, src=None):
        dst = self.at(c, self.b, s)
        _, _, _, ss, sr = self.sems(c, s)
        return remote(dst if src is None else src, dst, ss, sr, {"batch": 1 - self.b})

    def local(self, c):
        return pltpu.make_async_copy(self.mine.at[c], self.at(c, self.b, self.z), self.loc.at[c])

    def start(self, c):
        src = None if self.mine is None else self.mine.at[c]

        @pl.when(self.z < self.zs - 1)
        def _():
            self.up_copy(c, self.z, src).start()

        @pl.when(self.z > 0)
        def _():
            self.dn_copy(c, self.z, src).start()

        self.sib_copy(c, self.z, src).start()
        if self.mine is not None:
            self.local(c).start()

    def hop(self, c, k):
        low, high = self.z - k, self.z + k

        @pl.when(low >= 0)
        def _():
            self.dn_copy(c, low).wait_recv()

            @pl.when(self.z < self.zs - 1)
            def _():
                self.up_copy(c, low).start()

            self.sib_copy(c, low).start()

        @pl.when(high < self.zs)
        def _():
            self.dn_copy(c, high).wait_recv()

            @pl.when(self.z > 0)
            def _():
                self.dn_copy(c, high).start()

            self.sib_copy(c, high).start()

    def finish(self, c):
        if self.mine is not None:
            self.local(c).wait()
        for s in range(self.zs):
            dst = self.at(c, 1 - self.b, s)
            _, _, _, ss, sr = self.sems(c, s)
            remote(dst, dst, ss, sr, {"batch": 1 - self.b}).wait_recv()

    def drain(self, c):
        for s in range(self.zs):

            @pl.when((s <= self.z) & (self.z < self.zs - 1))
            def _():
                self.up_copy(c, s).wait_send()

            @pl.when((s >= self.z) & (self.z > 0))
            def _():
                self.dn_copy(c, s).wait_send()

            self.sib_copy(c, s).wait_send()


class Reduce:
    def __init__(self, zs, ends, ring, to_sib, r_sib, r_dn, r_up, tmp, out, left, sems):
        self.zs, self.ring, self.to_sib, self.out = zs, ring, to_sib, out
        self.ends, self.left = ends, left
        self.r_sib, self.r_dn, self.r_up = r_sib, r_dn, r_up
        self.tmp_s, self.tmp_d, self.tmp_u = tmp
        self.s_s, self.s_r, self.d_s, self.d_r, self.u_s, self.u_r, self.load, self.o_s, self.l_s = sems
        self.b, self.z = lax.axis_index("batch"), lax.axis_index("z")
        self.slots = ring.shape[0]
        self.size = ring.shape[1] // zs

    def rows(self, h):
        return pl.ds(pl.multiple_of(h * self.size, self.size), self.size)

    def sib(self, c):
        return remote(
            self.to_sib, self.r_sib.at[c], self.s_s.at[c], self.s_r.at[c], {"batch": 1 - self.b}
        )

    def dn(self, c, h):
        src = self.ring.at[lax.rem(c, self.slots), self.rows(h)]
        dst = self.r_dn.at[c, self.rows(h)]
        return remote(src, dst, self.d_s.at[c, h], self.d_r.at[c, h], {"z": self.z - 1})

    def up(self, c, h):
        src = self.ring.at[lax.rem(c, self.slots), self.rows(h)]
        dst = self.r_up.at[c, self.rows(h)]
        return remote(src, dst, self.u_s.at[c, h], self.u_r.at[c, h], {"z": self.z + 1})

    def load_sib(self, c):
        return pltpu.make_async_copy(self.r_sib.at[c], self.tmp_s, self.load.at[0])

    def load_dn(self, c, h):
        rows = self.rows(h)
        return pltpu.make_async_copy(self.r_dn.at[c, rows], self.tmp_d.at[rows], self.load.at[1 + h])

    def load_up(self, c, h):
        rows = self.rows(h)
        return pltpu.make_async_copy(
            self.r_up.at[c, rows], self.tmp_u.at[rows], self.load.at[1 + self.zs + h]
        )

    def arrive(self, c_sib, c_dn, c_up, count):
        @pl.when(in_range(c_sib, count))
        def _():
            self.sib(c_sib).wait_recv()
            self.load_sib(c_sib).start()

        for h in range(self.zs):

            @pl.when(in_range(c_dn, self.ends) & (self.z < self.zs - 1) & (h <= self.z))
            def _():
                self.dn(c_dn, h).wait_recv()
                self.load_dn(c_dn, h).start()

            @pl.when(in_range(c_up, self.ends) & (self.z > 0) & (h >= self.z))
            def _():
                self.up(c_up, h).wait_recv()
                self.load_up(c_up, h).start()

    def add(self, slot, rows, tmp):
        self.ring[slot, rows] = self.ring[slot, rows] + tmp[rows]

    def pass_on(self, c_sib, c_dn, c_up, count):
        @pl.when(in_range(c_sib, count))
        def _():
            self.load_sib(c_sib).wait()
            slot = lax.rem(c_sib, self.slots)
            for h in range(self.zs):
                self.add(slot, pl.ds(h * self.size, self.size), self.tmp_s)
            for h in range(self.zs - 1):

                @pl.when((self.z == self.zs - 1) & (c_sib < self.ends))
                def _():
                    self.dn(c_sib, h).start()

            for h in range(1, self.zs):

                @pl.when((self.z == 0) & (c_sib < self.ends))
                def _():
                    self.up(c_sib, h).start()

            if self.left is not None:

                @pl.when(c_sib >= self.ends)
                def _():
                    self.leave(c_sib).start()

        for h in range(self.zs):

            @pl.when(in_range(c_dn, self.ends) & (self.z < self.zs - 1) & (h <= self.z))
            def _():
                self.load_dn(c_dn, h).wait()
                self.add(lax.rem(c_dn, self.slots), pl.ds(h * self.size, self.size), self.tmp_d)

                @pl.when(h < self.z)
                def _():
                    self.dn(c_dn, h).start()

            @pl.when(in_range(c_up, self.ends) & (self.z > 0) & (h >= self.z))
            def _():
                self.load_up(c_up, h).wait()
                self.add(lax.rem(c_up, self.slots), pl.ds(h * self.size, self.size), self.tmp_u)

                @pl.when(h > self.z)
                def _():
                    self.up(c_up, h).start()

    def leave(self, c):
        src = self.ring.at[lax.rem(c, self.slots)]
        return pltpu.make_async_copy(src, self.left.at[c - self.ends], self.l_s.at[c - self.ends])

    def result(self, c):
        src = self.ring.at[lax.rem(c, self.slots), self.rows(self.z)]
        return pltpu.make_async_copy(src, self.out.at[c], self.o_s.at[0])

    def finish(self, c):
        for h in range(self.zs):

            @pl.when(h < self.z)
            def _():
                self.dn(c, h).wait_send()

            @pl.when(h > self.z)
            def _():
                self.up(c, h).wait_send()

        self.result(c).start()


def mlp_kernel(zs, nc, n1, n2, fc, skip, *refs):
    refs = list(refs)

    def take(count):
        out = refs[:count]
        del refs[:count]
        return out

    if n1:
        mats, full_one = take(3), take(1)[0]
        mine = None
    else:
        (mine,) = take(1)
    h2, dy, dh2_out, y_out, g_out, full, r_sib, r_dn, r_up = take(9)
    left = take(1)[0] if n2 < nc else None
    acc_y, acc_d, h2t, dyt, wbuf, hid_s, dgu_s, ring, to_sib, tmp_s, tmp_d, tmp_u = take(12)
    d_src, d_own, d_one, d_two = take(4)
    w_sem, x_s, x_r, k_s, sq_sem, st_sem = take(6)
    sems = refs
    b, z, x = lax.axis_index("batch"), lax.axis_index("z"), lax.axis_index("x")
    greet(z, zs)
    rest = nc - n1
    lag = 0 if n1 else zs + 1
    ahead = n1 - zs + 1 if n1 else 0
    gather = Gather(zs, mine, full, sems[:6])
    reduce = Reduce(
        zs, n2, ring, to_sib, r_sib, r_dn, r_up, (tmp_s, tmp_d, tmp_u), g_out, left, sems[6:]
    )
    slots = ring.shape[0]
    half = ring.shape[1]
    toks = h2.shape[0]
    part = toks // 4
    square = Square(d_src, d_own, d_one, d_two, Pool(sq_sem))

    if n1:
        trade = Exchange(
            mats, full, n1, zs, skip, [lambda i, r=r: r.at[i] for r in (x_s, x_r, k_s)]
        )
        stage = [ring.at[ring.shape[0] - 1], ring.at[ring.shape[0] - 2]]
        for c in range(rest):
            for side in range(2):
                trade.fetch(c, side, stage[side], st_sem.at[2 * c + side])

        def slices(c):
            rows = pl.ds(c * trade.rows, trade.rows)
            dst = full.at[c, trade.at]
            return (
                pltpu.make_async_copy(stage[0].at[rows], dst, k_s.at[c]),
                remote(stage[1].at[rows], dst, x_s.at[c], x_r.at[c], {"x": 1 - x}),
            )

        for c in range(rest):
            for side in range(2):
                rows = stage[side].at[pl.ds(c * trade.rows, trade.rows)]
                pltpu.make_async_copy(rows, rows, st_sem.at[2 * c + side]).wait()
                slices(c)[side].start()

    def weights(c):
        return pltpu.make_async_copy(full.at[c - n1], wbuf, w_sem.at[0])

    def weights_one(c):
        return pltpu.make_async_copy(full_one.at[c], wbuf, w_sem.at[0])

    if n1:
        weights_one(0).start()
    acc_y[...] = jnp.zeros_like(acc_y)
    acc_d[...] = jnp.zeros_like(acc_d)
    for m in range(4):
        at = slice(m * part, (m + 1) * part)
        h2t[:, at] = h2[at].T
        dyt[:, at] = dy[at].T

    nl = nc - n2

    def keep_slot(c):
        return jnp.maximum(c - n2, 0) if nl else 0

    def compute(c):
        k = keep_slot(c)
        col = lax.broadcasted_iota(jnp.int32, (1, fc), 1) + c * fc
        live = jnp.where((col >= skip) | (x == 0), 1.0, 0.0).astype(F32)
        gate_up = dot(h2[...], wbuf[:, : 2 * fc])
        d_hidden = dot(dy[...], wbuf[:, 2 * fc :]) * live
        gate, up = gate_up[:, :fc], gate_up[:, fc:]
        sig = 1.0 / (1.0 + jnp.exp(-gate))
        silu = gate * sig
        hid_s[k] = (silu * up * live).astype(BF)
        dgu_s[k, :, :fc] = (d_hidden * up * sig * (1.0 + gate * (1.0 - sig))).astype(BF)
        dgu_s[k, :, fc:] = (d_hidden * silu).astype(BF)
        acc_y[...] += dot_nt(hid_s[k], wbuf[:, 2 * fc :])
        acc_d[...] += dot_nt(dgu_s[k], wbuf[:, : 2 * fc])

        @pl.when(c == nc - 1)
        def _():
            for i in range(4):
                d_src[i] = acc_d[i * part : (i + 1) * part].astype(BF)
            square.start()

    def products(c):
        k = keep_slot(c)

        @pl.when(c > 0)
        def _():
            reduce.sib(c - 1).wait_send()

        theirs = pl.ds(pl.multiple_of((1 - b) * half, half), half)
        own = pl.ds(pl.multiple_of(b * half, half), half)
        to_sib[:, : 2 * fc] = dot(h2t[theirs], dgu_s[k]).astype(BF)
        to_sib[:, 2 * fc :] = dot(dyt[theirs], hid_s[k]).astype(BF)
        reduce.sib(c).start()
        slot = lax.rem(c, slots)
        ring[slot, :, : 2 * fc] = dot(h2t[own], dgu_s[k]).astype(BF)
        ring[slot, :, 2 * fc :] = dot(dyt[own], hid_s[k]).astype(BF)

    def begin(i):
        @pl.when(in_range(i, rest))
        def _():
            if n1:
                trade.arrived(i, i)
            gather.start(i)

    def tick(t, carry):
        if n1:
            @pl.when(t == slots - 3)
            def _():
                for c in range(rest):
                    trade.sent(c, c)

        c = t - lag

        @pl.when(in_range(c, nc))
        def _():
            weights(n1).wait()
            compute(c)

        g = t + ahead
        begin(g)
        for k in range(1, zs):

            @pl.when(in_range(g - k, rest))
            def _():
                gather.hop(g - k, k)

        @pl.when(in_range(g - zs, rest))
        def _():
            gather.finish(g - zs)
            weights(g - zs + n1).start()

        if n1:

            @pl.when(c + 1 < n1)
            def _():
                weights_one(c + 1).start()

        c_dn = c - 1 - 3 * (zs - 1 - z)
        c_up = c - 1 - 3 * z
        c_end = c - 3 * zs + 1

        def product_at(step):
            late = step - nl
            return jnp.where(
                in_range(step, n2), step, jnp.where((step >= nc) & (late < nc), late, -1)
            )

        c_sib = product_at(c - 1)
        reduce.arrive(c_sib, c_dn, c_up, nc)
        reduce.pass_on(c_sib, c_dn, c_up, nc)

        @pl.when(in_range(c_end, n2))
        def _():
            reduce.finish(c_end)
            reduce.result(c_end).wait()

        c_prod = product_at(c)

        @pl.when(c_prod >= 0)
        def _():
            products(c_prod)

        return carry

    for i in range(ahead):
        begin(i)
    lax.fori_loop(0, nc + lag, tick, 0)

    end = max(nc + nl + 1, n2 + 3 * zs - 1) + lag
    turn = min(nc + lag + 3, end)
    lax.fori_loop(nc + lag, turn, tick, 0)
    square.turn()
    for copy in square.first():
        copy.wait_send()
    for i in range(4):
        d_src[i] = acc_y[i * part : (i + 1) * part].astype(BF)
    y_copy = pltpu.make_async_copy(d_src, y_out, w_sem.at[0])
    y_copy.start()
    lax.fori_loop(turn, end, tick, 0)
    dh2_out[...] = square.result()
    for copy in square.second():
        copy.wait_send()
    y_copy.wait()
    reduce.sib(nc - 1).wait_send()
    for c in range(n2, nc):
        reduce.leave(c).wait()

    def drain(c, carry):
        gather.drain(c)
        return carry

    lax.fori_loop(0, rest, drain, 0)


def mlp_call(zs, nc, n1, n2, fc, skip, weights, h2, dy):
    toks, width = h2.shape
    half = width // 2
    slots = min(2 * zs, nc)
    rest = nc - n1
    dma = pltpu.SemaphoreType.DMA
    vm = pltpu.VMEM
    shape = jax.ShapeDtypeStruct
    any_spec = pl.BlockSpec(memory_space=pl.ANY)
    out = [
        shape((toks // 4, width), F32),
        shape((4, toks // 4, width), BF),
        shape((n2, half // zs, 3 * fc), BF),
        shape((rest, width, 3 * fc), BF),
        shape((nc, half, 3 * fc), BF),
        shape((n2, half, 3 * fc), BF),
        shape((n2, half, 3 * fc), BF),
    ]
    if n2 < nc:
        out.append(shape((nc - n2, half, 3 * fc), BF))
    result = pl.pallas_call(
        functools.partial(mlp_kernel, zs, nc, n1, n2, fc, skip),
        out_shape=out,
        in_specs=[any_spec] * len(weights) + [VMEM, VMEM],
        out_specs=[VMEM] + [any_spec] * (len(out) - 1),
        scratch_shapes=[
            vm((toks, width), F32),
            vm((toks, width), F32),
            vm((width, toks), BF),
            vm((width, toks), BF),
            vm((width, 3 * fc), BF),
            vm((max(nc - n2, 1), toks, fc), BF),
            vm((max(nc - n2, 1), toks, 2 * fc), BF),
            vm((slots, half, 3 * fc), BF),
            vm((half, 3 * fc), BF),
            vm((half, 3 * fc), BF),
            vm((half, 3 * fc), BF),
            vm((half, 3 * fc), BF),
            vm((4, toks // 4, width), BF),
            vm((4, toks // 4, half), BF),
            vm((4, toks // 4, half), BF),
            vm((2, toks // 4, half), BF),
            dma((1,)),
        ]
        + [dma((rest,))] * 3
        + [dma((13,)), dma((2 * rest,)), dma((rest,))]
        + [dma((rest, zs))] * 5
        + [dma((nc,))] * 2
        + [dma((nc, zs))] * 4
        + [dma((1 + 2 * zs,)), dma((1,)), dma((nc,))],
        compiler_params=pltpu.CompilerParams(
            collective_id=0, has_side_effects=True, vmem_limit_bytes=62 * 2**20
        ),
        cost_estimate=pl.CostEstimate(
            flops=18 * toks * width * fc * nc, bytes_accessed=80 * 2**20, transcendentals=0
        ),
    )(*weights, h2, dy)
    return list(result[:3]) + list(result[7:])


def final_kernel(skip, *refs):
    refs = list(refs)
    inputs = refs[:8]
    d_hidden, g_query, g_key, g_value, g_out, g_gate, g_up, g_down, output = refs[8:17]
    bufs, sem = refs[17:24] + [output], refs[24]
    x = lax.axis_index("x")
    copies = [
        pltpu.make_async_copy(src, dst, sem.at[i])
        for i, (src, dst) in enumerate(zip(inputs, bufs))
    ]
    for copy in copies:
        copy.start()
    near, left, far, gh, s_q, s_kv, s_wo, _ = bufs
    n2, nl = near.shape[0], left.shape[0]
    half = gh.shape[1]
    fc = far.shape[2] // 3
    split = (n2 + nl) * fc
    for i in (0, 2, 1):
        copies[i].wait()
    for c in range(n2 + nl):
        own = (near[c, x] if c < n2 else left[c - n2]).astype(F32)
        other = far[c].astype(F32)
        low = jnp.where(x == 0, own, other)
        high = jnp.where(x == 0, other, own)
        for w, out in enumerate((g_gate, g_up, g_down)):
            b = high[:, w * fc : (w + 1) * fc]
            first = split - skip + c * fc
            if c == 0:
                b = b[:, skip:]
                first = split
            out[:, c * fc : (c + 1) * fc] = low[:, w * fc : (w + 1) * fc]
            out[:, first : first + b.shape[1]] = b
    for i in (3, 4, 5, 6):
        copies[i].wait()
    for i in range(2):
        d_hidden[i * half : (i + 1) * half] = gh[i].astype(F32)
    g_query[...] = s_q[...].astype(F32)
    g_key[...] = s_kv[:, :HEAD_SIZE].astype(F32)
    g_value[...] = s_kv[:, HEAD_SIZE:].astype(F32)
    g_out[...] = s_wo[...].astype(F32)
    copies[7].wait()


def final_call(skip, ff, inputs):
    rows, three = inputs[2].shape[1:]
    _, half, width = inputs[3].shape
    q_cols = inputs[4].shape[1]
    shape = jax.ShapeDtypeStruct
    any_spec = pl.BlockSpec(memory_space=pl.ANY)
    out = [
        shape((2 * half, width), F32),
        shape((rows, q_cols), F32),
        shape((rows, HEAD_SIZE), F32),
        shape((rows, HEAD_SIZE), F32),
        shape((rows, q_cols), F32),
        shape((rows, ff), F32),
        shape((rows, ff), F32),
        shape((rows, ff), F32),
        shape(inputs[7].shape, BF),
    ]
    return pl.pallas_call(
        functools.partial(final_kernel, skip),
        out_shape=out,
        in_specs=[any_spec] * len(inputs),
        out_specs=[VMEM] * 9,
        scratch_shapes=[pltpu.VMEM(v.shape, BF) for v in inputs[:7]]
        + [pltpu.SemaphoreType.DMA((8,))],
        compiler_params=pltpu.CompilerParams(vmem_limit_bytes=60 * 2**20),
    )(*inputs)


def on_device(
    hidden,
    lengths,
    norm_attn,
    w_query,
    key_weight_matrix,
    value_weight_matrix,
    b_query,
    key_bias_rows,
    value_bias_rows,
    w_out,
    norm_mlp,
    w_gate,
    w_up,
    w_down,
    cotangent,
):
    homes = lax.axis_size("batch") * lax.axis_size("z") * lax.axis_size("x")
    shards = lax.axis_size("z") * lax.axis_size("x")
    z_i, x_i = lax.axis_index("z"), lax.axis_index("x")
    me = z_i * lax.axis_size("x") + x_i
    tok = hidden.shape[1]
    width = hidden.shape[2]
    half = tok // 2
    doc_lengths = lengths[0]
    heads = b_query.shape[0]
    heads_all = heads + 2
    q_cols = heads * HEAD_SIZE
    rows = norm_attn.shape[0]
    ff = w_gate.shape[1]
    ffh = -(-ff // 512) * 256
    fc = FC
    nc = ffh // fc

    home = (lax.axis_index("batch") * lax.axis_size("z") + z_i) * 2 + x_i
    per_home = HEAD_SIZE // homes

    def spot(value):
        here = jnp.arange(homes, dtype=jnp.int32)[None, :, None] == home
        return jnp.where(here, value[:, None, :], 0).reshape(-1)

    biases = jnp.concatenate([b_query, key_bias_rows, value_bias_rows], axis=0)
    small = jnp.concatenate(
        [spot(biases), spot(norm_attn[None]), spot(norm_mlp[None])]
    ).reshape(16, -1)

    zs = lax.axis_size("z")
    n1, n2 = (zs, nc - zs) if rows % 16 == 0 and 2 * zs < nc else (0, nc)
    three = (w_gate, w_up, w_down.T)
    skip = 2 * ffh - ff

    stored = me * tok + jnp.arange(tok, dtype=jnp.int32)
    q_rows = row_positions(stored, shards, half)
    doc_start = doc_starts_of(q_rows, doc_lengths)
    cosine_table, sine_table = rotary(q_rows - doc_start, HEAD_SIZE)
    cos2 = jnp.concatenate([cosine_table, cosine_table], axis=1)
    sin2 = jnp.concatenate([-sine_table, sine_table], axis=1)
    start_row = doc_start[None, :]

    x_in = hidden[0]
    (
        h_first,
        q_mat,
        out_low,
        lse,
        mid,
        vec,
        wkv,
        wq,
        wo_t,
        kv_all,
        h2,
        dy,
        *full_one,
    ) = forward_call(
        zs,
        heads,
        n1,
        skip,
        fc,
        x_in,
        jnp.concatenate([key_weight_matrix, value_weight_matrix], axis=1),
        w_query,
        w_out.T,
        small,
        cos2,
        sin2,
        start_row,
        cotangent[0].reshape(2, half, width),
        three if n1 else (),
    )
    h2 = h2.reshape(4 * half, width)
    dy = dy.reshape(4 * half, width)
    if n1:
        mlp_w = (*three, *full_one)
    else:

        def stacked(x_at):
            halves = [
                lax.dynamic_slice_in_dim(mat, x_at * (ff - ffh), ffh, axis=1).reshape(rows, nc, fc)
                for mat in three
            ]
            return jnp.transpose(jnp.concatenate(halves, axis=2), (1, 0, 2))

        keep = stacked(x_i)
        other = lax.ppermute(stacked(1 - x_i), "x", [(0, 1), (1, 0)])
        low = jnp.where(x_i == 0, keep, other)
        high = jnp.where(x_i == 0, other, keep)
        mlp_w = (jnp.concatenate([low, high], axis=1),)
    dh2, y_sum, mlp_g, *left = mlp_call(zs, nc, n1, n2, fc, skip, mlp_w, h2, dy)
    mlp_g = mlp_g.reshape(n2, 2, rows, 3 * fc)
    left = [v.reshape(nc - n2, zs, 2 * rows, 3 * fc) for v in left]

    output, d_hidden, s_q, s_kv, s_wo, g_vec, other, *left_own = backward_call(
        zs,
        heads,
        left,
        (y_sum, mlp_g, x_in, cotangent[0]),
        (h_first, q_mat, out_low, kv_all, wkv, wq, wo_t),
        (dh2, mid, vec, lse[:, None], cos2, sin2, start_row.reshape(2, 1, half)),
    )
    g_vec = g_vec.reshape(-1)
    g_bias = lax.dynamic_slice_in_dim(
        g_vec[: heads_all * HEAD_SIZE].reshape(heads_all, HEAD_SIZE), home * per_home, per_home, 1
    )
    g_norms = g_vec[heads_all * HEAD_SIZE :].reshape(2, width)
    g_norms = lax.dynamic_slice_in_dim(g_norms, home * rows, rows, 1)

    if n1:
        grads = final_call(skip, ff, (mlp_g, *left_own, other, d_hidden, s_q, s_kv, s_wo, output))
    else:
        keep = lax.dynamic_index_in_dim(mlp_g, x_i, 1, False)
        low = jnp.where(x_i == 0, keep, other)
        high = jnp.where(x_i == 0, other, keep)

        def whole(k):
            def cols(value):
                piece = value[:, :, k * fc : (k + 1) * fc]
                return jnp.transpose(piece, (1, 0, 2)).reshape(rows, ffh)

            return jnp.concatenate([cols(low), cols(high)[:, skip:]], axis=1).astype(F32)

        grads = (
            d_hidden.astype(F32).reshape(tok, width),
            s_q.astype(F32),
            s_kv[:, :HEAD_SIZE].astype(F32),
            s_kv[:, HEAD_SIZE:].astype(F32),
            s_wo.astype(F32),
            whole(0),
            whole(1),
            whole(2),
            output,
        )
    d_hidden, g_query, g_key, g_value, g_out, g_gate, g_up, g_down, output = grads
    return (
        output.reshape(1, tok, width),
        d_hidden[None],
        g_norms[0],
        g_query,
        g_key,
        g_value,
        g_bias[:heads],
        g_bias[heads : heads + 1],
        g_bias[heads + 1 :],
        g_out.T,
        g_norms[1],
        g_gate,
        g_up,
        g_down.T,
    )


def solution(mesh):
    seq = mesh.shape["seq"]
    fine = Mesh(
        mesh.devices.reshape(mesh.shape["batch"], seq // 2, 2, mesh.shape["tensor"]),
        ("batch", "z", "x", "tensor"),
    )
    toks = P("batch", ("z", "x"), None)
    home = ("batch", "z", "x")
    down = P(home, "tensor")
    across = P("tensor", home)
    return jax.shard_map(
        on_device,
        mesh=fine,
        in_specs=(
            toks,
            P("batch", None),
            P(home),
            down,
            down,
            down,
            across,
            across,
            across,
            across,
            P(home),
            down,
            down,
            across,
            toks,
        ),
        out_specs=(
            toks,
            toks,
            P(home),
            down,
            down,
            down,
            across,
            across,
            across,
            across,
            P(home),
            down,
            down,
            across,
        ),
        check_vma=False,
    )
```
